256 devices in a mesh: ctx: 64 (over z, x, core), tp: 4 (over y).
Axes of the slice: x: 4, y: 4, z: 8, core: 2. Of those that a mesh axis runs over, the one named last changes fastest.
Arguments:
- query_one: bfloat16 [12288, 4096], P('ctx', 'tp'), may hold values from -64 to 64
- key_one: bfloat16 [12288, 1024], P('ctx', 'tp'), may hold values from -6 to 6
- value_one: bfloat16 [12288, 1024], P('ctx', 'tp'), may hold values from -6 to 6
- segments: int32 [12288], P('ctx'), may hold values from 0 to 3, never falling along the last dimension, each value on 1 to 6144 neighbouring positions
- query_base: bfloat16 [12288, 4096], P('ctx', 'tp'), may hold values from -20 to 20
- key_two: bfloat16 [12288, 1024], P('ctx', 'tp'), may hold values from -3 to 3
- value_two: bfloat16 [12288, 1024], P('ctx', 'tp'), may hold values from -64 to 64
Outputs:
- attended: bfloat16 [12288, 4096], P('ctx', 'tp')
The draws below stay inside these ranges and needn't reach their ends.
Inputs may be any that keep to these rules, and one draw needn't show every extreme that they name: `segments`: document numbers never fall along the sequence; each of the 4 documents has 1 to 6144 tokens, one exactly that many.
All inputs are finite; a program needn't handle non-finite values.
Results may differ from the reference program's by a relative error of at most 0.0075.
Values may be sent and summed in bfloat16 or wider, within the bound.
No kernel may reach another device: no remote copies, remote signals or barrier semaphores. Data moves between devices by JAX's collectives and lax.ppermute only.
A program may use at most 192 MiB of HBM per device.

```python
import math
import jax
import jax.numpy as jnp
import numpy as np
from jax import lax

HEADS = 32
KV_HEADS = 8
HEAD_DIM = 128
TOK_DEV = 192
DOCS = 4
WIDTH = 4096
KV_WIDTH = 1024
TOKENS = 12288


def column_scales(columns, biggest):
    return biggest ** (jnp.arange(columns, dtype=jnp.float32) / (columns - 1))


def block_offsets(key, columns):
    levels = jax.random.uniform(key, (TOKENS // TOK_DEV, columns), jnp.float32, -1.0, 1.0)
    return jnp.repeat(levels, TOK_DEV, axis=0)


def draw_query_one(key, part):
    key = jax.random.fold_in(key, 11)
    base = jax.random.truncated_normal(key, -4.0, 4.0, (TOKENS, WIDTH), jnp.float32)
    scaled = base * column_scales(WIDTH, 10.0)[None, :]
    return scaled.astype(jnp.bfloat16)


def draw_value_two(key, part):
    key = jax.random.fold_in(key, 13)
    offsets = block_offsets(jax.random.fold_in(key, 1), KV_WIDTH)
    base = jax.random.truncated_normal(key, -4.0, 4.0, (TOKENS, KV_WIDTH), jnp.float32)
    scaled = (base + offsets) * column_scales(KV_WIDTH, 10.0)[None, :]
    return scaled.astype(jnp.bfloat16)


def draw_query_base(key, part):
    key = jax.random.fold_in(key, 17)
    base = jax.random.truncated_normal(key, -6.0, 6.0, (TOKENS, WIDTH), jnp.float32)
    return base.astype(jnp.bfloat16)


def draw_key_two(key, part):
    key = jax.random.fold_in(key, 19)
    base = 0.5 * jax.random.truncated_normal(key, -6.0, 6.0, (TOKENS, KV_WIDTH), jnp.float32)
    return base.astype(jnp.bfloat16)


def shard_levels(stream_key, dims, split, least, high):
    def one(dim, parts):
        steps = jax.random.uniform(jax.random.fold_in(jax.random.fold_in(stream_key, 6), dim), (parts,), jnp.float32, least / len(split), high / len(split))
        return jnp.repeat(jnp.exp(steps), dims[dim] // parts).reshape((-1,) + (1,) * (len(dims) - dim - 1))

    factor_of = one(*split[0])
    for cut in split[1:]:
        factor_of = factor_of * one(*cut)
    return factor_of


def split_up(count, total, limit, slope):
    portions = [(1 << 20) // math.isqrt(rank ** slope) + 1 for rank in range(2, count + 1)]
    surplus, holding = total - limit - (count - 1), [1] * (count - 1)
    while surplus > 0:
        movable = [i for i in range(count - 1) if holding[i] < limit]
        whole, budget = sum([portions[i] for i in movable]), surplus
        for i in movable:
            addition = min(limit - holding[i], max(1, budget * portions[i] // whole), surplus)
            holding[i] = holding[i] + addition
            surplus = surplus - addition
    return np.array([limit] + holding)


def ragged(stream_key, amount, total, reach, slope):
    if amount == 2:
        one = jax.random.randint(stream_key, (), max(1, total - reach), min(reach, total - 1) + 1)
        return jnp.stack([one, total - one])
    tallies = jnp.asarray(split_up(amount, total, reach, slope), jnp.int32)
    pairs = (amount - 1) // 2
    donor, sink = tallies[1:1 + 2 * pairs:2], tallies[2:2 + 2 * pairs:2]
    room = jnp.minimum(donor - 1, reach - sink)
    shifted = jax.random.randint(jax.random.fold_in(stream_key, 1), (pairs,), 0, 1 << 20) % (room + 1)
    tallies = tallies.at[1:1 + 2 * pairs:2].set(donor - shifted).at[2:2 + 2 * pairs:2].set(sink + shifted)
    return tallies[jax.random.permutation(jax.random.fold_in(stream_key, 2), amount)]


def normal_values(rng, shape, scale, reach, shards=(), kind=jnp.bfloat16):
    values = scale * jax.random.normal(rng, shape, jnp.float32)
    if shards:
        values = values * shard_levels(rng, shape, shards, -0.22, 0.18)
    return jnp.clip(values, -reach, reach).astype(kind)


def setup_inputs(seed: int = 0) -> dict:
    streams_of = jax.random.split(jax.random.key(seed), 8)
    return {
        "query_one": draw_query_one(jax.random.fold_in(streams_of[7], 71), 0),
        "key_one": normal_values(streams_of[1], (TOKENS, KV_WIDTH), 1.0, 6.0, ((0, 64), (1, 4))),
        "value_one": normal_values(streams_of[2], (TOKENS, KV_WIDTH), 1.0, 6.0, ((0, 64), (1, 4))),
        "segments": jnp.searchsorted(jnp.cumsum(ragged(streams_of[3], DOCS, TOKENS, TOKENS // 2, 2)), jnp.arange(TOKENS), side="right").astype(jnp.int32),
        "query_base": draw_query_base(jax.random.fold_in(streams_of[7], 71), 0),
        "key_two": draw_key_two(jax.random.fold_in(streams_of[7], 71), 0),
        "value_two": draw_value_two(jax.random.fold_in(streams_of[7], 71), 0),
    }


EPSILON = 1e-05
NEGATIVE = -1e+30
HIGHEST = lax.Precision.HIGHEST

def linear_layer(query_one, key_one, value_one, segments):
    repeat = HEADS // KV_HEADS
    blocks = TOKENS // TOK_DEV
    query_blocks = query_one.astype(jnp.float32).reshape(blocks, TOK_DEV, KV_HEADS, repeat, HEAD_DIM)
    key_blocks = key_one.astype(jnp.float32).reshape(blocks, TOK_DEV, KV_HEADS, HEAD_DIM)
    value_blocks = value_one.astype(jnp.float32).reshape(blocks, TOK_DEV, KV_HEADS, HEAD_DIM)
    segment_blocks = segments.reshape(blocks, TOK_DEV)
    places = jnp.arange(TOK_DEV, dtype=jnp.int32)
    causal = places[None, :] <= places[:, None]

    def advance(carried_in, block_item):
        running, open_doc = carried_in
        queries, keys_now, values_now, doc_ids = block_item
        scores = jnp.einsum('rgpd,sgd->gprs', queries, keys_now, precision=HIGHEST)
        visible = causal & (doc_ids[None, :] == doc_ids[:, None])
        scores = jnp.where(visible, scores, 0.0)
        inside = jnp.einsum('gprs,sge->rgpe', scores, values_now, precision=HIGHEST)
        earlier = jnp.einsum('rgpd,gde->rgpe', queries, running, precision=HIGHEST)
        earlier = jnp.where((doc_ids == open_doc)[:, None, None, None], earlier, 0.0)
        last_doc = doc_ids[TOK_DEV - 1]
        in_last = (doc_ids == last_doc)[:, None, None]
        new_state = jnp.einsum('rgd,rge->gde', jnp.where(in_last, keys_now, 0.0), values_now, precision=HIGHEST)
        running = new_state + jnp.where(open_doc == last_doc, running, 0.0)
        return ((running, last_doc), inside + earlier)
    start_state = (jnp.zeros((KV_HEADS, HEAD_DIM, HEAD_DIM), jnp.float32), jnp.int32(-1))
    outputs = lax.scan(advance, start_state, (query_blocks, key_blocks, value_blocks, segment_blocks))[1]
    return outputs.reshape(TOKENS, HEADS * HEAD_DIM)

def softmax_layer(query_two, key_two, value_two, segments):
    repeat = HEADS // KV_HEADS
    blocks = TOKENS // TOK_DEV
    query_blocks = query_two.reshape(blocks, TOK_DEV, KV_HEADS, repeat, HEAD_DIM)
    key_heads = jnp.moveaxis(key_two.reshape(TOKENS, KV_HEADS, HEAD_DIM), 1, 0)
    value_heads = jnp.moveaxis(value_two.reshape(TOKENS, KV_HEADS, HEAD_DIM), 1, 0)
    positions = jnp.arange(TOKENS, dtype=jnp.int32)
    score_scale = HEAD_DIM ** (-0.5)

    def one_block(block_item):
        queries, offset = block_item
        query_pos = offset + jnp.arange(TOK_DEV, dtype=jnp.int32)
        query_doc = lax.dynamic_slice_in_dim(segments, offset, TOK_DEV)
        visible = (positions[None, :] <= query_pos[:, None]) & (segments[None, :] == query_doc[:, None])

        def one_head(head_item):
            head_queries, head_keys, head_values = head_item
            scores = jnp.einsum('rpd,sd->prs', head_queries.astype(jnp.float32), head_keys.astype(jnp.float32), precision=HIGHEST) * score_scale
            scores = jnp.where(visible, scores, NEGATIVE)
            highest_score = lax.optimization_barrier(jnp.max(scores, axis=-1, keepdims=True))
            unrounded = jnp.where(visible, jnp.exp(scores - highest_score), 0.0)
            totals = lax.optimization_barrier(jnp.sum(unrounded, axis=-1))
            rounded = lax.optimization_barrier(unrounded.astype(jnp.bfloat16))
            summed = jnp.einsum('prs,sd->prd', rounded.astype(jnp.float32), head_values.astype(jnp.float32), precision=HIGHEST)
            return summed / totals[:, :, None]
        per_head = lax.map(one_head, (jnp.moveaxis(queries, 1, 0), key_heads, value_heads))
        return jnp.transpose(per_head, (2, 0, 1, 3)).reshape(TOK_DEV, HEADS * HEAD_DIM)
    offsets = jnp.arange(blocks, dtype=jnp.int32) * TOK_DEV
    mixed_blocks = lax.map(one_block, (query_blocks, offsets))
    return mixed_blocks.reshape(TOKENS, HEADS * HEAD_DIM).astype(jnp.bfloat16)

def reference(query_one, key_one, value_one, segments, query_base, key_two, value_two):
    first_out = linear_layer(query_one, key_one, value_one, segments)
    first_rms = lax.optimization_barrier(jnp.mean(first_out * first_out, axis=1, keepdims=True))
    query_two = (query_base.astype(jnp.float32) + first_out * lax.rsqrt(first_rms + EPSILON)).astype(jnp.bfloat16)
    second_out = softmax_layer(query_two, key_two, value_two, segments)
    widened = second_out.astype(jnp.float32)
    second_rms = lax.optimization_barrier(jnp.mean(widened * widened, axis=1, keepdims=True))
    return (widened * lax.rsqrt(second_rms + EPSILON)).astype(jnp.bfloat16)
```

```python
import jax
import jax.numpy as jnp
from jax import lax
from jax.experimental import pallas as pl
from jax.experimental.pallas import tpu as pltpu
from jax.sharding import PartitionSpec as P

HEAD_DIM = 128
WIDTH = 4096
EPSILON = 1e-05
NEGATIVE = -1e30

TOK = 192
PAIR = 384
REPEAT = 4
COLS = REPEAT * HEAD_DIM
Z, X, CORES, TP = 8, 4, 2, 4
BACK = 4
PRIOR = 16 * PAIR
CHUNK = 768
SCALE = HEAD_DIM ** (-0.5) * 1.4426950408889634

F32 = jnp.float32
BF16 = jnp.bfloat16
VMEM = pl.BlockSpec(memory_space=pltpu.VMEM)
SMEM = pl.BlockSpec(memory_space=pltpu.SMEM)
ANY = pl.BlockSpec(memory_space=pl.ANY)


def place():
    index = lax.axis_index("ctx")
    return index // (X * CORES), (index // CORES) % X, index % CORES


def call(kernel, outs, specs_in, specs_out, scratch=(), limit=None, name=None):
    return pl.pallas_call(
        kernel,
        out_shape=outs,
        in_specs=specs_in,
        out_specs=specs_out,
        scratch_shapes=list(scratch),
        compiler_params=pltpu.CompilerParams(vmem_limit_bytes=limit or 16 * 2**20),
        name=name,
    )


def count_below(ref, doc):
    found = jnp.int32(0)
    for step in (128, 64, 32, 16, 8, 4, 2, 1):
        tried = found + step
        last = ref[jnp.minimum(tried, TOK) - 1]
        found = jnp.where((tried <= TOK) & (last < doc), tried, found)
    return found


def half(core):
    return pl.ds(pl.multiple_of(core * HEAD_DIM, HEAD_DIM), HEAD_DIM)


def rows_of(core):
    return pl.ds(pl.multiple_of(core * TOK, 64), TOK)


def prep_kernel(
    seg, seg_r, k1, k1_r, v1, v1_r, k2, k2_r, v2, v2_r, pack_ref, state_ref, info_ref
):
    core = place()[2]
    mine, theirs = rows_of(core), rows_of(1 - core)
    pack_ref[mine, :HEAD_DIM] = k2[:, half(core)]
    pack_ref[mine, HEAD_DIM:] = v2[:, half(core)]
    pack_ref[theirs, :HEAD_DIM] = k2_r[:, half(core)]
    pack_ref[theirs, HEAD_DIM:] = v2_r[:, half(core)]
    below = [count_below(seg, d) for d in (1, 2, 3)]
    below_r = [count_below(seg_r, d) for d in (1, 2, 3)]
    bounds = [a + b for a, b in zip(below, below_r)]
    first = jnp.where(core == 0, seg[0], seg_r[0])
    last = jnp.where(core == 0, seg_r[TOK - 1], seg[TOK - 1])

    def pick(values, doc):
        out = jnp.int32(0)
        for d in (1, 2, 3):
            out = jnp.where(doc == d, values[d - 1], out)
        return out

    count = PAIR - pick(bounds, last)
    first_end = jnp.where(first == 3, PAIR, pick(bounds, first + 1))
    for place_in, value in enumerate((*bounds, first, last, count, first_end, 0)):
        info_ref[place_in] = jnp.int32(value)
    rows = lax.broadcasted_iota(jnp.int32, (TOK, HEAD_DIM), 0)
    state = jnp.zeros((HEAD_DIM, HEAD_DIM), F32)
    for keys, values, start in ((k1, v1, pick(below, last)), (k1_r, v1_r, pick(below_r, last))):
        masked = jnp.where(rows >= start, keys[:, half(core)].astype(F32), 0.0).astype(BF16)
        state += lax.dot_general(
            masked, values[:, half(core)], (((0,), (0,)), ((), ())), preferred_element_type=F32
        )
    state_ref[:HEAD_DIM] = state.astype(BF16)
    state_ref[HEAD_DIM:] = notes(last.astype(F32), count.astype(F32)).astype(BF16)


def notes(last, count):
    row = lax.broadcasted_iota(jnp.int32, (16, HEAD_DIM), 0)
    high = jnp.floor(count * (1.0 / 64.0))
    return jnp.where(
        row == 0, last, jnp.where(row == 1, high, jnp.where(row == 2, count - 64.0 * high, 0.0))
    )


def read_state(ref):
    tail = ref[HEAD_DIM:].astype(F32)
    return ref[:HEAD_DIM].astype(F32), tail[0:1], tail[1:2] * 64.0 + tail[2:3]


def plane_kernel(info, own, from1, from2, from3, prefix_ref, plane_ref):
    x = place()[1]
    first = info[3].astype(F32)
    items = [read_state(ref) for ref in (own, from1, from2, from3)]
    prefix = jnp.zeros((HEAD_DIM, HEAD_DIM), F32)
    prefix_count = jnp.zeros((1, HEAD_DIM), F32)
    for shift in (1, 2, 3):
        state, doc, count = items[shift]
        chosen = jnp.where((doc == first) & (x >= shift), 1.0, 0.0)
        prefix += state * chosen
        prefix_count += count * chosen
    prefix_ref[:HEAD_DIM] = prefix
    prefix_ref[HEAD_DIM:] = jnp.broadcast_to(prefix_count, (8, HEAD_DIM))
    last = items[0][1]
    for item in items[1:]:
        last = jnp.maximum(last, item[1])
    total = jnp.zeros((HEAD_DIM, HEAD_DIM), F32)
    total_count = jnp.zeros((1, HEAD_DIM), F32)
    for state, doc, count in items:
        chosen = jnp.where(doc == last, 1.0, 0.0)
        total += state * chosen
        total_count += count * chosen
    plane_ref[:HEAD_DIM] = total.astype(BF16)
    plane_ref[HEAD_DIM:] = notes(last, total_count).astype(BF16)


def document_start(info, rows):
    start = jnp.zeros_like(rows)
    for d in range(3):
        start = jnp.where(rows >= info[d], jnp.maximum(start, info[d]), start)
    return start


def split_dot(wide, narrow):
    high = wide.astype(BF16)
    low = (wide - high.astype(F32)).astype(BF16)
    return jnp.dot(high, narrow, preferred_element_type=F32) + jnp.dot(
        low, narrow, preferred_element_type=F32
    )


def inside_kernel(info, q1, q1_r, k1, k1_r, v1, v1_r, inside_ref, query_ref, keys, values):
    core = place()[2]
    mine, theirs = rows_of(core), rows_of(1 - core)
    own_cols = pl.ds(pl.multiple_of(core * COLS, COLS), COLS)
    query_ref[mine, :] = q1[:, own_cols]
    query_ref[theirs, :] = q1_r[:, own_cols]
    keys[mine, :] = k1[:, half(core)]
    keys[theirs, :] = k1_r[:, half(core)]
    values[mine, :] = v1[:, half(core)]
    values[theirs, :] = v1_r[:, half(core)]
    row = lax.broadcasted_iota(jnp.int32, (PAIR, PAIR), 0)
    column = lax.broadcasted_iota(jnp.int32, (PAIR, PAIR), 1)
    visible = (column <= row) & (column >= document_start(info, row))
    for head in range(REPEAT):
        cols = slice(head * HEAD_DIM, (head + 1) * HEAD_DIM)
        scores = lax.dot_general(
            query_ref[:, cols], keys[...], (((1,), (1,)), ((), ())), preferred_element_type=F32
        )
        scores = jnp.where(visible, scores, 0.0)
        inside_ref[:, cols] = split_dot(scores, values[...])


def row_sums(squares):
    high = squares.astype(BF16)
    low = (squares - high.astype(F32)).astype(BF16)
    ones = jnp.ones((8, squares.shape[1]), BF16)
    dims = (((1,), (1,)), ((), ()))
    return lax.dot_general(ones, high, dims, preferred_element_type=F32) + lax.dot_general(
        ones, low, dims, preferred_element_type=F32
    )


def first_kernel(
    info, prefix, from1, from2, from3, from4, inside, query, first_ref, sums_ref, count_ref
):
    z = place()[0]
    first = info[3].astype(F32)
    state = prefix[:HEAD_DIM]
    count = prefix[HEAD_DIM : HEAD_DIM + 1]
    for back, ref in enumerate((from1, from2, from3, from4), 1):
        one_state, doc, one_count = read_state(ref)
        chosen = jnp.where((doc == first) & (z >= back), 1.0, 0.0)
        state += one_state * chosen
        count += one_count * chosen
    count_ref[0] = jnp.max(count).astype(jnp.int32)
    high = state.astype(BF16)
    low = (state - high.astype(F32)).astype(BF16)
    in_first = lax.broadcasted_iota(jnp.int32, (PAIR, HEAD_DIM), 0) < info[6]
    squares = jnp.zeros((PAIR, HEAD_DIM), F32)
    for head in range(REPEAT):
        cols = slice(head * HEAD_DIM, (head + 1) * HEAD_DIM)
        queries = query[:, cols]
        earlier = jnp.dot(queries, high, preferred_element_type=F32) + jnp.dot(
            queries, low, preferred_element_type=F32
        )
        out = inside[:, cols] + jnp.where(in_first, earlier, 0.0)
        first_ref[:, cols] = out
        squares += out * out
    sums_ref[...] = row_sums(squares)


def row_scale(parts):
    total = parts[0][...]
    for part in parts[1:]:
        total = total + part[...]
    return lax.transpose(lax.rsqrt(total * (1.0 / WIDTH) + EPSILON), (1, 0))[:, :1]


def attention_kernel(*refs):
    info, reach, sum0, sum1, sum2, sum3, first, base, base_r = refs[:9]
    packs = refs[9 : 9 + 20]
    mine_ref, send_ref, mine_sums, send_sums = refs[29:33]
    kv, queries, tops, acc, scales, sems = refs[33:]
    _, x, core = place()
    prior = reach[0]
    low = PRIOR - prior
    chunk_first = low // CHUNK
    row_first = chunk_first * CHUNK

    def each_pack(act):
        for back in range(BACK + 1):
            for shift in range(X):
                if back == 0 and shift == 0:
                    distance = jnp.int32(0)
                else:
                    distance = 4 * back + shift - jnp.where(x < shift, 4, 0)
                start = (16 - distance) * PAIR
                needed = (distance >= 0) & (distance <= 16) & (start + PAIR > row_first)

                @pl.when(needed)
                def _():
                    at = pl.multiple_of(jnp.maximum(start, 0), PAIR)
                    act(
                        pltpu.make_async_copy(
                            packs[back * X + shift],
                            kv.at[pl.ds(at, PAIR), pl.ds(0, 2 * HEAD_DIM)],
                            sems.at[back * X + shift],
                        )
                    )

    each_pack(lambda copy: copy.start())
    kv[:, 2 * HEAD_DIM :] = jnp.ones((PRIOR + PAIR, HEAD_DIM), BF16)
    scales[...] = jnp.broadcast_to(row_scale((sum0, sum1, sum2, sum3)), (PAIR, HEAD_DIM))
    for part, where in ((base, rows_of(core)), (base_r, rows_of(1 - core))):
        for head in range(REPEAT):
            cols = pl.ds(pl.multiple_of(core * COLS + head * HEAD_DIM, HEAD_DIM), HEAD_DIM)
            value = part[:, cols].astype(F32) + (
                first[where, head * HEAD_DIM : (head + 1) * HEAD_DIM] * scales[where, :]
            )
            queries[head, where, :] = value.astype(BF16)
    tops[...] = jnp.full(tops.shape, NEGATIVE, F32)
    acc[...] = jnp.zeros(acc.shape, F32)
    each_pack(lambda copy: copy.wait())

    def absorb(head, start, length, visible):
        rows = pl.ds(start, length)
        scores = lax.dot_general(
            queries[head], kv[rows, :HEAD_DIM], (((1,), (1,)), ((), ())), preferred_element_type=F32
        )
        if visible is not None:
            scores = jnp.where(visible, scores, NEGATIVE)
        old_top = tops[head]
        top = jnp.maximum(old_top, jnp.max(scores, axis=1, keepdims=True))
        wide_top = jnp.concatenate([top] * (length // HEAD_DIM), axis=1)
        weights = jnp.exp2((scores - wide_top) * SCALE)
        if visible is not None:
            weights = jnp.where(visible, weights, 0.0)
        shrink = jnp.exp2((old_top - top) * SCALE)
        tops[head] = top
        acc[head] = acc[head] * jnp.concatenate([shrink, shrink], axis=1) + jnp.dot(
            weights.astype(BF16), kv[rows, HEAD_DIM:], preferred_element_type=F32
        )

    @pl.when(prior > 0)
    def _():
        column = lax.broadcasted_iota(jnp.int32, (PAIR, CHUNK), 1)
        visible = column >= low - row_first
        for head in range(REPEAT):
            absorb(head, pl.multiple_of(row_first, CHUNK), CHUNK, visible)

    @pl.loop(chunk_first + 1, PRIOR // CHUNK)
    def _(chunk):
        for head in range(REPEAT):
            absorb(head, pl.multiple_of(chunk * CHUNK, CHUNK), CHUNK, None)

    @pl.when(info[6] < PAIR)
    def _():
        in_first = lax.broadcasted_iota(jnp.int32, (PAIR, HEAD_DIM), 0) < info[6]
        for head in range(REPEAT):
            tops[head] = jnp.where(in_first, tops[head], NEGATIVE)
            acc[head] = jnp.where(jnp.concatenate([in_first, in_first], axis=1), acc[head], 0.0)

    row = lax.broadcasted_iota(jnp.int32, (PAIR, PAIR), 0)
    column = lax.broadcasted_iota(jnp.int32, (PAIR, PAIR), 1)
    visible = (column <= row) & (column >= document_start(info, row))
    for head in range(REPEAT):
        absorb(head, PRIOR, PAIR, visible)

    for out_ref, out_sums, where in (
        (mine_ref, mine_sums, rows_of(core)),
        (send_ref, send_sums, rows_of(1 - core)),
    ):
        squares = jnp.zeros((TOK, HEAD_DIM), F32)
        for head in range(REPEAT):
            summed = acc[head, where, :]
            out = (summed[:, :HEAD_DIM] / summed[:, HEAD_DIM:]).astype(BF16)
            out_ref[:, head * HEAD_DIM : (head + 1) * HEAD_DIM] = out
            widened = out.astype(F32)
            squares += widened * widened
        out_sums[...] = row_sums(squares)


def last_kernel(sum0, sum1, sum2, sum3, mine, theirs, out_ref):
    core = place()[2]
    scale = row_scale((sum0, sum1, sum2, sum3))
    for ref, side in ((mine, core), (theirs, 1 - core)):
        cols = pl.ds(pl.multiple_of(side * COLS, COLS), COLS)
        out_ref[:, cols] = (ref[...].astype(F32) * scale).astype(BF16)


def along(z_shift=0, x_shift=0, core_shift=0, keep=lambda z, x: True):
    pairs = []
    for z in range(Z):
        for x in range(X):
            for core in range(CORES):
                if keep(z, x):
                    to = ((z + z_shift) % Z * X + (x + x_shift) % X) * CORES
                    pairs.append(((z * X + x) * CORES + core, to + (core + core_shift) % CORES))
    return pairs


def swap(value):
    return lax.ppermute(value, "ctx", along(core_shift=1))


def over_tp(value):
    return [value] + [
        lax.ppermute(value, "tp", [(i, (i + shift) % TP) for i in range(TP)]) for shift in (1, 2, 3)
    ]


def shape(dims, kind):
    return jax.ShapeDtypeStruct(dims, kind)


def shards(query_one, key_one, value_one, segments, query_base, key_two, value_two):
    segments_r = swap(segments)
    k1_r, v1_r, k2_r, v2_r = swap(key_one), swap(value_one), swap(key_two), swap(value_two)
    q1_r, base_r = swap(query_one), swap(query_base)

    pack, state, info = call(
        prep_kernel,
        (shape((PAIR, 2 * HEAD_DIM), BF16), shape((144, HEAD_DIM), BF16), shape((8,), jnp.int32)),
        [SMEM, SMEM] + [VMEM] * 8,
        (VMEM, VMEM, SMEM),
        name="prep",
    )(segments, segments_r, key_one, k1_r, value_one, v1_r, key_two, k2_r, value_two, v2_r)

    columns = [pack]
    for back in range(BACK):
        columns.append(lax.ppermute(columns[-1], "ctx", along(z_shift=1)))
    packs = []
    for back in range(BACK + 1):
        packs.append(columns[back])
        for shift in (1, 2, 3):
            if back == 0:
                pairs = along(x_shift=shift, keep=lambda z, x: x + shift < X)
            elif back == BACK:
                pairs = along(x_shift=shift, keep=lambda z, x: x + shift >= X)
            else:
                pairs = along(x_shift=shift)
            packs.append(lax.ppermute(columns[back], "ctx", pairs))

    near = [lax.ppermute(state, "ctx", along(x_shift=shift)) for shift in (1, 2, 3)]
    prefix, plane = call(
        plane_kernel,
        (shape((HEAD_DIM + 8, HEAD_DIM), F32), shape((144, HEAD_DIM), BF16)),
        [SMEM] + [VMEM] * 4,
        (VMEM, VMEM),
        name="plane",
    )(info, state, *near)
    far = [lax.ppermute(plane, "ctx", along(z_shift=back)) for back in (1, 2, 3, 4)]

    inside, query = call(
        inside_kernel,
        (shape((PAIR, COLS), F32), shape((PAIR, COLS), BF16)),
        [SMEM] + [VMEM] * 6,
        (VMEM, VMEM),
        scratch=(pltpu.VMEM((PAIR, HEAD_DIM), BF16), pltpu.VMEM((PAIR, HEAD_DIM), BF16)),
        name="inside",
    )(info, query_one, q1_r, key_one, k1_r, value_one, v1_r)
    first, sums, reach = call(
        first_kernel,
        (shape((PAIR, COLS), F32), shape((8, PAIR), F32), shape((1,), jnp.int32)),
        [SMEM] + [VMEM] * 7,
        (VMEM, VMEM, SMEM),
        name="first",
    )(info, prefix, *far, inside, query)
    all_sums = over_tp(sums + swap(sums))

    mine, send, mine_sums, send_sums = call(
        attention_kernel,
        (
            shape((TOK, COLS), BF16),
            shape((TOK, COLS), BF16),
            shape((8, TOK), F32),
            shape((8, TOK), F32),
        ),
        [SMEM, SMEM] + [VMEM] * 7 + [ANY] * 20,
        (VMEM,) * 4,
        scratch=(
            pltpu.VMEM((PRIOR + PAIR, 3 * HEAD_DIM), BF16),
            pltpu.VMEM((REPEAT, PAIR, HEAD_DIM), BF16),
            pltpu.VMEM((REPEAT, PAIR, HEAD_DIM), F32),
            pltpu.VMEM((REPEAT, PAIR, 2 * HEAD_DIM), F32),
            pltpu.VMEM((PAIR, HEAD_DIM), F32),
            pltpu.SemaphoreType.DMA((20,)),
        ),
        limit=40 * 2**20,
        name="attention",
    )(info, reach, *all_sums, first, query_base, base_r, *packs)
    theirs = swap(send)
    out_sums = over_tp(mine_sums + swap(send_sums))
    return call(
        last_kernel, shape((TOK, 2 * COLS), BF16), [VMEM] * 6, VMEM, name="last"
    )(*out_sums, mine, theirs)


def solution(mesh):
    return jax.shard_map(
        shards,
        mesh=mesh,
        in_specs=(P("ctx", "tp"),) * 3 + (P("ctx"),) + (P("ctx", "tp"),) * 3,
        out_specs=P("ctx", "tp"),
        check_vma=False,
    )
```

```python
import jax
import jax.numpy as jnp
from jax import lax
from jax.experimental import pallas as pl
from jax.experimental.pallas import tpu as pltpu
from jax.sharding import Mesh, PartitionSpec as P

HEAD_DIM = 128
WIDTH = 4096
EPSILON = 1e-05
NEGATIVE = -1e30

TOK = 192
PAIR = 384
REPEAT = 4
COLS = REPEAT * HEAD_DIM
Z, X, CORES, TP = 8, 4, 2, 4
BACK = 4
PRIOR = 16 * PAIR
CHUNK = 1536
SCALE = HEAD_DIM ** (-0.5) * 1.4426950408889634

F32 = jnp.float32
BF16 = jnp.bfloat16
VMEM = pl.BlockSpec(memory_space=pltpu.VMEM)
SMEM = pl.BlockSpec(memory_space=pltpu.SMEM)
ANY = pl.BlockSpec(memory_space=pl.ANY)


def place():
    return lax.axis_index("z"), lax.axis_index("x"), lax.axis_index("core")


def call(kernel, outs, specs_in, specs_out, scratch=(), limit=None, name=None):
    return pl.pallas_call(
        kernel,
        out_shape=outs,
        in_specs=specs_in,
        out_specs=specs_out,
        scratch_shapes=list(scratch),
        compiler_params=pltpu.CompilerParams(vmem_limit_bytes=limit or 16 * 2**20),
        name=name,
    )


def count_below(ref, doc):
    found = jnp.int32(0)
    for step in (128, 64, 32, 16, 8, 4, 2, 1):
        tried = found + step
        last = ref[jnp.minimum(tried, TOK) - 1]
        found = jnp.where((tried <= TOK) & (last < doc), tried, found)
    return found


def half(core):
    return pl.ds(pl.multiple_of(core * HEAD_DIM, HEAD_DIM), HEAD_DIM)


def rows_of(core):
    return pl.ds(pl.multiple_of(core * TOK, 64), TOK)


def prep_kernel(
    seg_any, seg_r, k1_any, k1_r, v1_any, v1_r, k2_any, k2_r, v2_any, v2_r, q1_any, base_any,
    pack_ref, state_ref, query_ref, info_ref, seg, k1, v1, sems
):
    core = place()[2]
    mine, theirs = rows_of(core), rows_of(1 - core)
    other_cols = pl.ds(pl.multiple_of((1 - core) * COLS, COLS), COLS)
    copies = [
        pltpu.make_async_copy(source, to, sems.at[at])
        for at, (source, to) in enumerate(
            (
                (seg_any, seg),
                (k1_any.at[:, half(core)], k1),
                (v1_any.at[:, half(core)], v1),
                (k2_any.at[:, half(core)], pack_ref.at[mine, pl.ds(0, HEAD_DIM)]),
                (v2_any.at[:, half(core)], pack_ref.at[mine, pl.ds(HEAD_DIM, HEAD_DIM)]),
                (q1_any.at[:, other_cols], query_ref.at[0]),
                (base_any.at[:, other_cols], query_ref.at[1]),
            )
        )
    ]
    for copy in copies:
        copy.start()
    pack_ref[theirs, :HEAD_DIM] = k2_r[:, half(core)]
    pack_ref[theirs, HEAD_DIM:] = v2_r[:, half(core)]
    for copy in copies:
        copy.wait()
    below = [count_below(seg, d) for d in (1, 2, 3)]
    below_r = [count_below(seg_r, d) for d in (1, 2, 3)]
    bounds = [a + b for a, b in zip(below, below_r)]
    first = jnp.where(core == 0, seg[0], seg_r[0])
    last = jnp.where(core == 0, seg_r[TOK - 1], seg[TOK - 1])

    def pick(values, doc):
        out = jnp.int32(0)
        for d in (1, 2, 3):
            out = jnp.where(doc == d, values[d - 1], out)
        return out

    count = PAIR - pick(bounds, last)
    first_end = jnp.where(first == 3, PAIR, pick(bounds, first + 1))
    for place_in, value in enumerate((*bounds, first, last, count, first_end, 0)):
        info_ref[place_in] = jnp.int32(value)
    rows = lax.broadcasted_iota(jnp.int32, (TOK, HEAD_DIM), 0)
    state = jnp.zeros((HEAD_DIM, HEAD_DIM), F32)
    for keys, values, start in (
        (k1[...], v1[...], pick(below, last)),
        (k1_r[:, half(core)], v1_r[:, half(core)], pick(below_r, last)),
    ):
        masked = jnp.where(rows >= start, keys.astype(F32), 0.0).astype(BF16)
        state += lax.dot_general(
            masked, values, (((0,), (0,)), ((), ())), preferred_element_type=F32
        )
    state_ref[:HEAD_DIM] = state.astype(BF16)
    state_ref[HEAD_DIM:] = notes(last.astype(F32), count.astype(F32)).astype(BF16)


def notes(last, count):
    row = lax.broadcasted_iota(jnp.int32, (16, HEAD_DIM), 0)
    high = jnp.floor(count * (1.0 / 64.0))
    return jnp.where(
        row == 0, last, jnp.where(row == 1, high, jnp.where(row == 2, count - 64.0 * high, 0.0))
    )


def read_state(ref):
    tail = ref[HEAD_DIM:].astype(F32)
    return ref[:HEAD_DIM].astype(F32), tail[0:1], tail[1:2] * 64.0 + tail[2:3]


def plane_kernel(info, own, from1, from2, from3, prefix_ref, plane_ref):
    x = place()[1]
    first = info[3].astype(F32)
    items = [read_state(ref) for ref in (own, from1, from2, from3)]
    prefix = jnp.zeros((HEAD_DIM, HEAD_DIM), F32)
    prefix_count = jnp.zeros((1, HEAD_DIM), F32)
    for shift in (1, 2, 3):
        state, doc, count = items[shift]
        chosen = jnp.where((doc == first) & (x >= shift), 1.0, 0.0)
        prefix += state * chosen
        prefix_count += count * chosen
    prefix_ref[:HEAD_DIM] = prefix
    prefix_ref[HEAD_DIM:] = jnp.broadcast_to(prefix_count, (8, HEAD_DIM))
    last = items[0][1]
    for item in items[1:]:
        last = jnp.maximum(last, item[1])
    total = jnp.zeros((HEAD_DIM, HEAD_DIM), F32)
    total_count = jnp.zeros((1, HEAD_DIM), F32)
    for state, doc, count in items:
        chosen = jnp.where(doc == last, 1.0, 0.0)
        total += state * chosen
        total_count += count * chosen
    plane_ref[:HEAD_DIM] = total.astype(BF16)
    plane_ref[HEAD_DIM:] = notes(last, total_count).astype(BF16)


def document_start(info, rows):
    start = jnp.zeros_like(rows)
    for d in range(3):
        start = jnp.where(rows >= info[d], jnp.maximum(start, info[d]), start)
    return start


def split_dot(wide, narrow):
    high = wide.astype(BF16)
    low = (wide - high.astype(F32)).astype(BF16)
    return jnp.dot(high, narrow, preferred_element_type=F32) + jnp.dot(
        low, narrow, preferred_element_type=F32
    )


def inside_kernel(
    info, q1_any, queries_r, k1_any, k1_r, v1_any, v1_r, inside_ref, query_ref, keys, values, sems
):
    core = place()[2]
    mine, theirs = rows_of(core), rows_of(1 - core)
    own_cols = pl.ds(pl.multiple_of(core * COLS, COLS), COLS)
    copies = [
        pltpu.make_async_copy(source, to, sems.at[at])
        for at, (source, to) in enumerate(
            (
                (q1_any.at[:, own_cols], query_ref.at[mine, :]),
                (k1_any.at[:, half(core)], keys.at[mine, :]),
                (v1_any.at[:, half(core)], values.at[mine, :]),
            )
        )
    ]
    for copy in copies:
        copy.start()
    query_ref[theirs, :] = queries_r[0]
    keys[theirs, :] = k1_r[:, half(core)]
    values[theirs, :] = v1_r[:, half(core)]
    for copy in copies:
        copy.wait()
    row = lax.broadcasted_iota(jnp.int32, (PAIR, PAIR), 0)
    column = lax.broadcasted_iota(jnp.int32, (PAIR, PAIR), 1)
    visible = (column <= row) & (column >= document_start(info, row))
    for head in range(REPEAT):
        cols = slice(head * HEAD_DIM, (head + 1) * HEAD_DIM)
        scores = lax.dot_general(
            query_ref[:, cols], keys[...], (((1,), (1,)), ((), ())), preferred_element_type=F32
        )
        scores = jnp.where(visible, scores, 0.0)
        inside_ref[:, cols] = split_dot(scores, values[...])


def row_sums(squares):
    high = squares.astype(BF16)
    low = (squares - high.astype(F32)).astype(BF16)
    ones = jnp.ones((8, squares.shape[1]), BF16)
    dims = (((1,), (1,)), ((), ()))
    return lax.dot_general(ones, high, dims, preferred_element_type=F32) + lax.dot_general(
        ones, low, dims, preferred_element_type=F32
    )


def first_kernel(
    info, prefix, from1, from2, from3, from4, inside, query, first_ref, sums_ref, count_ref
):
    z = place()[0]
    first = info[3].astype(F32)
    state = prefix[:HEAD_DIM]
    count = prefix[HEAD_DIM : HEAD_DIM + 1]
    for back, ref in enumerate((from1, from2, from3, from4), 1):
        one_state, doc, one_count = read_state(ref)
        chosen = jnp.where((doc == first) & (z >= back), 1.0, 0.0)
        state += one_state * chosen
        count += one_count * chosen
    count_ref[0] = jnp.max(count).astype(jnp.int32)
    high = state.astype(BF16)
    low = (state - high.astype(F32)).astype(BF16)
    in_first = lax.broadcasted_iota(jnp.int32, (PAIR, HEAD_DIM), 0) < info[6]
    squares = jnp.zeros((PAIR, HEAD_DIM), F32)
    for head in range(REPEAT):
        cols = slice(head * HEAD_DIM, (head + 1) * HEAD_DIM)
        queries = query[:, cols]
        earlier = jnp.dot(queries, high, preferred_element_type=F32) + jnp.dot(
            queries, low, preferred_element_type=F32
        )
        out = inside[:, cols] + jnp.where(in_first, earlier, 0.0)
        first_ref[:, cols] = out
        squares += out * out
    sums = row_sums(squares)
    for to in range(CORES * TP):
        sums_ref[to] = sums


def row_scale(sums):
    total = sums[0]
    for device in range(1, CORES * TP):
        total = total + sums[device]
    return lax.transpose(lax.rsqrt(total * (1.0 / WIDTH) + EPSILON), (1, 0))[:, :1]


TILE = 128
TILES = [(head, slice(at, at + TILE)) for head in range(REPEAT) for at in range(0, PAIR, TILE)]


def attention_kernel(
    info, reach, sums, first, base_any, queries_r, own0, own1, own23, own4, *refs
):
    gathered = refs[:9]
    mine_ref, send_ref, sums_ref = refs[9:12]
    kv, queries, tops, acc, scales, base, sems = refs[12:]
    _, x, core = place()
    own_cols = pl.ds(pl.multiple_of(core * COLS, COLS), COLS)
    base_copy = pltpu.make_async_copy(base_any.at[:, own_cols], base, sems.at[20])
    base_copy.start()
    prior = reach[0]
    low = PRIOR - prior
    chunk_first = low // CHUNK
    row_first = chunk_first * CHUNK

    upper, lower = pl.ds(0, PAIR), pl.ds(PAIR, PAIR)
    packs = [(own0, 0), (own1, 4), (own23.at[upper], 8), (own23.at[lower], 12), (own4, 16)]
    for shift in (1, 2, 3):
        wrapped = jnp.where(x < shift, 4, 0)
        packs.append((gathered[shift - 1], 4 + shift - wrapped))
        packs.append((gathered[shift + 2], shift + 3 * wrapped))
        packs.append((gathered[shift + 5].at[upper], 8 + shift - wrapped))
        packs.append((gathered[shift + 5].at[lower], 12 + shift - wrapped))

    def each_pack(act):
        for at, (ref, distance) in enumerate(packs):
            start = (16 - jnp.int32(distance)) * PAIR

            @pl.when(start + PAIR > row_first)
            def _():
                rows = pl.ds(pl.multiple_of(start, PAIR), PAIR)
                act(pltpu.make_async_copy(ref, kv.at[rows, pl.ds(0, 2 * HEAD_DIM)], sems.at[at]))

    each_pack(lambda copy: copy.start())
    kv[:, 2 * HEAD_DIM :] = jnp.ones((PRIOR + PAIR, HEAD_DIM), BF16)
    scales[...] = jnp.broadcast_to(row_scale(sums), (PAIR, HEAD_DIM))
    tops[...] = jnp.full(tops.shape, NEGATIVE, F32)
    acc[...] = jnp.zeros(acc.shape, F32)
    base_copy.wait()
    for part, where in ((base, rows_of(core)), (queries_r.at[1], rows_of(1 - core))):
        for head in range(REPEAT):
            cols = slice(head * HEAD_DIM, (head + 1) * HEAD_DIM)
            value = part[:, cols].astype(F32) + first[where, cols] * scales[where, :]
            queries[head, where, :] = value.astype(BF16)
    each_pack(lambda copy: copy.wait())

    def scores_of(head, part, rows):
        return lax.dot_general(
            queries[head, part],
            kv[rows, :HEAD_DIM],
            (((1,), (1,)), ((), ())),
            preferred_element_type=F32,
        )

    def update(head, part, scores, rows, visible):
        if visible is not None:
            scores = jnp.where(visible, scores, NEGATIVE)
        old_top = tops[head, part]
        top = jnp.maximum(old_top, jnp.max(scores, axis=1, keepdims=True))
        wide_top = jnp.concatenate([top] * (scores.shape[1] // HEAD_DIM), axis=1)
        weights = jnp.exp2((scores - wide_top) * SCALE)
        if visible is not None:
            weights = jnp.where(visible, weights, 0.0)
        shrink = jnp.exp2((old_top - top) * SCALE)
        tops[head, part] = top
        acc[head, part] = acc[head, part] * jnp.concatenate([shrink, shrink], axis=1) + jnp.dot(
            weights.astype(BF16), kv[rows, HEAD_DIM:], preferred_element_type=F32
        )

    def sweep(start, length, visible):
        rows = pl.ds(start, length)
        ahead = scores_of(*TILES[0], rows)
        for at, (head, part) in enumerate(TILES):
            scores = ahead
            if at + 1 < len(TILES):
                ahead = scores_of(*TILES[at + 1], rows)
            update(head, part, scores, rows, None if visible is None else visible(part))

    @pl.when(prior > 0)
    def _():
        column = lax.broadcasted_iota(jnp.int32, (TILE, CHUNK), 1)
        sweep(pl.multiple_of(row_first, CHUNK), CHUNK, lambda part: column >= low - row_first)

    @pl.loop(chunk_first + 1, PRIOR // CHUNK)
    def _(chunk):
        sweep(pl.multiple_of(chunk * CHUNK, CHUNK), CHUNK, None)

    @pl.when(info[6] < PAIR)
    def _():
        in_first = lax.broadcasted_iota(jnp.int32, (PAIR, HEAD_DIM), 0) < info[6]
        for head in range(REPEAT):
            tops[head] = jnp.where(in_first, tops[head], NEGATIVE)
            acc[head] = jnp.where(jnp.concatenate([in_first, in_first], axis=1), acc[head], 0.0)

    def own_visible(part):
        row = lax.broadcasted_iota(jnp.int32, (TILE, PAIR), 0) + part.start
        column = lax.broadcasted_iota(jnp.int32, (TILE, PAIR), 1)
        return (column <= row) & (column >= document_start(info, row))

    sweep(PRIOR, PAIR, own_visible)

    for side in range(CORES):
        where = slice(side * TOK, (side + 1) * TOK)
        squares = jnp.zeros((TOK, HEAD_DIM), F32)
        outs = []
        for head in range(REPEAT):
            summed = acc[head, where, :]
            out = (summed[:, :HEAD_DIM] / summed[:, HEAD_DIM:]).astype(BF16)
            outs.append(out)
            widened = out.astype(F32)
            squares += widened * widened
        whole = jnp.concatenate(outs, axis=1)

        @pl.when(core == side)
        def _():
            mine_ref[...] = whole

        @pl.when(core != side)
        def _():
            send_ref[...] = whole

        sums = row_sums(squares)
        for to in range(TP):
            sums_ref[side * TP + to] = sums


def last_kernel(sums, mine, theirs, out_ref):
    core = place()[2]
    scale = row_scale(sums)
    for ref, side in ((mine, core), (theirs, 1 - core)):
        cols = pl.ds(pl.multiple_of(side * COLS, COLS), COLS)
        out_ref[:, cols] = (ref[...].astype(F32) * scale).astype(BF16)


CTX = ("z", "x", "core")


def move(value, z_shift=0, x_shift=0, core_shift=0):
    pairs = []
    for z in range(Z):
        for x in range(X):
            for core in range(CORES):
                to = ((z + z_shift) % Z * X + (x + x_shift) % X) * CORES
                pairs.append(((z * X + x) * CORES + core, to + (core + core_shift) % CORES))
    return lax.ppermute(value, CTX, pairs)


def swap(value):
    return move(value, core_shift=1)


def exchange(sums):
    return lax.all_to_all(sums, ("core", "tp"), 0, 0, tiled=True)


def shape(dims, kind):
    return jax.ShapeDtypeStruct(dims, kind)


def shards(query_one, key_one, value_one, segments, query_base, key_two, value_two):
    segments_r = swap(segments)
    k1_r, v1_r, k2_r, v2_r = swap(key_one), swap(value_one), swap(key_two), swap(value_two)
    own0, state, query_send, info = call(
        prep_kernel,
        (
            shape((PAIR, 2 * HEAD_DIM), BF16),
            shape((144, HEAD_DIM), BF16),
            shape((2, TOK, COLS), BF16),
            shape((8,), jnp.int32),
        ),
        [ANY, SMEM] + [ANY, VMEM] * 4 + [ANY] * 2,
        (VMEM, VMEM, VMEM, SMEM),
        scratch=(
            pltpu.SMEM((TOK,), jnp.int32),
            pltpu.VMEM((TOK, HEAD_DIM), BF16),
            pltpu.VMEM((TOK, HEAD_DIM), BF16),
            pltpu.SemaphoreType.DMA((7,)),
        ),
        name="prep",
    )(
        segments, segments_r, key_one, k1_r, value_one, v1_r, key_two, k2_r, value_two, v2_r,
        query_one, query_base,
    )
    queries_r = swap(query_send)

    own1 = move(own0, z_shift=1)
    near = [move(state, x_shift=shift) for shift in (1, 2, 3)]
    prefix, plane = call(
        plane_kernel,
        (shape((HEAD_DIM + 8, HEAD_DIM), F32), shape((144, HEAD_DIM), BF16)),
        [SMEM] + [VMEM] * 4,
        (VMEM, VMEM),
        name="plane",
    )(info, state, *near)
    far = [move(plane, z_shift=back) for back in (1, 2, 3, 4)]

    own4 = move(own0, z_shift=4)
    own23 = move(jnp.concatenate([own0, own1], axis=0), z_shift=2)
    x = lax.axis_index("x")
    gathered = [move(own1, x_shift=shift) for shift in (1, 2, 3)]
    gathered += [
        move(jnp.where(x + shift < X, own0, own4), x_shift=shift) for shift in (1, 2, 3)
    ]
    gathered += [move(own23, x_shift=shift) for shift in (1, 2, 3)]

    inside, query = call(
        inside_kernel,
        (shape((PAIR, COLS), F32), shape((PAIR, COLS), BF16)),
        [SMEM] + [ANY, VMEM] * 3,
        (VMEM, VMEM),
        scratch=(
            pltpu.VMEM((PAIR, HEAD_DIM), BF16),
            pltpu.VMEM((PAIR, HEAD_DIM), BF16),
            pltpu.SemaphoreType.DMA((3,)),
        ),
        name="inside",
    )(info, query_one, queries_r, key_one, k1_r, value_one, v1_r)
    first, sums, reach = call(
        first_kernel,
        (
            shape((PAIR, COLS), F32),
            shape((CORES * TP, 8, PAIR), F32),
            shape((1,), jnp.int32),
        ),
        [SMEM] + [VMEM] * 7,
        (VMEM, VMEM, SMEM),
        name="first",
    )(info, prefix, *far, inside, query)

    mine, send, out_sums = call(
        attention_kernel,
        (
            shape((TOK, COLS), BF16),
            shape((TOK, COLS), BF16),
            shape((CORES * TP, 8, TOK), F32),
        ),
        [SMEM, SMEM, VMEM, VMEM, ANY, VMEM] + [ANY] * 13,
        (VMEM,) * 3,
        scratch=(
            pltpu.VMEM((PRIOR + PAIR, 3 * HEAD_DIM), BF16),
            pltpu.VMEM((REPEAT, PAIR, HEAD_DIM), BF16),
            pltpu.VMEM((REPEAT, PAIR, HEAD_DIM), F32),
            pltpu.VMEM((REPEAT, PAIR, 2 * HEAD_DIM), F32),
            pltpu.VMEM((PAIR, HEAD_DIM), F32),
            pltpu.VMEM((TOK, COLS), BF16),
            pltpu.SemaphoreType.DMA((21,)),
        ),
        limit=40 * 2**20,
        name="attention",
    )(info, reach, exchange(sums), first, query_base, queries_r, own0, own1, own23, own4, *gathered)
    theirs = swap(send)
    return call(
        last_kernel, shape((TOK, 2 * COLS), BF16), [VMEM] * 3, VMEM, name="last"
    )(exchange(out_sums), mine, theirs)


def solution(mesh):
    grid = Mesh(mesh.devices.reshape(Z, X, CORES, TP), ("z", "x", "core", "tp"))
    tokens, both = P(CTX), P(CTX, "tp")
    return jax.shard_map(
        shards,
        mesh=grid,
        in_specs=(both,) * 3 + (tokens,) + (both,) * 3,
        out_specs=both,
        check_vma=False,
    )
```

```python
import jax
import jax.numpy as jnp
from jax import lax
from jax.experimental import pallas as pl
from jax.experimental.pallas import tpu as pltpu
from jax.sharding import Mesh, PartitionSpec as P

HEAD_DIM = 128
WIDTH = 4096
EPSILON = 1e-05
NEGATIVE = -1e30

TOK = 192
PAIR = 384
REPEAT = 4
COLS = REPEAT * HEAD_DIM
Z, X, CORES, TP = 8, 4, 2, 4
CHUNK = 2
SCALE = HEAD_DIM ** (-0.5) * 1.4426950408889634

F32 = jnp.float32
BF16 = jnp.bfloat16
VMEM = pl.BlockSpec(memory_space=pltpu.VMEM)
SMEM = pl.BlockSpec(memory_space=pltpu.SMEM)
HBM = pl.BlockSpec(memory_space=pltpu.HBM)


def place():
    return lax.axis_index("z"), lax.axis_index("x"), lax.axis_index("core")


def call(kernel, outs, specs_in, specs_out, scratch=(), aliases=None, limit=16, name=None):
    return pl.pallas_call(
        kernel,
        out_shape=outs,
        in_specs=specs_in,
        out_specs=specs_out,
        scratch_shapes=list(scratch),
        input_output_aliases=aliases or {},
        compiler_params=pltpu.CompilerParams(vmem_limit_bytes=limit * 2**20),
        name=name,
    )


def count_below(ref, doc):
    found = jnp.int32(0)
    for step in (128, 64, 32, 16, 8, 4, 2, 1):
        tried = found + step
        last = ref[jnp.minimum(tried, TOK) - 1]
        found = jnp.where((tried <= TOK) & (last < doc), tried, found)
    return found


def half(core):
    return pl.ds(pl.multiple_of(core * HEAD_DIM, HEAD_DIM), HEAD_DIM)


def rows_of(core):
    return pl.ds(pl.multiple_of(core * TOK, 64), TOK)


def prep_kernel(seg, seg_r, own, other, own0_ref, first_ref, state_ref, info_ref):
    core = place()[2]
    for side, ref in ((core, own), (1 - core, other)):
        first_ref[rows_of(side), :HEAD_DIM] = ref[0]
        first_ref[rows_of(side), HEAD_DIM:] = ref[1]
        own0_ref[rows_of(side), :HEAD_DIM] = ref[2]
        own0_ref[rows_of(side), HEAD_DIM:] = ref[3]
    below = [count_below(seg, d) for d in (1, 2, 3)]
    below_r = [count_below(seg_r, d) for d in (1, 2, 3)]
    bounds = [a + b for a, b in zip(below, below_r)]
    first = jnp.where(core == 0, seg[0], seg_r[0])
    last = jnp.where(core == 0, seg_r[TOK - 1], seg[TOK - 1])

    def pick(values, doc):
        out = jnp.int32(0)
        for d in (1, 2, 3):
            out = jnp.where(doc == d, values[d - 1], out)
        return out

    count = PAIR - pick(bounds, last)
    first_end = jnp.where(first == 3, PAIR, pick(bounds, first + 1))
    for place_in, value in enumerate((*bounds, first, last, count, first_end, 0)):
        info_ref[place_in] = jnp.int32(value)
    rows = lax.broadcasted_iota(jnp.int32, (PAIR, HEAD_DIM), 0)
    masked = jnp.where(rows >= PAIR - count, first_ref[:, :HEAD_DIM].astype(F32), 0.0)
    state = lax.dot_general(
        masked.astype(BF16),
        first_ref[:, HEAD_DIM:],
        (((0,), (0,)), ((), ())),
        preferred_element_type=F32,
    )
    state_ref[:HEAD_DIM] = state.astype(BF16)
    state_ref[HEAD_DIM:] = notes(last.astype(F32), count.astype(F32)).astype(BF16)


def notes(last, count):
    row = lax.broadcasted_iota(jnp.int32, (16, HEAD_DIM), 0)
    high = jnp.floor(count * (1.0 / 64.0))
    return jnp.where(
        row == 0, last, jnp.where(row == 1, high, jnp.where(row == 2, count - 64.0 * high, 0.0))
    )


def read_state(ref):
    tail = ref[HEAD_DIM:].astype(F32)
    return ref[:HEAD_DIM].astype(F32), tail[0:1], tail[1:2] * 64.0 + tail[2:3]


def plane_kernel(
    info, own, from1, from2, from3, own0, own1, queries_r, prefix_ref, plane_ref, own01_ref
):
    x = place()[1]
    own01_ref[:PAIR] = own0[...]
    own01_ref[PAIR:] = own1[...]
    first = info[3].astype(F32)
    items = [read_state(ref) for ref in (own, from1, from2, from3)]
    prefix = jnp.zeros((HEAD_DIM, HEAD_DIM), F32)
    prefix_count = jnp.zeros((1, HEAD_DIM), F32)
    for shift in (1, 2, 3):
        state, doc, count = items[shift]
        chosen = jnp.where((doc == first) & (x >= shift), 1.0, 0.0)
        prefix += state * chosen
        prefix_count += count * chosen
    prefix_ref[:HEAD_DIM] = prefix
    prefix_ref[HEAD_DIM:] = jnp.broadcast_to(prefix_count, (8, HEAD_DIM))
    last = items[0][1]
    for item in items[1:]:
        last = jnp.maximum(last, item[1])
    total = jnp.zeros((HEAD_DIM, HEAD_DIM), F32)
    total_count = jnp.zeros((1, HEAD_DIM), F32)
    for state, doc, count in items:
        chosen = jnp.where(doc == last, 1.0, 0.0)
        total += state * chosen
        total_count += count * chosen
    plane_ref[:HEAD_DIM] = total.astype(BF16)
    plane_ref[HEAD_DIM:] = notes(last, total_count).astype(BF16)


def document_start(info, rows):
    start = jnp.zeros_like(rows)
    for d in range(3):
        start = jnp.where(rows >= info[d], jnp.maximum(start, info[d]), start)
    return start


def split_dot(wide, narrow):
    high = wide.astype(BF16)
    low = (wide - high.astype(F32)).astype(BF16)
    return jnp.dot(high, narrow, preferred_element_type=F32) + jnp.dot(
        low, narrow, preferred_element_type=F32
    )


def inside_kernel(info, keep, queries_r, packed, inside_ref, query_ref):
    core = place()[2]
    query_ref[rows_of(core), :] = keep[0]
    query_ref[rows_of(1 - core), :] = queries_r[0]
    row = lax.broadcasted_iota(jnp.int32, (PAIR, PAIR), 0)
    column = lax.broadcasted_iota(jnp.int32, (PAIR, PAIR), 1)
    visible = (column <= row) & (column >= document_start(info, row))
    for head in range(REPEAT):
        cols = slice(head * HEAD_DIM, (head + 1) * HEAD_DIM)
        scores = lax.dot_general(
            query_ref[:, cols],
            packed[:, :HEAD_DIM],
            (((1,), (1,)), ((), ())),
            preferred_element_type=F32,
        )
        scores = jnp.where(visible, scores, 0.0)
        inside_ref[:, cols] = split_dot(scores, packed[:, HEAD_DIM:])


def row_sums(squares):
    high = squares.astype(BF16)
    low = (squares - high.astype(F32)).astype(BF16)
    ones = jnp.ones((8, squares.shape[1]), BF16)
    dims = (((1,), (1,)), ((), ()))
    return lax.dot_general(ones, high, dims, preferred_element_type=F32) + lax.dot_general(
        ones, low, dims, preferred_element_type=F32
    )


def first_kernel(
    info, prefix, from1, from2, from3, from4, inside, query, first_ref, sums_ref, count_ref
):
    z = place()[0]
    first = info[3].astype(F32)
    state = prefix[:HEAD_DIM]
    count = prefix[HEAD_DIM : HEAD_DIM + 1]
    for back, ref in enumerate((from1, from2, from3, from4), 1):
        one_state, doc, one_count = read_state(ref)
        chosen = jnp.where((doc == first) & (z >= back), 1.0, 0.0)
        state += one_state * chosen
        count += one_count * chosen
    count_ref[0] = jnp.max(count).astype(jnp.int32)
    high = state.astype(BF16)
    low = (state - high.astype(F32)).astype(BF16)
    in_first = lax.broadcasted_iota(jnp.int32, (PAIR, HEAD_DIM), 0) < info[6]
    squares = jnp.zeros((PAIR, HEAD_DIM), F32)
    for head in range(REPEAT):
        cols = slice(head * HEAD_DIM, (head + 1) * HEAD_DIM)
        queries = query[:, cols]
        earlier = jnp.dot(queries, high, preferred_element_type=F32) + jnp.dot(
            queries, low, preferred_element_type=F32
        )
        out = inside[:, cols] + jnp.where(in_first, earlier, 0.0)
        first_ref[:, cols] = out
        squares += out * out
    sums = row_sums(squares)
    for to in range(CORES * TP):
        sums_ref[to] = sums


def row_scale(sums):
    total = sums[0]
    for device in range(1, CORES * TP):
        total = total + sums[device]
    return lax.transpose(lax.rsqrt(total * (1.0 / WIDTH) + EPSILON), (1, 0))[:, :1]


TILE = 128
TILES = [(head, slice(at, at + TILE)) for head in range(REPEAT) for at in range(0, PAIR, TILE)]


def scores_of(queries, keys, head, part, rows):
    return lax.dot_general(
        queries[head, part],
        keys[rows, :HEAD_DIM],
        (((1,), (1,)), ((), ())),
        preferred_element_type=F32,
    )


def sweep(queries, kv, tops, acc, rows, visible=None, begin=False):
    ahead = scores_of(queries, kv, *TILES[0], rows)
    for at, (head, part) in enumerate(TILES):
        scores = ahead
        if at + 1 < len(TILES):
            ahead = scores_of(queries, kv, *TILES[at + 1], rows)
        if visible is not None:
            scores = jnp.where(visible(part), scores, NEGATIVE)
        top = jnp.max(scores, axis=1, keepdims=True)
        if begin:
            top = jnp.broadcast_to(top, (TILE, HEAD_DIM))
        else:
            old_top = tops[head, part]
            top = jnp.maximum(old_top, top)
        wide_top = jnp.concatenate([top] * (scores.shape[1] // HEAD_DIM), axis=1)
        weights = jnp.exp2((scores - wide_top) * SCALE)
        summed = jnp.dot(weights.astype(BF16), kv[rows, HEAD_DIM:], preferred_element_type=F32)
        tops[head, part] = top
        if begin:
            acc[head, part] = summed
        else:
            shrink = jnp.exp2((old_top - top) * SCALE)
            acc[head, part] = acc[head, part] * jnp.concatenate([shrink, shrink], axis=1) + summed


class Window:
    def __init__(self, info, prior, blocks, kv, bounds, sems):
        self.info, self.kv, self.bounds = info, kv, bounds
        used = jnp.int32(0)
        self.copies = []
        for at, (ref, distance) in enumerate(blocks):
            distance = jnp.int32(distance)
            needed = (distance >= 1) & (distance <= 16) & (prior > (distance - 1) * PAIR)
            slot = jnp.minimum(used, bounds.shape[0] - 1)
            rows = pl.ds(pl.multiple_of(slot * PAIR, PAIR), PAIR)
            copy = pltpu.make_async_copy(ref, kv.at[rows, pl.ds(0, 2 * HEAD_DIM)], sems.at[at])
            self.copies.append((needed, copy))

            @pl.when(needed)
            def _():
                copy.start()
                bounds[slot] = jnp.maximum(distance * PAIR - prior, 0)

            used = used + needed.astype(jnp.int32)
        self.steps = (used + CHUNK - 1) // CHUNK
        kv[:, 2 * HEAD_DIM :] = jnp.ones((kv.shape[0], HEAD_DIM), BF16)

        @pl.when(used % CHUNK != 0)
        def _():
            rows = pl.ds(pl.multiple_of(used * PAIR, PAIR), PAIR)
            kv[rows, : 2 * HEAD_DIM] = jnp.zeros((PAIR, 2 * HEAD_DIM), BF16)
            bounds[used] = jnp.int32(PAIR)

    def absorb(self, queries, tops, acc):
        for needed, copy in self.copies:
            pl.when(needed)(copy.wait)

        @pl.loop(0, self.steps)
        def _(step):
            rows = pl.ds(pl.multiple_of(step * CHUNK * PAIR, CHUNK * PAIR), CHUNK * PAIR)
            low0, low1 = self.bounds[step * CHUNK], self.bounds[step * CHUNK + 1]
            first_end = self.info[6]
            whole = (low0 == 0) & (low1 == 0) & (first_end == PAIR)

            @pl.when(whole)
            def _():
                sweep(queries, self.kv, tops, acc, rows)

            @pl.when(jnp.logical_not(whole))
            def _():
                def visible(part):
                    row = lax.broadcasted_iota(jnp.int32, (TILE, CHUNK * PAIR), 0) + part.start
                    column = lax.broadcasted_iota(jnp.int32, (TILE, CHUNK * PAIR), 1)
                    low = jnp.where(column < PAIR, low0, PAIR + low1)
                    return (column >= low) & (row < first_end)

                sweep(queries, self.kv, tops, acc, rows, visible)


SLOTS = 10


def near_kernel(
    info, reach, sums, first, keep, queries_r, own0, near_hbm, own23,
    queries, tops, acc, kv, own, scales, bounds, sems
):
    _, x, core = place()
    blocks = []
    for other in range(X):
        at = 2 * PAIR * other
        blocks.append((near_hbm.at[pl.ds(at + PAIR, PAIR)], 4 + x - other))
        if other < X - 1:
            blocks.append((near_hbm.at[pl.ds(at, PAIR)], x - other))
    blocks += [(own23.at[pl.ds(0, PAIR)], 8), (own23.at[pl.ds(PAIR, PAIR)], 12)]
    window = Window(info, reach[0], blocks, kv, bounds, sems)
    own[:, : 2 * HEAD_DIM] = own0[...]
    own[:, 2 * HEAD_DIM :] = jnp.ones((PAIR, HEAD_DIM), BF16)
    scales[...] = jnp.broadcast_to(row_scale(sums), (PAIR, HEAD_DIM))
    for part, where in ((keep.at[1], rows_of(core)), (queries_r.at[1], rows_of(1 - core))):
        for head in range(REPEAT):
            cols = slice(head * HEAD_DIM, (head + 1) * HEAD_DIM)
            value = part[:, cols].astype(F32) + first[where, cols] * scales[where, :]
            queries[head, where, :] = value.astype(BF16)

    def own_visible(part):
        row = lax.broadcasted_iota(jnp.int32, (TILE, PAIR), 0) + part.start
        column = lax.broadcasted_iota(jnp.int32, (TILE, PAIR), 1)
        return (column <= row) & (column >= document_start(info, row))

    sweep(queries, own, tops, acc, slice(0, PAIR), own_visible, begin=True)
    window.absorb(queries, tops, acc)


def far_kernel(
    info, reach, queries, old_tops, old_acc, own4, last1, last2, last3, far1, far2, far3,
    mine_ref, send_ref, sums_ref, tops, acc, kv, bounds, sems
):
    _, x, core = place()
    blocks = [(own4, 16)]
    for shift, last, far in zip((1, 2, 3), (last1, last2, last3), (far1, far2, far3)):
        wrapped = jnp.where(x < shift, 4, 0)
        blocks.append((far.at[pl.ds(0, PAIR)], 8 + shift - wrapped))
        blocks.append((far.at[pl.ds(PAIR, PAIR)], 12 + shift - wrapped))
        blocks.append((last, jnp.where(x < shift, 12 + shift, 0)))
    window = Window(info, reach[0], blocks, kv, bounds, sems)
    window.absorb(queries, tops, acc)
    for side in range(CORES):
        where = slice(side * TOK, (side + 1) * TOK)
        squares = jnp.zeros((TOK, HEAD_DIM), F32)
        outs = []
        for head in range(REPEAT):
            summed = acc[head, where, :]
            out = (summed[:, :HEAD_DIM] / summed[:, HEAD_DIM:]).astype(BF16)
            outs.append(out)
            widened = out.astype(F32)
            squares += widened * widened
        whole = jnp.concatenate(outs, axis=1)

        @pl.when(core == side)
        def _():
            mine_ref[...] = whole

        @pl.when(core != side)
        def _():
            send_ref[...] = whole

        sums = row_sums(squares)
        for to in range(TP):
            sums_ref[side * TP + to] = sums


def last_kernel(sums, mine, theirs, out_ref):
    core = place()[2]
    scale = row_scale(sums)
    for ref, side in ((mine, core), (theirs, 1 - core)):
        cols = pl.ds(pl.multiple_of(side * COLS, COLS), COLS)
        out_ref[:, cols] = (ref[...].astype(F32) * scale).astype(BF16)


CTX = ("z", "x", "core")


def move(value, z_shift=0, x_shift=0, core_shift=0, keep=lambda x: True):
    pairs = []
    for z in range(Z):
        for x in range(X):
            for core in range(CORES):
                to = ((z + z_shift) % Z * X + (x + x_shift) % X) * CORES
                if keep(x):
                    pairs.append(((z * X + x) * CORES + core, to + (core + core_shift) % CORES))
    return lax.ppermute(value, CTX, pairs)


def swap(value):
    return move(value, core_shift=1)


def exchange(sums):
    return lax.all_to_all(sums, ("core", "tp"), 0, 0, tiled=True)


def shape(dims, kind):
    return jax.ShapeDtypeStruct(dims, kind)


def shards(query_one, key_one, value_one, segments, query_base, key_two, value_two):
    core = lax.axis_index("core")

    def halves(arrays):
        low = jnp.stack([array[:, : array.shape[1] // 2] for array in arrays])
        high = jnp.stack([array[:, array.shape[1] // 2 :] for array in arrays])
        return jnp.where(core == 0, low, high), jnp.where(core == 0, high, low)

    segments_r = swap(segments)
    own_keep, own_send = halves((key_one, value_one, key_two, value_two))
    own0, packed, state, info = call(
        prep_kernel,
        (
            shape((PAIR, 2 * HEAD_DIM), BF16),
            shape((PAIR, 2 * HEAD_DIM), BF16),
            shape((144, HEAD_DIM), BF16),
            shape((8,), jnp.int32),
        ),
        [SMEM, SMEM, VMEM, VMEM],
        (VMEM,) * 3 + (SMEM,),
        name="prep",
    )(segments, segments_r, own_keep, swap(own_send))
    keep, query_send = halves((query_one, query_base))
    queries_r = swap(query_send)

    own1 = move(own0, z_shift=1)
    near = [move(state, x_shift=shift) for shift in (1, 2, 3)]
    prefix, plane, own01 = call(
        plane_kernel,
        (
            shape((HEAD_DIM + 8, HEAD_DIM), F32),
            shape((144, HEAD_DIM), BF16),
            shape((2 * PAIR, 2 * HEAD_DIM), BF16),
        ),
        [SMEM] + [VMEM] * 7,
        (VMEM,) * 3,
        name="plane",
    )(info, state, *near, own0, own1, queries_r)
    far = [move(plane, z_shift=back) for back in (1, 2, 3, 4)]
    own23 = move(own01, z_shift=2)
    near_packs = lax.all_gather(own01, "x", axis=0, tiled=True)

    inside, query = call(
        inside_kernel,
        (shape((PAIR, COLS), F32), shape((PAIR, COLS), BF16)),
        [SMEM] + [VMEM] * 3,
        (VMEM,) * 2,
        name="inside",
    )(info, keep, queries_r, packed)
    first, sums, reach = call(
        first_kernel,
        (
            shape((PAIR, COLS), F32),
            shape((CORES * TP, 8, PAIR), F32),
            shape((1,), jnp.int32),
        ),
        [SMEM] + [VMEM] * 7,
        (VMEM, VMEM, SMEM),
        name="first",
    )(info, prefix, *far, inside, query)


    def once_known(value):
        return jnp.where(reach[0] >= 0, value, jnp.zeros_like(value))

    own4 = move(once_known(own0), z_shift=4)
    later23 = once_known(own23)
    far23 = [move(later23, x_shift=shift) for shift in (1, 2, 3)]
    far4 = [move(own4, x_shift=shift, keep=lambda x: x + shift >= X) for shift in (1, 2, 3)]
    queries, tops, acc = call(
        near_kernel,
        (
            shape((REPEAT, PAIR, HEAD_DIM), BF16),
            shape((REPEAT, PAIR, HEAD_DIM), F32),
            shape((REPEAT, PAIR, 2 * HEAD_DIM), F32),
        ),
        [SMEM, SMEM] + [VMEM] * 5 + [HBM, VMEM],
        (VMEM,) * 3,
        scratch=(
            pltpu.VMEM((SLOTS * PAIR, 3 * HEAD_DIM), BF16),
            pltpu.VMEM((PAIR, 3 * HEAD_DIM), BF16),
            pltpu.VMEM((PAIR, HEAD_DIM), F32),
            pltpu.SMEM((SLOTS,), jnp.int32),
            pltpu.SemaphoreType.DMA((9,)),
        ),
        name="near",
    )(info, reach, exchange(sums), first, keep, queries_r, own0, near_packs, own23)
    mine, send, out_sums, _, _ = call(
        far_kernel,
        (
            shape((TOK, COLS), BF16),
            shape((TOK, COLS), BF16),
            shape((CORES * TP, 8, TOK), F32),
            shape((REPEAT, PAIR, HEAD_DIM), F32),
            shape((REPEAT, PAIR, 2 * HEAD_DIM), F32),
        ),
        [SMEM, SMEM] + [VMEM] * 10,
        (VMEM,) * 5,
        scratch=(
            pltpu.VMEM((SLOTS * PAIR, 3 * HEAD_DIM), BF16),
            pltpu.SMEM((SLOTS,), jnp.int32),
            pltpu.SemaphoreType.DMA((10,)),
        ),
        aliases={3: 3, 4: 4},
        name="far",
    )(info, reach, queries, tops, acc, own4, *far4, *far23)
    theirs = swap(send)
    return call(
        last_kernel, shape((TOK, 2 * COLS), BF16), [VMEM] * 3, VMEM, name="last"
    )(exchange(out_sums), mine, theirs)


def solution(mesh):
    grid = Mesh(mesh.devices.reshape(Z, X, CORES, TP), ("z", "x", "core", "tp"))
    tokens, both = P(CTX), P(CTX, "tp")
    return jax.shard_map(
        shards,
        mesh=grid,
        in_specs=(both,) * 3 + (tokens,) + (both,) * 3,
        out_specs=both,
        check_vma=False,
    )
```

```python
import jax
import jax.numpy as jnp
from jax import lax
from jax.experimental import pallas as pl
from jax.experimental.pallas import tpu as pltpu
from jax.sharding import Mesh, PartitionSpec as P

HEAD_DIM = 128
WIDTH = 4096
EPSILON = 1e-05
NEGATIVE = -1e30

TOK = 192
PAIR = 384
REPEAT = 4
COLS = REPEAT * HEAD_DIM
Z, X, CORES, TP = 8, 4, 2, 4
CHUNK = 2
SCALE = HEAD_DIM ** (-0.5) * 1.4426950408889634

F32 = jnp.float32
BF16 = jnp.bfloat16
VMEM = pl.BlockSpec(memory_space=pltpu.VMEM)
SMEM = pl.BlockSpec(memory_space=pltpu.SMEM)
HBM = pl.BlockSpec(memory_space=pltpu.HBM)


def place():
    return lax.axis_index("z"), lax.axis_index("x"), lax.axis_index("core")


def call(kernel, outs, specs_in, specs_out, scratch=(), aliases=None, limit=16, name=None):
    return pl.pallas_call(
        kernel,
        out_shape=outs,
        in_specs=specs_in,
        out_specs=specs_out,
        scratch_shapes=list(scratch),
        input_output_aliases=aliases or {},
        compiler_params=pltpu.CompilerParams(vmem_limit_bytes=limit * 2**20),
        name=name,
    )


def count_below(ref, doc):
    found = jnp.int32(0)
    for step in (128, 64, 32, 16, 8, 4, 2, 1):
        tried = found + step
        last = ref[jnp.minimum(tried, TOK) - 1]
        found = jnp.where((tried <= TOK) & (last < doc), tried, found)
    return found


def half(core):
    return pl.ds(pl.multiple_of(core * HEAD_DIM, HEAD_DIM), HEAD_DIM)


def rows_of(core):
    return pl.ds(pl.multiple_of(core * TOK, 64), TOK)


def prep_kernel(seg, seg_r, own, other, own0_ref, first_ref, state_ref, info_ref):
    core = place()[2]
    for side, ref in ((core, own), (1 - core, other)):
        first_ref[rows_of(side), :HEAD_DIM] = ref[0]
        first_ref[rows_of(side), HEAD_DIM:] = ref[1]
        own0_ref[rows_of(side), :HEAD_DIM] = ref[2]
        own0_ref[rows_of(side), HEAD_DIM:] = ref[3]
    below = [count_below(seg, d) for d in (1, 2, 3)]
    below_r = [count_below(seg_r, d) for d in (1, 2, 3)]
    bounds = [a + b for a, b in zip(below, below_r)]
    first = jnp.where(core == 0, seg[0], seg_r[0])
    last = jnp.where(core == 0, seg_r[TOK - 1], seg[TOK - 1])

    def pick(values, doc):
        out = jnp.int32(0)
        for d in (1, 2, 3):
            out = jnp.where(doc == d, values[d - 1], out)
        return out

    count = PAIR - pick(bounds, last)
    first_end = jnp.where(first == 3, PAIR, pick(bounds, first + 1))
    for place_in, value in enumerate((*bounds, first, last, count, first_end, 0)):
        info_ref[place_in] = jnp.int32(value)
    rows = lax.broadcasted_iota(jnp.int32, (PAIR, HEAD_DIM), 0)
    masked = jnp.where(rows >= PAIR - count, first_ref[:, :HEAD_DIM].astype(F32), 0.0)
    state = lax.dot_general(
        masked.astype(BF16),
        first_ref[:, HEAD_DIM:],
        (((0,), (0,)), ((), ())),
        preferred_element_type=F32,
    )
    state_ref[:HEAD_DIM] = state.astype(BF16)
    state_ref[HEAD_DIM:] = notes(last.astype(F32), count.astype(F32)).astype(BF16)


def notes(last, count):
    row = lax.broadcasted_iota(jnp.int32, (16, HEAD_DIM), 0)
    high = jnp.floor(count * (1.0 / 64.0))
    return jnp.where(
        row == 0, last, jnp.where(row == 1, high, jnp.where(row == 2, count - 64.0 * high, 0.0))
    )


def read_state(ref):
    tail = ref[HEAD_DIM:].astype(F32)
    return ref[:HEAD_DIM].astype(F32), tail[0:1], tail[1:2] * 64.0 + tail[2:3]


def plane_kernel(
    info, own, from1, from2, from3, own0, own1, queries_r, prefix_ref, plane_ref, own01_ref
):
    x = place()[1]
    own01_ref[:PAIR] = own0[...]
    own01_ref[PAIR:] = own1[...]
    first = info[3].astype(F32)
    items = [read_state(ref) for ref in (own, from1, from2, from3)]
    prefix = jnp.zeros((HEAD_DIM, HEAD_DIM), F32)
    prefix_count = jnp.zeros((1, HEAD_DIM), F32)
    for shift in (1, 2, 3):
        state, doc, count = items[shift]
        chosen = jnp.where((doc == first) & (x >= shift), 1.0, 0.0)
        prefix += state * chosen
        prefix_count += count * chosen
    prefix_ref[:HEAD_DIM] = prefix
    prefix_ref[HEAD_DIM:] = jnp.broadcast_to(prefix_count, (8, HEAD_DIM))
    last = items[0][1]
    for item in items[1:]:
        last = jnp.maximum(last, item[1])
    total = jnp.zeros((HEAD_DIM, HEAD_DIM), F32)
    total_count = jnp.zeros((1, HEAD_DIM), F32)
    for state, doc, count in items:
        chosen = jnp.where(doc == last, 1.0, 0.0)
        total += state * chosen
        total_count += count * chosen
    plane_ref[:HEAD_DIM] = total.astype(BF16)
    plane_ref[HEAD_DIM:] = notes(last, total_count).astype(BF16)


def document_start(info, rows):
    start = jnp.zeros_like(rows)
    for d in range(3):
        start = jnp.where(rows >= info[d], jnp.maximum(start, info[d]), start)
    return start


def split_dot(wide, narrow):
    high = wide.astype(BF16)
    low = (wide - high.astype(F32)).astype(BF16)
    return jnp.dot(high, narrow, preferred_element_type=F32) + jnp.dot(
        low, narrow, preferred_element_type=F32
    )


def inside_kernel(info, keep, queries_r, packed, inside_ref, query_ref):
    core = place()[2]
    query_ref[rows_of(core), :] = keep[0]
    query_ref[rows_of(1 - core), :] = queries_r[0]
    row = lax.broadcasted_iota(jnp.int32, (PAIR, PAIR), 0)
    column = lax.broadcasted_iota(jnp.int32, (PAIR, PAIR), 1)
    visible = (column <= row) & (column >= document_start(info, row))
    for head in range(REPEAT):
        cols = slice(head * HEAD_DIM, (head + 1) * HEAD_DIM)
        scores = lax.dot_general(
            query_ref[:, cols],
            packed[:, :HEAD_DIM],
            (((1,), (1,)), ((), ())),
            preferred_element_type=F32,
        )
        scores = jnp.where(visible, scores, 0.0)
        inside_ref[:, cols] = split_dot(scores, packed[:, HEAD_DIM:])


def row_sums(squares):
    high = squares.astype(BF16)
    low = (squares - high.astype(F32)).astype(BF16)
    ones = jnp.ones((8, squares.shape[1]), BF16)
    dims = (((1,), (1,)), ((), ()))
    return lax.dot_general(ones, high, dims, preferred_element_type=F32) + lax.dot_general(
        ones, low, dims, preferred_element_type=F32
    )


def first_kernel(
    info, prefix, from1, from2, from3, from4, inside, query, first_ref, sums_ref, count_ref
):
    z = place()[0]
    first = info[3].astype(F32)
    state = prefix[:HEAD_DIM]
    count = prefix[HEAD_DIM : HEAD_DIM + 1]
    for back, ref in enumerate((from1, from2, from3, from4), 1):
        one_state, doc, one_count = read_state(ref)
        chosen = jnp.where((doc == first) & (z >= back), 1.0, 0.0)
        state += one_state * chosen
        count += one_count * chosen
    count_ref[0] = jnp.max(count).astype(jnp.int32)
    high = state.astype(BF16)
    low = (state - high.astype(F32)).astype(BF16)
    in_first = lax.broadcasted_iota(jnp.int32, (PAIR, HEAD_DIM), 0) < info[6]
    squares = jnp.zeros((PAIR, HEAD_DIM), F32)
    for head in range(REPEAT):
        cols = slice(head * HEAD_DIM, (head + 1) * HEAD_DIM)
        queries = query[:, cols]
        earlier = jnp.dot(queries, high, preferred_element_type=F32) + jnp.dot(
            queries, low, preferred_element_type=F32
        )
        out = inside[:, cols] + jnp.where(in_first, earlier, 0.0)
        first_ref[:, cols] = out
        squares += out * out
    sums = row_sums(squares)
    for to in range(CORES * TP):
        sums_ref[to] = sums


def row_scale(sums):
    total = sums[0]
    for device in range(1, CORES * TP):
        total = total + sums[device]
    return lax.transpose(lax.rsqrt(total * (1.0 / WIDTH) + EPSILON), (1, 0))[:, :1]


TILE = 128
TILES = [(head, slice(at, at + TILE)) for head in range(REPEAT) for at in range(0, PAIR, TILE)]


def scores_of(queries, keys, head, part, rows):
    return lax.dot_general(
        queries[head, part],
        keys[rows, :HEAD_DIM],
        (((1,), (1,)), ((), ())),
        preferred_element_type=F32,
    )


def sweep(queries, kv, tops, acc, rows, visible=None, begin=False):
    ahead = scores_of(queries, kv, *TILES[0], rows)
    for at, (head, part) in enumerate(TILES):
        scores = ahead
        if at + 1 < len(TILES):
            ahead = scores_of(queries, kv, *TILES[at + 1], rows)
        if visible is not None:
            scores = jnp.where(visible(part), scores, NEGATIVE)
        top = jnp.max(scores, axis=1, keepdims=True)
        if begin:
            top = jnp.broadcast_to(top, (TILE, HEAD_DIM))
        else:
            old_top = tops[head, part]
            top = jnp.maximum(old_top, top)
        wide_top = jnp.concatenate([top] * (scores.shape[1] // HEAD_DIM), axis=1)
        weights = jnp.exp2((scores - wide_top) * SCALE)
        summed = jnp.dot(weights.astype(BF16), kv[rows, HEAD_DIM:], preferred_element_type=F32)
        tops[head, part] = top
        if begin:
            acc[head, part] = summed
        else:
            shrink = jnp.exp2((old_top - top) * SCALE)
            acc[head, part] = acc[head, part] * jnp.concatenate([shrink, shrink], axis=1) + summed


class Window:
    def __init__(self, info, prior, blocks, kv, bounds, sems):
        self.info, self.kv, self.bounds = info, kv, bounds
        used = jnp.int32(0)
        self.copies = []
        for at, (ref, distance) in enumerate(blocks):
            distance = jnp.int32(distance)
            needed = (distance >= 1) & (distance <= 16) & (prior > (distance - 1) * PAIR)
            slot = jnp.minimum(used, bounds.shape[0] - 1)
            rows = pl.ds(pl.multiple_of(slot * PAIR, PAIR), PAIR)
            copy = pltpu.make_async_copy(ref, kv.at[rows, pl.ds(0, 2 * HEAD_DIM)], sems.at[at])
            self.copies.append((needed, copy))

            @pl.when(needed)
            def _():
                copy.start()
                bounds[slot] = jnp.maximum(distance * PAIR - prior, 0)

            used = used + needed.astype(jnp.int32)
        self.steps = (used + CHUNK - 1) // CHUNK
        kv[:, 2 * HEAD_DIM :] = jnp.ones((kv.shape[0], HEAD_DIM), BF16)

        @pl.when(used % CHUNK != 0)
        def _():
            rows = pl.ds(pl.multiple_of(used * PAIR, PAIR), PAIR)
            kv[rows, : 2 * HEAD_DIM] = jnp.zeros((PAIR, 2 * HEAD_DIM), BF16)
            bounds[used] = jnp.int32(PAIR)

    def absorb(self, queries, tops, acc):
        for needed, copy in self.copies:
            pl.when(needed)(copy.wait)

        @pl.loop(0, self.steps)
        def _(step):
            rows = pl.ds(pl.multiple_of(step * CHUNK * PAIR, CHUNK * PAIR), CHUNK * PAIR)
            low0, low1 = self.bounds[step * CHUNK], self.bounds[step * CHUNK + 1]
            first_end = self.info[6]
            whole = (low0 == 0) & (low1 == 0) & (first_end == PAIR)

            @pl.when(whole)
            def _():
                sweep(queries, self.kv, tops, acc, rows)

            @pl.when(jnp.logical_not(whole))
            def _():
                def visible(part):
                    row = lax.broadcasted_iota(jnp.int32, (TILE, CHUNK * PAIR), 0) + part.start
                    column = lax.broadcasted_iota(jnp.int32, (TILE, CHUNK * PAIR), 1)
                    low = jnp.where(column < PAIR, low0, PAIR + low1)
                    return (column >= low) & (row < first_end)

                sweep(queries, self.kv, tops, acc, rows, visible)


SLOTS = 10


def near_kernel(
    info, reach, sums, first, keep, queries_r, own0, near_hbm, own23,
    queries, tops, acc, kv, own, scales, bounds, sems
):
    _, x, core = place()
    blocks = []
    for other in range(X):
        at = 2 * PAIR * other
        blocks.append((near_hbm.at[pl.ds(at + PAIR, PAIR)], 4 + x - other))
        if other < X - 1:
            blocks.append((near_hbm.at[pl.ds(at, PAIR)], x - other))
    blocks += [(own23.at[pl.ds(0, PAIR)], 8), (own23.at[pl.ds(PAIR, PAIR)], 12)]
    window = Window(info, reach[0], blocks, kv, bounds, sems)
    own[:, : 2 * HEAD_DIM] = own0[...]
    own[:, 2 * HEAD_DIM :] = jnp.ones((PAIR, HEAD_DIM), BF16)
    scales[...] = jnp.broadcast_to(row_scale(sums), (PAIR, HEAD_DIM))
    for part, where in ((keep.at[1], rows_of(core)), (queries_r.at[1], rows_of(1 - core))):
        for head in range(REPEAT):
            cols = slice(head * HEAD_DIM, (head + 1) * HEAD_DIM)
            value = part[:, cols].astype(F32) + first[where, cols] * scales[where, :]
            queries[head, where, :] = value.astype(BF16)

    def own_visible(part):
        row = lax.broadcasted_iota(jnp.int32, (TILE, PAIR), 0) + part.start
        column = lax.broadcasted_iota(jnp.int32, (TILE, PAIR), 1)
        return (column <= row) & (column >= document_start(info, row))

    sweep(queries, own, tops, acc, slice(0, PAIR), own_visible, begin=True)
    window.absorb(queries, tops, acc)


def far_kernel(
    info, reach, queries, old_tops, old_acc, own4, last1, last2, last3, far1, far2, far3,
    mine_ref, send_ref, sums_ref, tops, acc, kv, bounds, sems
):
    _, x, core = place()
    blocks = [(own4, 16)]
    for shift, last, far in zip((1, 2, 3), (last1, last2, last3), (far1, far2, far3)):
        wrapped = jnp.where(x < shift, 4, 0)
        blocks.append((far.at[pl.ds(0, PAIR)], 8 + shift - wrapped))
        blocks.append((far.at[pl.ds(PAIR, PAIR)], 12 + shift - wrapped))
        blocks.append((last, jnp.where(x < shift, 12 + shift, 0)))
    window = Window(info, reach[0], blocks, kv, bounds, sems)
    window.absorb(queries, tops, acc)
    for side in range(CORES):
        where = slice(side * TOK, (side + 1) * TOK)
        squares = jnp.zeros((TOK, HEAD_DIM), F32)
        outs = []
        for head in range(REPEAT):
            summed = acc[head, where, :]
            out = (summed[:, :HEAD_DIM] / summed[:, HEAD_DIM:]).astype(BF16)
            outs.append(out)
            widened = out.astype(F32)
            squares += widened * widened
        whole = jnp.concatenate(outs, axis=1)

        @pl.when(core == side)
        def _():
            mine_ref[...] = whole

        @pl.when(core != side)
        def _():
            send_ref[...] = whole

        sums = row_sums(squares)
        for to in range(TP):
            sums_ref[side * TP + to] = sums


def last_kernel(sums, mine, theirs, out_ref):
    core = place()[2]
    scale = row_scale(sums)
    for ref, side in ((mine, core), (theirs, 1 - core)):
        cols = pl.ds(pl.multiple_of(side * COLS, COLS), COLS)
        out_ref[:, cols] = (ref[...].astype(F32) * scale).astype(BF16)


CTX = ("z", "x", "core")


def move(value, z_shift=0, x_shift=0, core_shift=0, keep=lambda x: True):
    pairs = []
    for z in range(Z):
        for x in range(X):
            for core in range(CORES):
                to = ((z + z_shift) % Z * X + (x + x_shift) % X) * CORES
                if keep(x):
                    pairs.append(((z * X + x) * CORES + core, to + (core + core_shift) % CORES))
    return lax.ppermute(value, CTX, pairs)


def swap(value):
    return move(value, core_shift=1)


def exchange(sums):
    return lax.all_to_all(sums, ("core", "tp"), 0, 0, tiled=True)


def shape(dims, kind):
    return jax.ShapeDtypeStruct(dims, kind)


def shards(query_one, key_one, value_one, segments, query_base, key_two, value_two):
    core = lax.axis_index("core")

    def halves(arrays):
        low = jnp.stack([array[:, : array.shape[1] // 2] for array in arrays])
        high = jnp.stack([array[:, array.shape[1] // 2 :] for array in arrays])
        return jnp.where(core == 0, low, high), jnp.where(core == 0, high, low)

    segments_r = swap(segments)
    own_keep, own_send = halves((key_one, value_one, key_two, value_two))
    own0, packed, state, info = call(
        prep_kernel,
        (
            shape((PAIR, 2 * HEAD_DIM), BF16),
            shape((PAIR, 2 * HEAD_DIM), BF16),
            shape((144, HEAD_DIM), BF16),
            shape((8,), jnp.int32),
        ),
        [SMEM, SMEM, VMEM, VMEM],
        (VMEM,) * 3 + (SMEM,),
        name="prep",
    )(segments, segments_r, own_keep, swap(own_send))
    keep, query_send = halves((query_one, query_base))
    queries_r = swap(query_send)

    own1 = move(own0, z_shift=1)
    near = [move(state, x_shift=shift) for shift in (1, 2, 3)]
    prefix, plane, own01 = call(
        plane_kernel,
        (
            shape((HEAD_DIM + 8, HEAD_DIM), F32),
            shape((144, HEAD_DIM), BF16),
            shape((2 * PAIR, 2 * HEAD_DIM), BF16),
        ),
        [SMEM] + [VMEM] * 7,
        (VMEM,) * 3,
        name="plane",
    )(info, state, *near, own0, own1, queries_r)
    far = [move(plane, z_shift=back) for back in (1, 2, 3, 4)]
    own23 = move(own01, z_shift=2)
    near_packs = lax.all_gather(own01, "x", axis=0, tiled=True)

    inside, query = call(
        inside_kernel,
        (shape((PAIR, COLS), F32), shape((PAIR, COLS), BF16)),
        [SMEM] + [VMEM] * 3,
        (VMEM,) * 2,
        name="inside",
    )(info, keep, queries_r, packed)
    first, sums, reach = call(
        first_kernel,
        (
            shape((PAIR, COLS), F32),
            shape((CORES * TP, 8, PAIR), F32),
            shape((1,), jnp.int32),
        ),
        [SMEM] + [VMEM] * 7,
        (VMEM, VMEM, SMEM),
        name="first",
    )(info, prefix, *far, inside, query)


    all_sums = exchange(sums)

    def after(known, value):
        return jnp.where(known >= 0, value, jnp.zeros_like(value))

    own4 = move(after(jnp.abs(inside[0, 0]), own0), z_shift=4)
    later23, later4 = after(all_sums[0, 0, 0], own23), after(all_sums[0, 0, 0], own4)
    far23 = [move(later23, x_shift=shift) for shift in (1, 2, 3)]
    far4 = [move(later4, x_shift=shift, keep=lambda x: x + shift >= X) for shift in (1, 2, 3)]
    queries, tops, acc = call(
        near_kernel,
        (
            shape((REPEAT, PAIR, HEAD_DIM), BF16),
            shape((REPEAT, PAIR, HEAD_DIM), F32),
            shape((REPEAT, PAIR, 2 * HEAD_DIM), F32),
        ),
        [SMEM, SMEM] + [VMEM] * 5 + [HBM, VMEM],
        (VMEM,) * 3,
        scratch=(
            pltpu.VMEM((SLOTS * PAIR, 3 * HEAD_DIM), BF16),
            pltpu.VMEM((PAIR, 3 * HEAD_DIM), BF16),
            pltpu.VMEM((PAIR, HEAD_DIM), F32),
            pltpu.SMEM((SLOTS,), jnp.int32),
            pltpu.SemaphoreType.DMA((9,)),
        ),
        name="near",
    )(info, reach, all_sums, first, keep, queries_r, own0, near_packs, own23)
    mine, send, out_sums, _, _ = call(
        far_kernel,
        (
            shape((TOK, COLS), BF16),
            shape((TOK, COLS), BF16),
            shape((CORES * TP, 8, TOK), F32),
            shape((REPEAT, PAIR, HEAD_DIM), F32),
            shape((REPEAT, PAIR, 2 * HEAD_DIM), F32),
        ),
        [SMEM, SMEM] + [VMEM] * 10,
        (VMEM,) * 5,
        scratch=(
            pltpu.VMEM((SLOTS * PAIR, 3 * HEAD_DIM), BF16),
            pltpu.SMEM((SLOTS,), jnp.int32),
            pltpu.SemaphoreType.DMA((10,)),
        ),
        aliases={3: 3, 4: 4},
        name="far",
    )(info, reach, queries, tops, acc, own4, *far4, *far23)
    theirs = swap(send)
    return call(
        last_kernel, shape((TOK, 2 * COLS), BF16), [VMEM] * 3, VMEM, name="last"
    )(exchange(out_sums), mine, theirs)


def solution(mesh):
    grid = Mesh(mesh.devices.reshape(Z, X, CORES, TP), ("z", "x", "core", "tp"))
    tokens, both = P(CTX), P(CTX, "tp")
    return jax.shard_map(
        shards,
        mesh=grid,
        in_specs=(both,) * 3 + (tokens,) + (both,) * 3,
        out_specs=both,
        check_vma=False,
    )
```

```python
import jax
import jax.numpy as jnp
from jax import lax
from jax.experimental import pallas as pl
from jax.experimental.pallas import tpu as pltpu
from jax.sharding import Mesh, PartitionSpec as P

HEAD_DIM = 128
WIDTH = 4096
EPSILON = 1e-05
NEGATIVE = -1e30

TOK = 192
PAIR = 384
REPEAT = 4
COLS = REPEAT * HEAD_DIM
Z, X, CORES, TP = 8, 4, 2, 4
CHUNK = 2
SCALE = HEAD_DIM ** (-0.5) * 1.4426950408889634

F32 = jnp.float32
BF16 = jnp.bfloat16
VMEM = pl.BlockSpec(memory_space=pltpu.VMEM)
SMEM = pl.BlockSpec(memory_space=pltpu.SMEM)
HBM = pl.BlockSpec(memory_space=pltpu.HBM)


def place():
    return lax.axis_index("z"), lax.axis_index("x"), lax.axis_index("core")


def call(kernel, outs, specs_in, specs_out, scratch=(), aliases=None, limit=16, name=None):
    return pl.pallas_call(
        kernel,
        out_shape=outs,
        in_specs=specs_in,
        out_specs=specs_out,
        scratch_shapes=list(scratch),
        input_output_aliases=aliases or {},
        compiler_params=pltpu.CompilerParams(vmem_limit_bytes=limit * 2**20),
        name=name,
    )


def count_below(ref, doc):
    found = jnp.int32(0)
    for step in (128, 64, 32, 16, 8, 4, 2, 1):
        tried = found + step
        last = ref[jnp.minimum(tried, TOK) - 1]
        found = jnp.where((tried <= TOK) & (last < doc), tried, found)
    return found


def half(core):
    return pl.ds(pl.multiple_of(core * HEAD_DIM, HEAD_DIM), HEAD_DIM)


def rows_of(core):
    return pl.ds(pl.multiple_of(core * TOK, 64), TOK)


def prep_kernel(seg, seg_r, own, other, own0_ref, first_ref, state_ref, info_ref):
    core = place()[2]
    for side, ref in ((core, own), (1 - core, other)):
        first_ref[rows_of(side), :HEAD_DIM] = ref[0]
        first_ref[rows_of(side), HEAD_DIM:] = ref[1]
        own0_ref[rows_of(side), :HEAD_DIM] = ref[2]
        own0_ref[rows_of(side), HEAD_DIM:] = ref[3]
    below = [count_below(seg, d) for d in (1, 2, 3)]
    below_r = [count_below(seg_r, d) for d in (1, 2, 3)]
    bounds = [a + b for a, b in zip(below, below_r)]
    first = jnp.where(core == 0, seg[0], seg_r[0])
    last = jnp.where(core == 0, seg_r[TOK - 1], seg[TOK - 1])

    def pick(values, doc):
        out = jnp.int32(0)
        for d in (1, 2, 3):
            out = jnp.where(doc == d, values[d - 1], out)
        return out

    count = PAIR - pick(bounds, last)
    first_end = jnp.where(first == 3, PAIR, pick(bounds, first + 1))
    for place_in, value in enumerate((*bounds, first, last, count, first_end, 0)):
        info_ref[place_in] = jnp.int32(value)
    rows = lax.broadcasted_iota(jnp.int32, (PAIR, HEAD_DIM), 0)
    masked = jnp.where(rows >= PAIR - count, first_ref[:, :HEAD_DIM].astype(F32), 0.0)
    state = lax.dot_general(
        masked.astype(BF16),
        first_ref[:, HEAD_DIM:],
        (((0,), (0,)), ((), ())),
        preferred_element_type=F32,
    )
    state_ref[:HEAD_DIM] = state.astype(BF16)
    state_ref[HEAD_DIM:] = notes(last.astype(F32), count.astype(F32)).astype(BF16)


def notes(last, count):
    row = lax.broadcasted_iota(jnp.int32, (16, HEAD_DIM), 0)
    high = jnp.floor(count * (1.0 / 64.0))
    return jnp.where(
        row == 0, last, jnp.where(row == 1, high, jnp.where(row == 2, count - 64.0 * high, 0.0))
    )


def read_state(ref):
    tail = ref[HEAD_DIM:].astype(F32)
    return ref[:HEAD_DIM].astype(F32), tail[0:1], tail[1:2] * 64.0 + tail[2:3]


def plane_kernel(
    info, own, from1, from2, from3, queries_r, prefix_ref, plane_ref
):
    x = place()[1]
    first = info[3].astype(F32)
    items = [read_state(ref) for ref in (own, from1, from2, from3)]
    prefix = jnp.zeros((HEAD_DIM, HEAD_DIM), F32)
    prefix_count = jnp.zeros((1, HEAD_DIM), F32)
    for shift in (1, 2, 3):
        state, doc, count = items[shift]
        chosen = jnp.where((doc == first) & (x >= shift), 1.0, 0.0)
        prefix += state * chosen
        prefix_count += count * chosen
    prefix_ref[:HEAD_DIM] = prefix
    prefix_ref[HEAD_DIM:] = jnp.broadcast_to(prefix_count, (8, HEAD_DIM))
    last = items[0][1]
    for item in items[1:]:
        last = jnp.maximum(last, item[1])
    total = jnp.zeros((HEAD_DIM, HEAD_DIM), F32)
    total_count = jnp.zeros((1, HEAD_DIM), F32)
    for state, doc, count in items:
        chosen = jnp.where(doc == last, 1.0, 0.0)
        total += state * chosen
        total_count += count * chosen
    plane_ref[:HEAD_DIM] = total.astype(BF16)
    plane_ref[HEAD_DIM:] = notes(last, total_count).astype(BF16)


def document_start(info, rows):
    start = jnp.zeros_like(rows)
    for d in range(3):
        start = jnp.where(rows >= info[d], jnp.maximum(start, info[d]), start)
    return start


def split_dot(wide, narrow):
    high = wide.astype(BF16)
    low = (wide - high.astype(F32)).astype(BF16)
    return jnp.dot(high, narrow, preferred_element_type=F32) + jnp.dot(
        low, narrow, preferred_element_type=F32
    )


def inside_kernel(info, keep, queries_r, packed, inside_ref, query_ref):
    core = place()[2]
    query_ref[rows_of(core), :] = keep[0]
    query_ref[rows_of(1 - core), :] = queries_r[0]
    row = lax.broadcasted_iota(jnp.int32, (PAIR, PAIR), 0)
    column = lax.broadcasted_iota(jnp.int32, (PAIR, PAIR), 1)
    visible = (column <= row) & (column >= document_start(info, row))
    for head in range(REPEAT):
        cols = slice(head * HEAD_DIM, (head + 1) * HEAD_DIM)
        scores = lax.dot_general(
            query_ref[:, cols],
            packed[:, :HEAD_DIM],
            (((1,), (1,)), ((), ())),
            preferred_element_type=F32,
        )
        scores = jnp.where(visible, scores, 0.0)
        inside_ref[:, cols] = split_dot(scores, packed[:, HEAD_DIM:])


def row_sums(squares):
    high = squares.astype(BF16)
    low = (squares - high.astype(F32)).astype(BF16)
    ones = jnp.ones((8, squares.shape[1]), BF16)
    dims = (((1,), (1,)), ((), ()))
    return lax.dot_general(ones, high, dims, preferred_element_type=F32) + lax.dot_general(
        ones, low, dims, preferred_element_type=F32
    )


def first_kernel(
    info, prefix, from1, from2, from3, from4, inside, query, first_ref, sums_ref, count_ref
):
    z = place()[0]
    first = info[3].astype(F32)
    state = prefix[:HEAD_DIM]
    count = prefix[HEAD_DIM : HEAD_DIM + 1]
    for back, ref in enumerate((from1, from2, from3, from4), 1):
        one_state, doc, one_count = read_state(ref)
        chosen = jnp.where((doc == first) & (z >= back), 1.0, 0.0)
        state += one_state * chosen
        count += one_count * chosen
    count_ref[0] = jnp.max(count).astype(jnp.int32)
    high = state.astype(BF16)
    low = (state - high.astype(F32)).astype(BF16)
    in_first = lax.broadcasted_iota(jnp.int32, (PAIR, HEAD_DIM), 0) < info[6]
    squares = jnp.zeros((PAIR, HEAD_DIM), F32)
    for head in range(REPEAT):
        cols = slice(head * HEAD_DIM, (head + 1) * HEAD_DIM)
        queries = query[:, cols]
        earlier = jnp.dot(queries, high, preferred_element_type=F32) + jnp.dot(
            queries, low, preferred_element_type=F32
        )
        out = inside[:, cols] + jnp.where(in_first, earlier, 0.0)
        first_ref[:, cols] = out
        squares += out * out
    sums = row_sums(squares)
    for to in range(CORES * TP):
        sums_ref[to] = sums


def row_scale(sums):
    total = sums[0]
    for device in range(1, CORES * TP):
        total = total + sums[device]
    return lax.transpose(lax.rsqrt(total * (1.0 / WIDTH) + EPSILON), (1, 0))[:, :1]


TILE = 128
TILES = [(head, slice(at, at + TILE)) for head in range(REPEAT) for at in range(0, PAIR, TILE)]


def scores_of(queries, keys, head, part, rows):
    return lax.dot_general(
        queries[head, part],
        keys[rows, :HEAD_DIM],
        (((1,), (1,)), ((), ())),
        preferred_element_type=F32,
    )


def sweep(queries, kv, tops, acc, rows, visible=None, begin=False):
    ahead = scores_of(queries, kv, *TILES[0], rows)
    for at, (head, part) in enumerate(TILES):
        scores = ahead
        if at + 1 < len(TILES):
            ahead = scores_of(queries, kv, *TILES[at + 1], rows)
        if visible is not None:
            scores = jnp.where(visible(part), scores, NEGATIVE)
        top = jnp.max(scores, axis=1, keepdims=True)
        if begin:
            top = jnp.broadcast_to(top, (TILE, HEAD_DIM))
        else:
            old_top = tops[head, part]
            top = jnp.maximum(old_top, top)
        wide_top = jnp.concatenate([top] * (scores.shape[1] // HEAD_DIM), axis=1)
        weights = jnp.exp2((scores - wide_top) * SCALE)
        summed = jnp.dot(weights.astype(BF16), kv[rows, HEAD_DIM:], preferred_element_type=F32)
        tops[head, part] = top
        if begin:
            acc[head, part] = summed
        else:
            shrink = jnp.exp2((old_top - top) * SCALE)
            acc[head, part] = acc[head, part] * jnp.concatenate([shrink, shrink], axis=1) + summed


class Window:
    def __init__(self, info, prior, blocks, kv, bounds, sems):
        self.info, self.kv, self.bounds = info, kv, bounds
        used = jnp.int32(0)
        self.copies = []
        for at, (ref, distance) in enumerate(blocks):
            distance = jnp.int32(distance)
            needed = (distance >= 1) & (distance <= 16) & (prior > (distance - 1) * PAIR)
            slot = jnp.minimum(used, bounds.shape[0] - 1)
            rows = pl.ds(pl.multiple_of(slot * PAIR, PAIR), PAIR)
            copy = pltpu.make_async_copy(ref, kv.at[rows, pl.ds(0, 2 * HEAD_DIM)], sems.at[at])
            self.copies.append((needed, copy))

            @pl.when(needed)
            def _():
                copy.start()
                bounds[slot] = jnp.maximum(distance * PAIR - prior, 0)

            used = used + needed.astype(jnp.int32)
        self.steps = (used + CHUNK - 1) // CHUNK
        kv[:, 2 * HEAD_DIM :] = jnp.ones((kv.shape[0], HEAD_DIM), BF16)

        @pl.when(used % CHUNK != 0)
        def _():
            rows = pl.ds(pl.multiple_of(used * PAIR, PAIR), PAIR)
            kv[rows, : 2 * HEAD_DIM] = jnp.zeros((PAIR, 2 * HEAD_DIM), BF16)
            bounds[used] = jnp.int32(PAIR)

    def absorb(self, queries, tops, acc):
        for needed, copy in self.copies:
            pl.when(needed)(copy.wait)

        @pl.loop(0, self.steps)
        def _(step):
            rows = pl.ds(pl.multiple_of(step * CHUNK * PAIR, CHUNK * PAIR), CHUNK * PAIR)
            low0, low1 = self.bounds[step * CHUNK], self.bounds[step * CHUNK + 1]
            first_end = self.info[6]
            whole = (low0 == 0) & (low1 == 0) & (first_end == PAIR)

            @pl.when(whole)
            def _():
                sweep(queries, self.kv, tops, acc, rows)

            @pl.when(jnp.logical_not(whole))
            def _():
                def visible(part):
                    row = lax.broadcasted_iota(jnp.int32, (TILE, CHUNK * PAIR), 0) + part.start
                    column = lax.broadcasted_iota(jnp.int32, (TILE, CHUNK * PAIR), 1)
                    low = jnp.where(column < PAIR, low0, PAIR + low1)
                    return (column >= low) & (row < first_end)

                sweep(queries, self.kv, tops, acc, rows, visible)


SLOTS = 10


def near_kernel(
    info, reach, sums, first, keep, queries_r, own0, own1, own2, own3, own4, *refs
):
    others3, others4 = refs[:3], refs[3:6]
    queries, tops, acc, kv, own, scales, bounds, sems = refs[6:]
    _, x, core = place()
    blocks = [(own1, 4), (own2, 8), (own3, 12), (own4, 16)]
    for shift, other3, other4 in zip((1, 2, 3), others3, others4):
        blocks.append((other3, 12 + shift - jnp.where(x < shift, 4, 0)))
        blocks.append((other4, jnp.where(x < shift, 12 + shift, 0)))
    window = Window(info, reach[0], blocks, kv, bounds, sems)
    own[:, : 2 * HEAD_DIM] = own0[...]
    own[:, 2 * HEAD_DIM :] = jnp.ones((PAIR, HEAD_DIM), BF16)
    scales[...] = jnp.broadcast_to(row_scale(sums), (PAIR, HEAD_DIM))
    for part, where in ((keep.at[1], rows_of(core)), (queries_r.at[1], rows_of(1 - core))):
        for head in range(REPEAT):
            cols = slice(head * HEAD_DIM, (head + 1) * HEAD_DIM)
            value = part[:, cols].astype(F32) + first[where, cols] * scales[where, :]
            queries[head, where, :] = value.astype(BF16)

    def own_visible(part):
        row = lax.broadcasted_iota(jnp.int32, (TILE, PAIR), 0) + part.start
        column = lax.broadcasted_iota(jnp.int32, (TILE, PAIR), 1)
        return (column <= row) & (column >= document_start(info, row))

    sweep(queries, own, tops, acc, slice(0, PAIR), own_visible, begin=True)
    window.absorb(queries, tops, acc)


def far_kernel(
    info, reach, queries, old_tops, old_acc, gathered,
    mine_ref, send_ref, sums_ref, tops, acc, kv, bounds, sems
):
    _, x, core = place()
    blocks = []
    for shift in (1, 2, 3):
        wrapped = jnp.where(x < shift, 4, 0)
        for back in range(3):
            at = pl.multiple_of((x - shift + wrapped) * (3 * PAIR) + back * PAIR, PAIR)
            blocks.append((gathered.at[pl.ds(at, PAIR)], 4 * back + shift - wrapped))
    window = Window(info, reach[0], blocks, kv, bounds, sems)
    window.absorb(queries, tops, acc)
    for side in range(CORES):
        where = slice(side * TOK, (side + 1) * TOK)
        squares = jnp.zeros((TOK, HEAD_DIM), F32)
        outs = []
        for head in range(REPEAT):
            summed = acc[head, where, :]
            out = (summed[:, :HEAD_DIM] / summed[:, HEAD_DIM:]).astype(BF16)
            outs.append(out)
            widened = out.astype(F32)
            squares += widened * widened
        whole = jnp.concatenate(outs, axis=1)

        @pl.when(core == side)
        def _():
            mine_ref[...] = whole

        @pl.when(core != side)
        def _():
            send_ref[...] = whole

        sums = row_sums(squares)
        for to in range(TP):
            sums_ref[side * TP + to] = sums


def last_kernel(sums, mine, theirs, out_ref):
    core = place()[2]
    scale = row_scale(sums)
    for ref, side in ((mine, core), (theirs, 1 - core)):
        cols = pl.ds(pl.multiple_of(side * COLS, COLS), COLS)
        out_ref[:, cols] = (ref[...].astype(F32) * scale).astype(BF16)


CTX = ("z", "x", "core")


def move(value, z_shift=0, x_shift=0, core_shift=0, keep=lambda x: True):
    pairs = []
    for z in range(Z):
        for x in range(X):
            for core in range(CORES):
                to = ((z + z_shift) % Z * X + (x + x_shift) % X) * CORES
                if keep(x):
                    pairs.append(((z * X + x) * CORES + core, to + (core + core_shift) % CORES))
    return lax.ppermute(value, CTX, pairs)


def swap(value):
    return move(value, core_shift=1)


def exchange(sums):
    return lax.all_to_all(sums, ("core", "tp"), 0, 0, tiled=True)


def shape(dims, kind):
    return jax.ShapeDtypeStruct(dims, kind)


def shards(query_one, key_one, value_one, segments, query_base, key_two, value_two):
    core = lax.axis_index("core")

    def halves(arrays):
        low = jnp.stack([array[:, : array.shape[1] // 2] for array in arrays])
        high = jnp.stack([array[:, array.shape[1] // 2 :] for array in arrays])
        return jnp.where(core == 0, low, high), jnp.where(core == 0, high, low)

    segments_r = swap(segments)
    own_keep, own_send = halves((key_one, value_one, key_two, value_two))
    own0, packed, state, info = call(
        prep_kernel,
        (
            shape((PAIR, 2 * HEAD_DIM), BF16),
            shape((PAIR, 2 * HEAD_DIM), BF16),
            shape((144, HEAD_DIM), BF16),
            shape((8,), jnp.int32),
        ),
        [SMEM, SMEM, VMEM, VMEM],
        (VMEM,) * 3 + (SMEM,),
        name="prep",
    )(segments, segments_r, own_keep, swap(own_send))
    keep, query_send = halves((query_one, query_base))
    queries_r = swap(query_send)

    own1 = move(own0, z_shift=1)
    near = [move(state, x_shift=shift) for shift in (1, 2, 3)]
    prefix, plane = call(
        plane_kernel,
        (shape((HEAD_DIM + 8, HEAD_DIM), F32), shape((144, HEAD_DIM), BF16)),
        [SMEM] + [VMEM] * 5,
        (VMEM,) * 2,
        name="plane",
    )(info, state, *near, queries_r)
    far = [move(plane, z_shift=back) for back in (1, 2, 3, 4)]
    own2 = move(own1, z_shift=1)
    own3 = move(own2, z_shift=1)
    own4 = move(own3, z_shift=1)
    gathered = lax.all_gather(jnp.concatenate([own0, own1, own2]), "x", axis=0, tiled=True)

    inside, query = call(
        inside_kernel,
        (shape((PAIR, COLS), F32), shape((PAIR, COLS), BF16)),
        [SMEM] + [VMEM] * 3,
        (VMEM,) * 2,
        name="inside",
    )(info, keep, queries_r, packed)
    first, sums, reach = call(
        first_kernel,
        (
            shape((PAIR, COLS), F32),
            shape((CORES * TP, 8, PAIR), F32),
            shape((1,), jnp.int32),
        ),
        [SMEM] + [VMEM] * 7,
        (VMEM, VMEM, SMEM),
        name="first",
    )(info, prefix, *far, inside, query)


    all_sums = exchange(sums)

    def after(known, value):
        return jnp.where(known >= 0, value, jnp.zeros_like(value))

    later3, later4 = after(reach[0], own3), after(reach[0], own4)
    far3 = [move(later3, x_shift=shift) for shift in (1, 2, 3)]
    far4 = [move(later4, x_shift=shift, keep=lambda x: x + shift >= X) for shift in (1, 2, 3)]
    queries, tops, acc = call(
        near_kernel,
        (
            shape((REPEAT, PAIR, HEAD_DIM), BF16),
            shape((REPEAT, PAIR, HEAD_DIM), F32),
            shape((REPEAT, PAIR, 2 * HEAD_DIM), F32),
        ),
        [SMEM, SMEM] + [VMEM] * 15,
        (VMEM,) * 3,
        scratch=(
            pltpu.VMEM((SLOTS * PAIR, 3 * HEAD_DIM), BF16),
            pltpu.VMEM((PAIR, 3 * HEAD_DIM), BF16),
            pltpu.VMEM((PAIR, HEAD_DIM), F32),
            pltpu.SMEM((SLOTS,), jnp.int32),
            pltpu.SemaphoreType.DMA((10,)),
        ),
        name="near",
    )(
        info, reach, all_sums, first, keep, queries_r, own0, own1, own2, own3, own4, *far3, *far4
    )
    mine, send, out_sums, _, _ = call(
        far_kernel,
        (
            shape((TOK, COLS), BF16),
            shape((TOK, COLS), BF16),
            shape((CORES * TP, 8, TOK), F32),
            shape((REPEAT, PAIR, HEAD_DIM), F32),
            shape((REPEAT, PAIR, 2 * HEAD_DIM), F32),
        ),
        [SMEM, SMEM] + [VMEM] * 3 + [HBM],
        (VMEM,) * 5,
        scratch=(
            pltpu.VMEM((SLOTS * PAIR, 3 * HEAD_DIM), BF16),
            pltpu.SMEM((SLOTS,), jnp.int32),
            pltpu.SemaphoreType.DMA((10,)),
        ),
        aliases={3: 3, 4: 4},
        name="far",
    )(info, reach, queries, tops, acc, gathered)
    theirs = swap(send)
    return call(
        last_kernel, shape((TOK, 2 * COLS), BF16), [VMEM] * 3, VMEM, name="last"
    )(exchange(out_sums), mine, theirs)


def solution(mesh):
    grid = Mesh(mesh.devices.reshape(Z, X, CORES, TP), ("z", "x", "core", "tp"))
    tokens, both = P(CTX), P(CTX, "tp")
    return jax.shard_map(
        shards,
        mesh=grid,
        in_specs=(both,) * 3 + (tokens,) + (both,) * 3,
        out_specs=both,
        check_vma=False,
    )
```

```python
import jax
import jax.numpy as jnp
from jax import lax
from jax.experimental import pallas as pl
from jax.experimental.pallas import tpu as pltpu
from jax.sharding import Mesh, PartitionSpec as P

HEAD_DIM = 128
WIDTH = 4096
EPSILON = 1e-05
NEGATIVE = -1e30

TOK = 192
PAIR = 384
REPEAT = 4
COLS = REPEAT * HEAD_DIM
Z, X, CORES, TP = 8, 4, 2, 4
CHUNK = 2
SCALE = HEAD_DIM ** (-0.5) * 1.4426950408889634

F32 = jnp.float32
BF16 = jnp.bfloat16
VMEM = pl.BlockSpec(memory_space=pltpu.VMEM)
SMEM = pl.BlockSpec(memory_space=pltpu.SMEM)
HBM = pl.BlockSpec(memory_space=pltpu.HBM)


def place():
    return lax.axis_index("z"), lax.axis_index("x"), lax.axis_index("core")


def call(kernel, outs, specs_in, specs_out, scratch=(), aliases=None, limit=16, name=None):
    return pl.pallas_call(
        kernel,
        out_shape=outs,
        in_specs=specs_in,
        out_specs=specs_out,
        scratch_shapes=list(scratch),
        input_output_aliases=aliases or {},
        compiler_params=pltpu.CompilerParams(vmem_limit_bytes=limit * 2**20),
        name=name,
    )


def count_below(ref, doc):
    found = jnp.int32(0)
    for step in (128, 64, 32, 16, 8, 4, 2, 1):
        tried = found + step
        last = ref[jnp.minimum(tried, TOK) - 1]
        found = jnp.where((tried <= TOK) & (last < doc), tried, found)
    return found


def half(core):
    return pl.ds(pl.multiple_of(core * HEAD_DIM, HEAD_DIM), HEAD_DIM)


def rows_of(core):
    return pl.ds(pl.multiple_of(core * TOK, 64), TOK)


def prep_kernel(seg, seg_r, own, other, own0_ref, first_ref, state_ref, info_ref):
    core = place()[2]
    for side, ref in ((core, own), (1 - core, other)):
        first_ref[rows_of(side), :HEAD_DIM] = ref[0]
        first_ref[rows_of(side), HEAD_DIM:] = ref[1]
        own0_ref[rows_of(side), :HEAD_DIM] = ref[2]
        own0_ref[rows_of(side), HEAD_DIM:] = ref[3]
    below = [count_below(seg, d) for d in (1, 2, 3)]
    below_r = [count_below(seg_r, d) for d in (1, 2, 3)]
    bounds = [a + b for a, b in zip(below, below_r)]
    first = jnp.where(core == 0, seg[0], seg_r[0])
    last = jnp.where(core == 0, seg_r[TOK - 1], seg[TOK - 1])

    def pick(values, doc):
        out = jnp.int32(0)
        for d in (1, 2, 3):
            out = jnp.where(doc == d, values[d - 1], out)
        return out

    count = PAIR - pick(bounds, last)
    first_end = jnp.where(first == 3, PAIR, pick(bounds, first + 1))
    for place_in, value in enumerate((*bounds, first, last, count, first_end, 0)):
        info_ref[place_in] = jnp.int32(value)
    rows = lax.broadcasted_iota(jnp.int32, (PAIR, HEAD_DIM), 0)
    masked = jnp.where(rows >= PAIR - count, first_ref[:, :HEAD_DIM].astype(F32), 0.0)
    state = lax.dot_general(
        masked.astype(BF16),
        first_ref[:, HEAD_DIM:],
        (((0,), (0,)), ((), ())),
        preferred_element_type=F32,
    )
    state_ref[:HEAD_DIM] = state.astype(BF16)
    state_ref[HEAD_DIM:] = notes(last.astype(F32), count.astype(F32)).astype(BF16)


def notes(last, count):
    row = lax.broadcasted_iota(jnp.int32, (16, HEAD_DIM), 0)
    high = jnp.floor(count * (1.0 / 64.0))
    return jnp.where(
        row == 0, last, jnp.where(row == 1, high, jnp.where(row == 2, count - 64.0 * high, 0.0))
    )


def read_state(ref):
    tail = ref[HEAD_DIM:].astype(F32)
    return ref[:HEAD_DIM].astype(F32), tail[0:1], tail[1:2] * 64.0 + tail[2:3]


def plane_kernel(
    info, own, from1, from2, from3, queries_r, prefix_ref, plane_ref
):
    x = place()[1]
    first = info[3].astype(F32)
    items = [read_state(ref) for ref in (own, from1, from2, from3)]
    prefix = jnp.zeros((HEAD_DIM, HEAD_DIM), F32)
    prefix_count = jnp.zeros((1, HEAD_DIM), F32)
    for shift in (1, 2, 3):
        state, doc, count = items[shift]
        chosen = jnp.where((doc == first) & (x >= shift), 1.0, 0.0)
        prefix += state * chosen
        prefix_count += count * chosen
    prefix_ref[:HEAD_DIM] = prefix
    prefix_ref[HEAD_DIM:] = jnp.broadcast_to(prefix_count, (8, HEAD_DIM))
    last = items[0][1]
    for item in items[1:]:
        last = jnp.maximum(last, item[1])
    total = jnp.zeros((HEAD_DIM, HEAD_DIM), F32)
    total_count = jnp.zeros((1, HEAD_DIM), F32)
    for state, doc, count in items:
        chosen = jnp.where(doc == last, 1.0, 0.0)
        total += state * chosen
        total_count += count * chosen
    plane_ref[:HEAD_DIM] = total.astype(BF16)
    plane_ref[HEAD_DIM:] = notes(last, total_count).astype(BF16)


def document_start(info, rows):
    start = jnp.zeros_like(rows)
    for d in range(3):
        start = jnp.where(rows >= info[d], jnp.maximum(start, info[d]), start)
    return start


def split_dot(wide, narrow):
    high = wide.astype(BF16)
    low = (wide - high.astype(F32)).astype(BF16)
    return jnp.dot(high, narrow, preferred_element_type=F32) + jnp.dot(
        low, narrow, preferred_element_type=F32
    )


def inside_kernel(info, keep, queries_r, packed, inside_ref, query_ref):
    core = place()[2]
    query_ref[rows_of(core), :] = keep[0]
    query_ref[rows_of(1 - core), :] = queries_r[0]
    row = lax.broadcasted_iota(jnp.int32, (PAIR, PAIR), 0)
    column = lax.broadcasted_iota(jnp.int32, (PAIR, PAIR), 1)
    visible = (column <= row) & (column >= document_start(info, row))
    for head in range(REPEAT):
        cols = slice(head * HEAD_DIM, (head + 1) * HEAD_DIM)
        scores = lax.dot_general(
            query_ref[:, cols],
            packed[:, :HEAD_DIM],
            (((1,), (1,)), ((), ())),
            preferred_element_type=F32,
        )
        scores = jnp.where(visible, scores, 0.0)
        inside_ref[:, cols] = split_dot(scores, packed[:, HEAD_DIM:])


def row_sums(squares):
    high = squares.astype(BF16)
    low = (squares - high.astype(F32)).astype(BF16)
    ones = jnp.ones((8, squares.shape[1]), BF16)
    dims = (((1,), (1,)), ((), ()))
    return lax.dot_general(ones, high, dims, preferred_element_type=F32) + lax.dot_general(
        ones, low, dims, preferred_element_type=F32
    )


def first_kernel(
    info, prefix, from1, from2, from3, from4, inside, query, first_ref, sums_ref, count_ref
):
    z = place()[0]
    first = info[3].astype(F32)
    state = prefix[:HEAD_DIM]
    count = prefix[HEAD_DIM : HEAD_DIM + 1]
    for back, ref in enumerate((from1, from2, from3, from4), 1):
        one_state, doc, one_count = read_state(ref)
        chosen = jnp.where((doc == first) & (z >= back), 1.0, 0.0)
        state += one_state * chosen
        count += one_count * chosen
    count_ref[0] = jnp.max(count).astype(jnp.int32)
    high = state.astype(BF16)
    low = (state - high.astype(F32)).astype(BF16)
    in_first = lax.broadcasted_iota(jnp.int32, (PAIR, HEAD_DIM), 0) < info[6]
    squares = jnp.zeros((PAIR, HEAD_DIM), F32)
    for head in range(REPEAT):
        cols = slice(head * HEAD_DIM, (head + 1) * HEAD_DIM)
        queries = query[:, cols]
        earlier = jnp.dot(queries, high, preferred_element_type=F32) + jnp.dot(
            queries, low, preferred_element_type=F32
        )
        out = inside[:, cols] + jnp.where(in_first, earlier, 0.0)
        first_ref[:, cols] = out
        squares += out * out
    sums = row_sums(squares)
    for to in range(CORES * TP):
        sums_ref[to] = sums


def row_scale(sums):
    total = sums[0]
    for device in range(1, CORES * TP):
        total = total + sums[device]
    return lax.transpose(lax.rsqrt(total * (1.0 / WIDTH) + EPSILON), (1, 0))[:, :1]


TILE = 128
TILES = [(head, slice(at, at + TILE)) for head in range(REPEAT) for at in range(0, PAIR, TILE)]


def scores_of(queries, keys, head, part, rows):
    return lax.dot_general(
        queries[head, part],
        keys[rows, :HEAD_DIM],
        (((1,), (1,)), ((), ())),
        preferred_element_type=F32,
    )


def sweep(queries, kv, tops, acc, rows, visible=None, begin=False):
    ahead = scores_of(queries, kv, *TILES[0], rows)
    for at, (head, part) in enumerate(TILES):
        scores = ahead
        if at + 1 < len(TILES):
            ahead = scores_of(queries, kv, *TILES[at + 1], rows)
        if visible is not None:
            scores = jnp.where(visible(part), scores, NEGATIVE)
        top = jnp.max(scores, axis=1, keepdims=True)
        if begin:
            top = jnp.broadcast_to(top, (TILE, HEAD_DIM))
        else:
            old_top = tops[head, part]
            top = jnp.maximum(old_top, top)
        wide_top = jnp.concatenate([top] * (scores.shape[1] // HEAD_DIM), axis=1)
        weights = jnp.exp2((scores - wide_top) * SCALE)
        summed = jnp.dot(weights.astype(BF16), kv[rows, HEAD_DIM:], preferred_element_type=F32)
        tops[head, part] = top
        if begin:
            acc[head, part] = summed
        else:
            shrink = jnp.exp2((old_top - top) * SCALE)
            acc[head, part] = acc[head, part] * jnp.concatenate([shrink, shrink], axis=1) + summed


class Window:
    def __init__(self, info, prior, blocks, kv, bounds, sems):
        self.info, self.kv, self.bounds = info, kv, bounds
        used = jnp.int32(0)
        self.copies = []
        for at, (ref, distance) in enumerate(blocks):
            distance = jnp.int32(distance)
            needed = (distance >= 1) & (distance <= 16) & (prior > (distance - 1) * PAIR)
            slot = jnp.minimum(used, bounds.shape[0] - 1)
            rows = pl.ds(pl.multiple_of(slot * PAIR, PAIR), PAIR)
            copy = pltpu.make_async_copy(ref, kv.at[rows, pl.ds(0, 2 * HEAD_DIM)], sems.at[at])
            self.copies.append((needed, copy))

            @pl.when(needed)
            def _():
                copy.start()
                bounds[slot] = jnp.maximum(distance * PAIR - prior, 0)

            used = used + needed.astype(jnp.int32)
        self.steps = (used + CHUNK - 1) // CHUNK
        kv[:, 2 * HEAD_DIM :] = jnp.ones((kv.shape[0], HEAD_DIM), BF16)

        @pl.when(used % CHUNK != 0)
        def _():
            rows = pl.ds(pl.multiple_of(used * PAIR, PAIR), PAIR)
            kv[rows, : 2 * HEAD_DIM] = jnp.zeros((PAIR, 2 * HEAD_DIM), BF16)
            bounds[used] = jnp.int32(PAIR)

    def absorb(self, queries, tops, acc):
        for needed, copy in self.copies:
            pl.when(needed)(copy.wait)

        @pl.loop(0, self.steps)
        def _(step):
            rows = pl.ds(pl.multiple_of(step * CHUNK * PAIR, CHUNK * PAIR), CHUNK * PAIR)
            low0, low1 = self.bounds[step * CHUNK], self.bounds[step * CHUNK + 1]
            first_end = self.info[6]
            whole = (low0 == 0) & (low1 == 0) & (first_end == PAIR)

            @pl.when(whole)
            def _():
                sweep(queries, self.kv, tops, acc, rows)

            @pl.when(jnp.logical_not(whole))
            def _():
                def visible(part):
                    row = lax.broadcasted_iota(jnp.int32, (TILE, CHUNK * PAIR), 0) + part.start
                    column = lax.broadcasted_iota(jnp.int32, (TILE, CHUNK * PAIR), 1)
                    low = jnp.where(column < PAIR, low0, PAIR + low1)
                    return (column >= low) & (row < first_end)

                sweep(queries, self.kv, tops, acc, rows, visible)


SLOTS = 10


def near_kernel(
    info, reach, sums, first, keep, queries_r, own0, own1, own2, own3, own4, *refs
):
    others1, others2 = refs[:3], refs[3:6]
    queries, tops, acc, kv, own, scales, bounds, sems = refs[6:]
    _, x, core = place()
    blocks = [(own1, 4), (own2, 8), (own3, 12), (own4, 16)]
    for shift, other1, other2 in zip((1, 2, 3), others1, others2):
        wrapped = jnp.where(x < shift, 4, 0)
        blocks.append((other1, 4 + shift - wrapped))
        blocks.append((other2, 8 + shift - wrapped))
    window = Window(info, reach[0], blocks, kv, bounds, sems)
    own[:, : 2 * HEAD_DIM] = own0[...]
    own[:, 2 * HEAD_DIM :] = jnp.ones((PAIR, HEAD_DIM), BF16)
    scales[...] = jnp.broadcast_to(row_scale(sums), (PAIR, HEAD_DIM))
    for part, where in ((keep.at[1], rows_of(core)), (queries_r.at[1], rows_of(1 - core))):
        for head in range(REPEAT):
            cols = slice(head * HEAD_DIM, (head + 1) * HEAD_DIM)
            value = part[:, cols].astype(F32) + first[where, cols] * scales[where, :]
            queries[head, where, :] = value.astype(BF16)

    def own_visible(part):
        row = lax.broadcasted_iota(jnp.int32, (TILE, PAIR), 0) + part.start
        column = lax.broadcasted_iota(jnp.int32, (TILE, PAIR), 1)
        return (column <= row) & (column >= document_start(info, row))

    sweep(queries, own, tops, acc, slice(0, PAIR), own_visible, begin=True)
    window.absorb(queries, tops, acc)


def far_kernel(info, reach, queries, old_tops, old_acc, *refs):
    others3, others04 = refs[:3], refs[3:6]
    mine_ref, send_ref, sums_ref, tops, acc, kv, bounds, sems = refs[6:]
    _, x, core = place()
    blocks = []
    for shift, other3, other04 in zip((1, 2, 3), others3, others04):
        blocks.append((other3, 12 + shift - jnp.where(x < shift, 4, 0)))
        blocks.append((other04, jnp.where(x < shift, 12 + shift, shift)))
    window = Window(info, reach[0], blocks, kv, bounds, sems)
    window.absorb(queries, tops, acc)
    for side in range(CORES):
        where = slice(side * TOK, (side + 1) * TOK)
        squares = jnp.zeros((TOK, HEAD_DIM), F32)
        outs = []
        for head in range(REPEAT):
            summed = acc[head, where, :]
            out = (summed[:, :HEAD_DIM] / summed[:, HEAD_DIM:]).astype(BF16)
            outs.append(out)
            widened = out.astype(F32)
            squares += widened * widened
        whole = jnp.concatenate(outs, axis=1)

        @pl.when(core == side)
        def _():
            mine_ref[...] = whole

        @pl.when(core != side)
        def _():
            send_ref[...] = whole

        sums = row_sums(squares)
        for to in range(TP):
            sums_ref[side * TP + to] = sums


def last_kernel(sums, mine, theirs, out_ref):
    core = place()[2]
    scale = row_scale(sums)
    for ref, side in ((mine, core), (theirs, 1 - core)):
        cols = pl.ds(pl.multiple_of(side * COLS, COLS), COLS)
        out_ref[:, cols] = (ref[...].astype(F32) * scale).astype(BF16)


CTX = ("z", "x", "core")


def move(value, z_shift=0, x_shift=0, core_shift=0, keep=lambda x: True):
    pairs = []
    for z in range(Z):
        for x in range(X):
            for core in range(CORES):
                to = ((z + z_shift) % Z * X + (x + x_shift) % X) * CORES
                if keep(x):
                    pairs.append(((z * X + x) * CORES + core, to + (core + core_shift) % CORES))
    return lax.ppermute(value, CTX, pairs)


def swap(value):
    return move(value, core_shift=1)


def exchange(sums):
    return lax.all_to_all(sums, ("core", "tp"), 0, 0, tiled=True)


def shape(dims, kind):
    return jax.ShapeDtypeStruct(dims, kind)


def shards(query_one, key_one, value_one, segments, query_base, key_two, value_two):
    core = lax.axis_index("core")

    def halves(arrays):
        low = jnp.stack([array[:, : array.shape[1] // 2] for array in arrays])
        high = jnp.stack([array[:, array.shape[1] // 2 :] for array in arrays])
        return jnp.where(core == 0, low, high), jnp.where(core == 0, high, low)

    segments_r = swap(segments)
    own_keep, own_send = halves((key_one, value_one, key_two, value_two))
    own0, packed, state, info = call(
        prep_kernel,
        (
            shape((PAIR, 2 * HEAD_DIM), BF16),
            shape((PAIR, 2 * HEAD_DIM), BF16),
            shape((144, HEAD_DIM), BF16),
            shape((8,), jnp.int32),
        ),
        [SMEM, SMEM, VMEM, VMEM],
        (VMEM,) * 3 + (SMEM,),
        name="prep",
    )(segments, segments_r, own_keep, swap(own_send))
    keep, query_send = halves((query_one, query_base))
    queries_r = swap(query_send)

    own1 = move(own0, z_shift=1)
    near = [move(state, x_shift=shift) for shift in (1, 2, 3)]
    prefix, plane = call(
        plane_kernel,
        (shape((HEAD_DIM + 8, HEAD_DIM), F32), shape((144, HEAD_DIM), BF16)),
        [SMEM] + [VMEM] * 5,
        (VMEM,) * 2,
        name="plane",
    )(info, state, *near, queries_r)
    far = [move(plane, z_shift=back) for back in (1, 2, 3, 4)]

    def after(known, value):
        return jnp.where(known >= 0, value, jnp.zeros_like(value))

    own2 = move(own1, z_shift=1)
    own3 = move(own2, z_shift=1)
    own4 = move(own3, z_shift=1)

    inside, query = call(
        inside_kernel,
        (shape((PAIR, COLS), F32), shape((PAIR, COLS), BF16)),
        [SMEM] + [VMEM] * 3,
        (VMEM,) * 2,
        name="inside",
    )(info, keep, queries_r, packed)
    first, sums, reach = call(
        first_kernel,
        (
            shape((PAIR, COLS), F32),
            shape((CORES * TP, 8, PAIR), F32),
            shape((1,), jnp.int32),
        ),
        [SMEM] + [VMEM] * 7,
        (VMEM, VMEM, SMEM),
        name="first",
    )(info, prefix, *far, inside, query)


    all_sums = exchange(sums)
    x = lax.axis_index("x")
    x_shifts = (1, 2, 3)
    others = [move(after(reach[0], own1), x_shift=shift) for shift in x_shifts]
    others += [move(own2, x_shift=shift) for shift in x_shifts]
    others += [move(own3, x_shift=shift) for shift in x_shifts]
    late4 = after(all_sums[0, 0, 0], own4)
    others += [move(jnp.where(x + shift < X, own0, late4), x_shift=shift) for shift in x_shifts]
    queries, tops, acc = call(
        near_kernel,
        (
            shape((REPEAT, PAIR, HEAD_DIM), BF16),
            shape((REPEAT, PAIR, HEAD_DIM), F32),
            shape((REPEAT, PAIR, 2 * HEAD_DIM), F32),
        ),
        [SMEM, SMEM] + [VMEM] * 15,
        (VMEM,) * 3,
        scratch=(
            pltpu.VMEM((SLOTS * PAIR, 3 * HEAD_DIM), BF16),
            pltpu.VMEM((PAIR, 3 * HEAD_DIM), BF16),
            pltpu.VMEM((PAIR, HEAD_DIM), F32),
            pltpu.SMEM((SLOTS,), jnp.int32),
            pltpu.SemaphoreType.DMA((10,)),
        ),
        name="near",
    )(
        info, reach, all_sums, first, keep, queries_r, own0, own1, own2, own3, own4, *others[:6]
    )
    mine, send, out_sums, _, _ = call(
        far_kernel,
        (
            shape((TOK, COLS), BF16),
            shape((TOK, COLS), BF16),
            shape((CORES * TP, 8, TOK), F32),
            shape((REPEAT, PAIR, HEAD_DIM), F32),
            shape((REPEAT, PAIR, 2 * HEAD_DIM), F32),
        ),
        [SMEM, SMEM] + [VMEM] * 9,
        (VMEM,) * 5,
        scratch=(
            pltpu.VMEM((SLOTS * PAIR, 3 * HEAD_DIM), BF16),
            pltpu.SMEM((SLOTS,), jnp.int32),
            pltpu.SemaphoreType.DMA((10,)),
        ),
        aliases={3: 3, 4: 4},
        name="far",
    )(info, reach, queries, tops, acc, *others[6:])
    theirs = swap(send)
    return call(
        last_kernel, shape((TOK, 2 * COLS), BF16), [VMEM] * 3, VMEM, name="last"
    )(exchange(out_sums), mine, theirs)


def solution(mesh):
    grid = Mesh(mesh.devices.reshape(Z, X, CORES, TP), ("z", "x", "core", "tp"))
    tokens, both = P(CTX), P(CTX, "tp")
    return jax.shard_map(
        shards,
        mesh=grid,
        in_specs=(both,) * 3 + (tokens,) + (both,) * 3,
        out_specs=both,
        check_vma=False,
    )
```

```python
import jax
import jax.numpy as jnp
from jax import lax
from jax.experimental import pallas as pl
from jax.experimental.pallas import tpu as pltpu
from jax.sharding import Mesh, PartitionSpec as P

HEAD_DIM = 128
WIDTH = 4096
EPSILON = 1e-05
NEGATIVE = -1e30

TOK = 192
PAIR = 384
REPEAT = 4
COLS = REPEAT * HEAD_DIM
Z, X, CORES, TP = 8, 4, 2, 4
CHUNK = 2
SCALE = HEAD_DIM ** (-0.5) * 1.4426950408889634

F32 = jnp.float32
BF16 = jnp.bfloat16
VMEM = pl.BlockSpec(memory_space=pltpu.VMEM)
SMEM = pl.BlockSpec(memory_space=pltpu.SMEM)
HBM = pl.BlockSpec(memory_space=pltpu.HBM)


def place():
    return lax.axis_index("z"), lax.axis_index("x"), lax.axis_index("core")


def call(kernel, outs, specs_in, specs_out, scratch=(), aliases=None, limit=16, name=None):
    return pl.pallas_call(
        kernel,
        out_shape=outs,
        in_specs=specs_in,
        out_specs=specs_out,
        scratch_shapes=list(scratch),
        input_output_aliases=aliases or {},
        compiler_params=pltpu.CompilerParams(vmem_limit_bytes=limit * 2**20),
        name=name,
    )


def count_below(ref, doc):
    found = jnp.int32(0)
    for step in (128, 64, 32, 16, 8, 4, 2, 1):
        tried = found + step
        last = ref[jnp.minimum(tried, TOK) - 1]
        found = jnp.where((tried <= TOK) & (last < doc), tried, found)
    return found


def half(core):
    return pl.ds(pl.multiple_of(core * HEAD_DIM, HEAD_DIM), HEAD_DIM)


def rows_of(core):
    return pl.ds(pl.multiple_of(core * TOK, 64), TOK)


def prep_kernel(seg, seg_r, own, other, own0_ref, first_ref, state_ref, info_ref):
    core = place()[2]
    for side, ref in ((core, own), (1 - core, other)):
        first_ref[rows_of(side), :HEAD_DIM] = ref[0]
        first_ref[rows_of(side), HEAD_DIM:] = ref[1]
        own0_ref[rows_of(side), :HEAD_DIM] = ref[2]
        own0_ref[rows_of(side), HEAD_DIM:] = ref[3]
    below = [count_below(seg, d) for d in (1, 2, 3)]
    below_r = [count_below(seg_r, d) for d in (1, 2, 3)]
    bounds = [a + b for a, b in zip(below, below_r)]
    first = jnp.where(core == 0, seg[0], seg_r[0])
    last = jnp.where(core == 0, seg_r[TOK - 1], seg[TOK - 1])

    def pick(values, doc):
        out = jnp.int32(0)
        for d in (1, 2, 3):
            out = jnp.where(doc == d, values[d - 1], out)
        return out

    count = PAIR - pick(bounds, last)
    first_end = jnp.where(first == 3, PAIR, pick(bounds, first + 1))
    for place_in, value in enumerate((*bounds, first, last, count, first_end, 0)):
        info_ref[place_in] = jnp.int32(value)
    rows = lax.broadcasted_iota(jnp.int32, (PAIR, HEAD_DIM), 0)
    masked = jnp.where(rows >= PAIR - count, first_ref[:, :HEAD_DIM].astype(F32), 0.0)
    state = lax.dot_general(
        masked.astype(BF16),
        first_ref[:, HEAD_DIM:],
        (((0,), (0,)), ((), ())),
        preferred_element_type=F32,
    )
    state_ref[:HEAD_DIM] = state.astype(BF16)
    state_ref[HEAD_DIM:] = notes(last.astype(F32), count.astype(F32)).astype(BF16)


def notes(last, count):
    row = lax.broadcasted_iota(jnp.int32, (16, HEAD_DIM), 0)
    high = jnp.floor(count * (1.0 / 64.0))
    return jnp.where(
        row == 0, last, jnp.where(row == 1, high, jnp.where(row == 2, count - 64.0 * high, 0.0))
    )


def read_state(ref):
    tail = ref[HEAD_DIM:].astype(F32)
    return ref[:HEAD_DIM].astype(F32), tail[0:1], tail[1:2] * 64.0 + tail[2:3]


def plane_kernel(
    info, own, from1, from2, from3, own1, queries_r, prefix_ref, plane_ref, later1_ref
):
    x = place()[1]
    later1_ref[...] = own1[...]
    first = info[3].astype(F32)
    items = [read_state(ref) for ref in (own, from1, from2, from3)]
    prefix = jnp.zeros((HEAD_DIM, HEAD_DIM), F32)
    prefix_count = jnp.zeros((1, HEAD_DIM), F32)
    for shift in (1, 2, 3):
        state, doc, count = items[shift]
        chosen = jnp.where((doc == first) & (x >= shift), 1.0, 0.0)
        prefix += state * chosen
        prefix_count += count * chosen
    prefix_ref[:HEAD_DIM] = prefix
    prefix_ref[HEAD_DIM:] = jnp.broadcast_to(prefix_count, (8, HEAD_DIM))
    last = items[0][1]
    for item in items[1:]:
        last = jnp.maximum(last, item[1])
    total = jnp.zeros((HEAD_DIM, HEAD_DIM), F32)
    total_count = jnp.zeros((1, HEAD_DIM), F32)
    for state, doc, count in items:
        chosen = jnp.where(doc == last, 1.0, 0.0)
        total += state * chosen
        total_count += count * chosen
    plane_ref[:HEAD_DIM] = total.astype(BF16)
    plane_ref[HEAD_DIM:] = notes(last, total_count).astype(BF16)


def document_start(info, rows):
    start = jnp.zeros_like(rows)
    for d in range(3):
        start = jnp.where(rows >= info[d], jnp.maximum(start, info[d]), start)
    return start


def split_dot(wide, narrow):
    high = wide.astype(BF16)
    low = (wide - high.astype(F32)).astype(BF16)
    return jnp.dot(high, narrow, preferred_element_type=F32) + jnp.dot(
        low, narrow, preferred_element_type=F32
    )


def inside_kernel(info, keep, queries_r, packed, inside_ref, query_ref):
    core = place()[2]
    query_ref[rows_of(core), :] = keep[0]
    query_ref[rows_of(1 - core), :] = queries_r[0]
    row = lax.broadcasted_iota(jnp.int32, (PAIR, PAIR), 0)
    column = lax.broadcasted_iota(jnp.int32, (PAIR, PAIR), 1)
    visible = (column <= row) & (column >= document_start(info, row))
    for head in range(REPEAT):
        cols = slice(head * HEAD_DIM, (head + 1) * HEAD_DIM)
        scores = lax.dot_general(
            query_ref[:, cols],
            packed[:, :HEAD_DIM],
            (((1,), (1,)), ((), ())),
            preferred_element_type=F32,
        )
        scores = jnp.where(visible, scores, 0.0)
        inside_ref[:, cols] = split_dot(scores, packed[:, HEAD_DIM:])


def row_sums(squares):
    high = squares.astype(BF16)
    low = (squares - high.astype(F32)).astype(BF16)
    ones = jnp.ones((8, squares.shape[1]), BF16)
    dims = (((1,), (1,)), ((), ()))
    return lax.dot_general(ones, high, dims, preferred_element_type=F32) + lax.dot_general(
        ones, low, dims, preferred_element_type=F32
    )


def first_kernel(
    info, prefix, from1, from2, from3, from4, inside, query, first_ref, sums_ref, count_ref
):
    z = place()[0]
    first = info[3].astype(F32)
    state = prefix[:HEAD_DIM]
    count = prefix[HEAD_DIM : HEAD_DIM + 1]
    for back, ref in enumerate((from1, from2, from3, from4), 1):
        one_state, doc, one_count = read_state(ref)
        chosen = jnp.where((doc == first) & (z >= back), 1.0, 0.0)
        state += one_state * chosen
        count += one_count * chosen
    count_ref[0] = jnp.max(count).astype(jnp.int32)
    high = state.astype(BF16)
    low = (state - high.astype(F32)).astype(BF16)
    in_first = lax.broadcasted_iota(jnp.int32, (PAIR, HEAD_DIM), 0) < info[6]
    squares = jnp.zeros((PAIR, HEAD_DIM), F32)
    for head in range(REPEAT):
        cols = slice(head * HEAD_DIM, (head + 1) * HEAD_DIM)
        queries = query[:, cols]
        earlier = jnp.dot(queries, high, preferred_element_type=F32) + jnp.dot(
            queries, low, preferred_element_type=F32
        )
        out = inside[:, cols] + jnp.where(in_first, earlier, 0.0)
        first_ref[:, cols] = out
        squares += out * out
    sums = row_sums(squares)
    for to in range(CORES * TP):
        sums_ref[to] = sums


def row_scale(sums):
    total = sums[0]
    for device in range(1, CORES * TP):
        total = total + sums[device]
    return lax.transpose(lax.rsqrt(total * (1.0 / WIDTH) + EPSILON), (1, 0))[:, :1]


TILE = 128
TILES = [(head, slice(at, at + TILE)) for head in range(REPEAT) for at in range(0, PAIR, TILE)]


def scores_of(queries, keys, head, part, rows):
    return lax.dot_general(
        queries[head, part],
        keys[rows, :HEAD_DIM],
        (((1,), (1,)), ((), ())),
        preferred_element_type=F32,
    )


def sweep(queries, kv, tops, acc, rows, visible=None):
    ahead = scores_of(queries, kv, *TILES[0], rows)
    for at, (head, part) in enumerate(TILES):
        scores = ahead
        if at + 1 < len(TILES):
            ahead = scores_of(queries, kv, *TILES[at + 1], rows)
        if visible is not None:
            scores = jnp.where(visible(part), scores, NEGATIVE)
        top = jnp.max(scores, axis=1, keepdims=True)
        old_top = tops[head, part]
        top = jnp.maximum(old_top, top)
        wide_top = jnp.concatenate([top] * (scores.shape[1] // HEAD_DIM), axis=1)
        weights = jnp.exp2((scores - wide_top) * SCALE)
        summed = jnp.dot(weights.astype(BF16), kv[rows, HEAD_DIM:], preferred_element_type=F32)
        tops[head, part] = top
        shrink = jnp.exp2((old_top - top) * SCALE)
        acc[head, part] = acc[head, part] * jnp.concatenate([shrink, shrink], axis=1) + summed


class Window:
    def __init__(self, prior, blocks, kv, bounds, sems):
        self.kv, self.bounds = kv, bounds
        used = jnp.int32(0)
        self.copies = []
        for at, (ref, distance) in enumerate(blocks):
            distance = jnp.int32(distance)
            needed = (distance >= 1) & (distance <= 16) & (prior > (distance - 1) * PAIR)
            slot = jnp.minimum(used, bounds.shape[0] - 1)
            rows = pl.ds(pl.multiple_of(slot * PAIR, PAIR), PAIR)
            copy = pltpu.make_async_copy(ref, kv.at[rows, pl.ds(0, 2 * HEAD_DIM)], sems.at[at])
            self.copies.append((needed, copy))

            @pl.when(needed)
            def _():
                copy.start()
                bounds[slot] = jnp.maximum(distance * PAIR - prior, 0)

            used = used + needed.astype(jnp.int32)
        self.steps = (used + CHUNK - 1) // CHUNK
        kv[:, 2 * HEAD_DIM :] = jnp.ones((kv.shape[0], HEAD_DIM), BF16)

        @pl.when(used % CHUNK != 0)
        def _():
            rows = pl.ds(pl.multiple_of(used * PAIR, PAIR), PAIR)
            kv[rows, : 2 * HEAD_DIM] = jnp.zeros((PAIR, 2 * HEAD_DIM), BF16)
            bounds[used] = jnp.int32(PAIR)

    def absorb(self, queries, tops, acc):
        for needed, copy in self.copies:
            pl.when(needed)(copy.wait)

        @pl.loop(0, self.steps)
        def _(step):
            rows = pl.ds(pl.multiple_of(step * CHUNK * PAIR, CHUNK * PAIR), CHUNK * PAIR)
            low0, low1 = self.bounds[step * CHUNK], self.bounds[step * CHUNK + 1]
            whole = (low0 == 0) & (low1 == 0)

            @pl.when(whole)
            def _():
                sweep(queries, self.kv, tops, acc, rows)

            @pl.when(jnp.logical_not(whole))
            def _():
                column = lax.broadcasted_iota(jnp.int32, (1, CHUNK * PAIR), 1)
                seen = column >= jnp.where(column < PAIR, low0, PAIR + low1)
                sweep(queries, self.kv, tops, acc, rows, lambda part: seen)


SLOTS = 10


def near_kernel(
    reach, sums, first, keep, queries_r, own1, own2, own3, own4, *refs
):
    others1, others2 = refs[:3], refs[3:6]
    queries, tops, acc, kv, scales, bounds, sems = refs[6:]
    _, x, core = place()
    blocks = [(own1, 4), (own2, 8), (own3, 12), (own4, 16)]
    for shift, other1, other2 in zip((1, 2, 3), others1, others2):
        wrapped = jnp.where(x < shift, 4, 0)
        blocks.append((other1, 4 + shift - wrapped))
        blocks.append((other2, 8 + shift - wrapped))
    window = Window(reach[0], blocks, kv, bounds, sems)
    tops[...] = jnp.full(tops.shape, NEGATIVE, F32)
    acc[...] = jnp.zeros(acc.shape, F32)
    scales[...] = jnp.broadcast_to(row_scale(sums), (PAIR, HEAD_DIM))
    for part, where in ((keep.at[1], rows_of(core)), (queries_r.at[1], rows_of(1 - core))):
        for head in range(REPEAT):
            cols = slice(head * HEAD_DIM, (head + 1) * HEAD_DIM)
            value = part[:, cols].astype(F32) + first[where, cols] * scales[where, :]
            queries[head, where, :] = value.astype(BF16)
    window.absorb(queries, tops, acc)


def far_kernel(info, reach, queries, old_tops, old_acc, own0, *refs):
    others3, others04 = refs[:3], refs[3:6]
    mine_ref, send_ref, sums_ref, tops, acc, kv, own, bounds, sems = refs[6:]
    _, x, core = place()
    blocks = []
    for shift, other3, other04 in zip((1, 2, 3), others3, others04):
        blocks.append((other3, 12 + shift - jnp.where(x < shift, 4, 0)))
        blocks.append((other04, jnp.where(x < shift, 12 + shift, shift)))
    window = Window(reach[0], blocks, kv, bounds, sems)
    own[:, : 2 * HEAD_DIM] = own0[...]
    own[:, 2 * HEAD_DIM :] = jnp.ones((PAIR, HEAD_DIM), BF16)
    window.absorb(queries, tops, acc)

    @pl.when(info[6] < PAIR)
    def _():
        in_first = lax.broadcasted_iota(jnp.int32, (PAIR, HEAD_DIM), 0) < info[6]
        for head in range(REPEAT):
            tops[head] = jnp.where(in_first, tops[head], NEGATIVE)
            acc[head] = jnp.where(jnp.concatenate([in_first, in_first], axis=1), acc[head], 0.0)

    def own_visible(part):
        row = lax.broadcasted_iota(jnp.int32, (TILE, PAIR), 0) + part.start
        column = lax.broadcasted_iota(jnp.int32, (TILE, PAIR), 1)
        return (column <= row) & (column >= document_start(info, row))

    sweep(queries, own, tops, acc, slice(0, PAIR), own_visible)
    for side in range(CORES):
        where = slice(side * TOK, (side + 1) * TOK)
        squares = jnp.zeros((TOK, HEAD_DIM), F32)
        outs = []
        for head in range(REPEAT):
            summed = acc[head, where, :]
            out = (summed[:, :HEAD_DIM] / summed[:, HEAD_DIM:]).astype(BF16)
            outs.append(out)
            widened = out.astype(F32)
            squares += widened * widened
        whole = jnp.concatenate(outs, axis=1)

        @pl.when(core == side)
        def _():
            mine_ref[...] = whole

        @pl.when(core != side)
        def _():
            send_ref[...] = whole

        sums = row_sums(squares)
        for to in range(TP):
            sums_ref[side * TP + to] = sums


def last_kernel(sums, mine, theirs, out_ref):
    core = place()[2]
    scale = row_scale(sums)
    for ref, side in ((mine, core), (theirs, 1 - core)):
        cols = pl.ds(pl.multiple_of(side * COLS, COLS), COLS)
        out_ref[:, cols] = (ref[...].astype(F32) * scale).astype(BF16)


CTX = ("z", "x", "core")


def move(value, z_shift=0, x_shift=0, core_shift=0, keep=lambda x: True):
    pairs = []
    for z in range(Z):
        for x in range(X):
            for core in range(CORES):
                to = ((z + z_shift) % Z * X + (x + x_shift) % X) * CORES
                if keep(x):
                    pairs.append(((z * X + x) * CORES + core, to + (core + core_shift) % CORES))
    return lax.ppermute(value, CTX, pairs)


def swap(value):
    return move(value, core_shift=1)


def exchange(sums):
    return lax.all_to_all(sums, ("core", "tp"), 0, 0, tiled=True)


def shape(dims, kind):
    return jax.ShapeDtypeStruct(dims, kind)


def shards(query_one, key_one, value_one, segments, query_base, key_two, value_two):
    core = lax.axis_index("core")

    def halves(arrays):
        low = jnp.stack([array[:, : array.shape[1] // 2] for array in arrays])
        high = jnp.stack([array[:, array.shape[1] // 2 :] for array in arrays])
        return jnp.where(core == 0, low, high), jnp.where(core == 0, high, low)

    segments_r = swap(segments)
    own_keep, own_send = halves((key_one, value_one, key_two, value_two))
    own0, packed, state, info = call(
        prep_kernel,
        (
            shape((PAIR, 2 * HEAD_DIM), BF16),
            shape((PAIR, 2 * HEAD_DIM), BF16),
            shape((144, HEAD_DIM), BF16),
            shape((8,), jnp.int32),
        ),
        [SMEM, SMEM, VMEM, VMEM],
        (VMEM,) * 3 + (SMEM,),
        name="prep",
    )(segments, segments_r, own_keep, swap(own_send))
    keep, query_send = halves((query_one, query_base))
    queries_r = swap(query_send)

    own1 = move(own0, z_shift=1)
    near = [move(state, x_shift=shift) for shift in (1, 2, 3)]
    prefix, plane, later1 = call(
        plane_kernel,
        (
            shape((HEAD_DIM + 8, HEAD_DIM), F32),
            shape((144, HEAD_DIM), BF16),
            shape((PAIR, 2 * HEAD_DIM), BF16),
        ),
        [SMEM] + [VMEM] * 6,
        (VMEM,) * 3,
        name="plane",
    )(info, state, *near, own1, queries_r)
    far = [move(plane, z_shift=back) for back in (1, 2, 3, 4)]

    def after(known, value):
        return jnp.where(known >= 0, value, jnp.zeros_like(value))

    own2 = move(later1, z_shift=1)
    own3 = move(own2, z_shift=1)
    own4 = move(own3, z_shift=1)

    inside, query = call(
        inside_kernel,
        (shape((PAIR, COLS), F32), shape((PAIR, COLS), BF16)),
        [SMEM] + [VMEM] * 3,
        (VMEM,) * 2,
        name="inside",
    )(info, keep, queries_r, packed)
    first, sums, reach = call(
        first_kernel,
        (
            shape((PAIR, COLS), F32),
            shape((CORES * TP, 8, PAIR), F32),
            shape((1,), jnp.int32),
        ),
        [SMEM] + [VMEM] * 7,
        (VMEM, VMEM, SMEM),
        name="first",
    )(info, prefix, *far, inside, query)


    all_sums = exchange(sums)
    x = lax.axis_index("x")
    x_shifts = (1, 2, 3)
    others = [move(after(reach[0], own1), x_shift=shift) for shift in x_shifts]
    others += [move(own2, x_shift=shift) for shift in x_shifts]
    others += [move(own3, x_shift=shift) for shift in x_shifts]
    late4 = after(all_sums[0, 0, 0], own4)
    others += [move(jnp.where(x + shift < X, own0, late4), x_shift=shift) for shift in x_shifts]
    queries, tops, acc = call(
        near_kernel,
        (
            shape((REPEAT, PAIR, HEAD_DIM), BF16),
            shape((REPEAT, PAIR, HEAD_DIM), F32),
            shape((REPEAT, PAIR, 2 * HEAD_DIM), F32),
        ),
        [SMEM] + [VMEM] * 14,
        (VMEM,) * 3,
        scratch=(
            pltpu.VMEM((SLOTS * PAIR, 3 * HEAD_DIM), BF16),
            pltpu.VMEM((PAIR, HEAD_DIM), F32),
            pltpu.SMEM((SLOTS,), jnp.int32),
            pltpu.SemaphoreType.DMA((10,)),
        ),
        name="near",
    )(
        reach, all_sums, first, keep, queries_r, own1, own2, own3, own4, *others[:6]
    )
    mine, send, out_sums, _, _ = call(
        far_kernel,
        (
            shape((TOK, COLS), BF16),
            shape((TOK, COLS), BF16),
            shape((CORES * TP, 8, TOK), F32),
            shape((REPEAT, PAIR, HEAD_DIM), F32),
            shape((REPEAT, PAIR, 2 * HEAD_DIM), F32),
        ),
        [SMEM, SMEM] + [VMEM] * 10,
        (VMEM,) * 5,
        scratch=(
            pltpu.VMEM((SLOTS * PAIR, 3 * HEAD_DIM), BF16),
            pltpu.VMEM((PAIR, 3 * HEAD_DIM), BF16),
            pltpu.SMEM((SLOTS,), jnp.int32),
            pltpu.SemaphoreType.DMA((10,)),
        ),
        aliases={3: 3, 4: 4},
        name="far",
    )(info, reach, queries, tops, acc, own0, *others[6:])
    theirs = swap(send)
    return call(
        last_kernel, shape((TOK, 2 * COLS), BF16), [VMEM] * 3, VMEM, name="last"
    )(exchange(out_sums), mine, theirs)


def solution(mesh):
    grid = Mesh(mesh.devices.reshape(Z, X, CORES, TP), ("z", "x", "core", "tp"))
    tokens, both = P(CTX), P(CTX, "tp")
    return jax.shard_map(
        shards,
        mesh=grid,
        in_specs=(both,) * 3 + (tokens,) + (both,) * 3,
        out_specs=both,
        check_vma=False,
    )
```

```python
import jax
import jax.numpy as jnp
from jax import lax
from jax.experimental import pallas as pl
from jax.experimental.pallas import tpu as pltpu
from jax.sharding import Mesh, PartitionSpec as P

HEAD_DIM = 128
WIDTH = 4096
EPSILON = 1e-05
NEGATIVE = -1e30

TOK = 192
PAIR = 384
REPEAT = 4
COLS = REPEAT * HEAD_DIM
Z, X, CORES, TP = 8, 4, 2, 4
CHUNK = 2
SCALE = HEAD_DIM ** (-0.5) * 1.4426950408889634

F32 = jnp.float32
BF16 = jnp.bfloat16
VMEM = pl.BlockSpec(memory_space=pltpu.VMEM)
SMEM = pl.BlockSpec(memory_space=pltpu.SMEM)
HBM = pl.BlockSpec(memory_space=pltpu.HBM)


def place():
    return lax.axis_index("z"), lax.axis_index("x"), lax.axis_index("core")


def call(kernel, outs, specs_in, specs_out, scratch=(), aliases=None, limit=16, name=None):
    return pl.pallas_call(
        kernel,
        out_shape=outs,
        in_specs=specs_in,
        out_specs=specs_out,
        scratch_shapes=list(scratch),
        input_output_aliases=aliases or {},
        compiler_params=pltpu.CompilerParams(vmem_limit_bytes=limit * 2**20),
        name=name,
    )


def count_below(ref, doc):
    found = jnp.int32(0)
    for step in (128, 64, 32, 16, 8, 4, 2, 1):
        tried = found + step
        last = ref[jnp.minimum(tried, TOK) - 1]
        found = jnp.where((tried <= TOK) & (last < doc), tried, found)
    return found


def half(core):
    return pl.ds(pl.multiple_of(core * HEAD_DIM, HEAD_DIM), HEAD_DIM)


def rows_of(core):
    return pl.ds(pl.multiple_of(core * TOK, 64), TOK)


def prep_kernel(seg, seg_r, own, other, own0_ref, first_ref, state_ref, info_ref):
    core = place()[2]
    for side, ref in ((core, own), (1 - core, other)):
        first_ref[rows_of(side), :HEAD_DIM] = ref[0]
        first_ref[rows_of(side), HEAD_DIM:] = ref[1]
        own0_ref[rows_of(side), :HEAD_DIM] = ref[2]
        own0_ref[rows_of(side), HEAD_DIM:] = ref[3]
    below = [count_below(seg, d) for d in (1, 2, 3)]
    below_r = [count_below(seg_r, d) for d in (1, 2, 3)]
    bounds = [a + b for a, b in zip(below, below_r)]
    first = jnp.where(core == 0, seg[0], seg_r[0])
    last = jnp.where(core == 0, seg_r[TOK - 1], seg[TOK - 1])

    def pick(values, doc):
        out = jnp.int32(0)
        for d in (1, 2, 3):
            out = jnp.where(doc == d, values[d - 1], out)
        return out

    count = PAIR - pick(bounds, last)
    first_end = jnp.where(first == 3, PAIR, pick(bounds, first + 1))
    for place_in, value in enumerate((*bounds, first, last, count, first_end, 0)):
        info_ref[place_in] = jnp.int32(value)
    rows = lax.broadcasted_iota(jnp.int32, (PAIR, HEAD_DIM), 0)
    masked = jnp.where(rows >= PAIR - count, first_ref[:, :HEAD_DIM].astype(F32), 0.0)
    state = lax.dot_general(
        masked.astype(BF16),
        first_ref[:, HEAD_DIM:],
        (((0,), (0,)), ((), ())),
        preferred_element_type=F32,
    )
    state_ref[:HEAD_DIM] = state.astype(BF16)
    state_ref[HEAD_DIM:] = notes(last.astype(F32), count.astype(F32)).astype(BF16)


def notes(last, count):
    row = lax.broadcasted_iota(jnp.int32, (16, HEAD_DIM), 0)
    high = jnp.floor(count * (1.0 / 64.0))
    return jnp.where(
        row == 0, last, jnp.where(row == 1, high, jnp.where(row == 2, count - 64.0 * high, 0.0))
    )


def read_state(ref):
    tail = ref[HEAD_DIM:].astype(F32)
    return ref[:HEAD_DIM].astype(F32), tail[0:1], tail[1:2] * 64.0 + tail[2:3]


def plane_kernel(
    info, own, from1, from2, from3, own1, queries_r, prefix_ref, plane_ref, later1_ref
):
    x = place()[1]
    later1_ref[...] = own1[...]
    first = info[3].astype(F32)
    items = [read_state(ref) for ref in (own, from1, from2, from3)]
    prefix = jnp.zeros((HEAD_DIM, HEAD_DIM), F32)
    prefix_count = jnp.zeros((1, HEAD_DIM), F32)
    for shift in (1, 2, 3):
        state, doc, count = items[shift]
        chosen = jnp.where((doc == first) & (x >= shift), 1.0, 0.0)
        prefix += state * chosen
        prefix_count += count * chosen
    prefix_ref[:HEAD_DIM] = prefix
    prefix_ref[HEAD_DIM:] = jnp.broadcast_to(prefix_count, (8, HEAD_DIM))
    last = items[0][1]
    for item in items[1:]:
        last = jnp.maximum(last, item[1])
    total = jnp.zeros((HEAD_DIM, HEAD_DIM), F32)
    total_count = jnp.zeros((1, HEAD_DIM), F32)
    for state, doc, count in items:
        chosen = jnp.where(doc == last, 1.0, 0.0)
        total += state * chosen
        total_count += count * chosen
    plane_ref[:HEAD_DIM] = total.astype(BF16)
    plane_ref[HEAD_DIM:] = notes(last, total_count).astype(BF16)


def document_start(info, rows):
    start = jnp.zeros_like(rows)
    for d in range(3):
        start = jnp.where(rows >= info[d], jnp.maximum(start, info[d]), start)
    return start


def split_dot(wide, narrow):
    high = wide.astype(BF16)
    low = (wide - high.astype(F32)).astype(BF16)
    return jnp.dot(high, narrow, preferred_element_type=F32) + jnp.dot(
        low, narrow, preferred_element_type=F32
    )


def inside_kernel(info, keep, queries_r, packed, inside_ref, query_ref):
    core = place()[2]
    query_ref[rows_of(core), :] = keep[0]
    query_ref[rows_of(1 - core), :] = queries_r[0]
    row = lax.broadcasted_iota(jnp.int32, (PAIR, PAIR), 0)
    column = lax.broadcasted_iota(jnp.int32, (PAIR, PAIR), 1)
    visible = (column <= row) & (column >= document_start(info, row))
    for head in range(REPEAT):
        cols = slice(head * HEAD_DIM, (head + 1) * HEAD_DIM)
        scores = lax.dot_general(
            query_ref[:, cols],
            packed[:, :HEAD_DIM],
            (((1,), (1,)), ((), ())),
            preferred_element_type=F32,
        )
        scores = jnp.where(visible, scores, 0.0)
        inside_ref[:, cols] = split_dot(scores, packed[:, HEAD_DIM:])


def row_sums(squares):
    high = squares.astype(BF16)
    low = (squares - high.astype(F32)).astype(BF16)
    ones = jnp.ones((8, squares.shape[1]), BF16)
    dims = (((1,), (1,)), ((), ()))
    return lax.dot_general(ones, high, dims, preferred_element_type=F32) + lax.dot_general(
        ones, low, dims, preferred_element_type=F32
    )


def first_kernel(
    info, prefix, from1, from2, from3, from4, inside, query, own1, own2,
    first_ref, sums_ref, count_ref, pair12_ref, later2_ref
):
    pair12_ref[:PAIR] = own1[...]
    pair12_ref[PAIR:] = own2[...]
    later2_ref[...] = own2[...]
    z = place()[0]
    first = info[3].astype(F32)
    state = prefix[:HEAD_DIM]
    count = prefix[HEAD_DIM : HEAD_DIM + 1]
    for back, ref in enumerate((from1, from2, from3, from4), 1):
        one_state, doc, one_count = read_state(ref)
        chosen = jnp.where((doc == first) & (z >= back), 1.0, 0.0)
        state += one_state * chosen
        count += one_count * chosen
    count_ref[0] = jnp.max(count).astype(jnp.int32)
    high = state.astype(BF16)
    low = (state - high.astype(F32)).astype(BF16)
    in_first = lax.broadcasted_iota(jnp.int32, (PAIR, HEAD_DIM), 0) < info[6]
    squares = jnp.zeros((PAIR, HEAD_DIM), F32)
    for head in range(REPEAT):
        cols = slice(head * HEAD_DIM, (head + 1) * HEAD_DIM)
        queries = query[:, cols]
        earlier = jnp.dot(queries, high, preferred_element_type=F32) + jnp.dot(
            queries, low, preferred_element_type=F32
        )
        out = inside[:, cols] + jnp.where(in_first, earlier, 0.0)
        first_ref[:, cols] = out
        squares += out * out
    sums = row_sums(squares)
    for to in range(CORES * TP):
        sums_ref[to] = sums


def row_scale(sums):
    total = sums[0]
    for device in range(1, CORES * TP):
        total = total + sums[device]
    return lax.transpose(lax.rsqrt(total * (1.0 / WIDTH) + EPSILON), (1, 0))[:, :1]


def payload_kernel(own0, own3, own4, *refs):
    x = place()[1]
    for shift, payload in enumerate(refs[4:], 1):
        payload[:PAIR] = own3[...]

        @pl.when(x + shift < X)
        def _():
            payload[PAIR:] = own0[...]

        @pl.when(x + shift >= X)
        def _():
            payload[PAIR:] = own4[...]


TILE = 128
TILES = [(head, slice(at, at + TILE)) for head in range(REPEAT) for at in range(0, PAIR, TILE)]


def scores_of(queries, keys, head, part, rows):
    return lax.dot_general(
        queries[head, part],
        keys[rows, :HEAD_DIM],
        (((1,), (1,)), ((), ())),
        preferred_element_type=F32,
    )


def sweep(queries, kv, tops, acc, rows, visible=None):
    ahead = scores_of(queries, kv, *TILES[0], rows)
    for at, (head, part) in enumerate(TILES):
        scores = ahead
        if at + 1 < len(TILES):
            ahead = scores_of(queries, kv, *TILES[at + 1], rows)
        if visible is not None:
            scores = jnp.where(visible(part), scores, NEGATIVE)
        top = jnp.max(scores, axis=1, keepdims=True)
        old_top = tops[head, part]
        top = jnp.maximum(old_top, top)
        wide_top = jnp.concatenate([top] * (scores.shape[1] // HEAD_DIM), axis=1)
        weights = jnp.exp2((scores - wide_top) * SCALE)
        summed = jnp.dot(weights.astype(BF16), kv[rows, HEAD_DIM:], preferred_element_type=F32)
        tops[head, part] = top
        shrink = jnp.exp2((old_top - top) * SCALE)
        acc[head, part] = acc[head, part] * jnp.concatenate([shrink, shrink], axis=1) + summed


class Window:
    def __init__(self, prior, blocks, kv, bounds, sems):
        self.kv, self.bounds = kv, bounds
        used = jnp.int32(0)
        self.copies = []
        for at, (ref, distance) in enumerate(blocks):
            distance = jnp.int32(distance)
            needed = (distance >= 1) & (distance <= 16) & (prior > (distance - 1) * PAIR)
            slot = jnp.minimum(used, bounds.shape[0] - 1)
            rows = pl.ds(pl.multiple_of(slot * PAIR, PAIR), PAIR)
            copy = pltpu.make_async_copy(ref, kv.at[rows, pl.ds(0, 2 * HEAD_DIM)], sems.at[at])
            self.copies.append((needed, copy))

            @pl.when(needed)
            def _():
                copy.start()
                bounds[slot] = jnp.maximum(distance * PAIR - prior, 0)

            used = used + needed.astype(jnp.int32)
        self.steps = (used + CHUNK - 1) // CHUNK
        kv[:, 2 * HEAD_DIM :] = jnp.ones((kv.shape[0], HEAD_DIM), BF16)

        @pl.when(used % CHUNK != 0)
        def _():
            rows = pl.ds(pl.multiple_of(used * PAIR, PAIR), PAIR)
            kv[rows, : 2 * HEAD_DIM] = jnp.zeros((PAIR, 2 * HEAD_DIM), BF16)
            bounds[used] = jnp.int32(PAIR)

    def absorb(self, queries, tops, acc):
        for needed, copy in self.copies:
            pl.when(needed)(copy.wait)

        @pl.loop(0, self.steps)
        def _(step):
            rows = pl.ds(pl.multiple_of(step * CHUNK * PAIR, CHUNK * PAIR), CHUNK * PAIR)
            low0, low1 = self.bounds[step * CHUNK], self.bounds[step * CHUNK + 1]
            whole = (low0 == 0) & (low1 == 0)

            @pl.when(whole)
            def _():
                sweep(queries, self.kv, tops, acc, rows)

            @pl.when(jnp.logical_not(whole))
            def _():
                column = lax.broadcasted_iota(jnp.int32, (1, CHUNK * PAIR), 1)
                seen = column >= jnp.where(column < PAIR, low0, PAIR + low1)
                sweep(queries, self.kv, tops, acc, rows, lambda part: seen)


SLOTS = 10


def near_kernel(
    reach, sums, first, keep, queries_r, own1, own2, own3, own4, *refs
):
    others = refs[:3]
    queries, tops, acc, kv, scales, bounds, sems = refs[3:]
    _, x, core = place()
    blocks = [(own1, 4), (own2, 8), (own3, 12), (own4, 16)]
    for shift, other in enumerate(others, 1):
        wrapped = jnp.where(x < shift, 4, 0)
        blocks.append((other.at[pl.ds(0, PAIR)], 4 + shift - wrapped))
        blocks.append((other.at[pl.ds(PAIR, PAIR)], 8 + shift - wrapped))
    window = Window(reach[0], blocks, kv, bounds, sems)
    tops[...] = jnp.full(tops.shape, NEGATIVE, F32)
    acc[...] = jnp.zeros(acc.shape, F32)
    scales[...] = jnp.broadcast_to(row_scale(sums), (PAIR, HEAD_DIM))
    for part, where in ((keep.at[1], rows_of(core)), (queries_r.at[1], rows_of(1 - core))):
        for head in range(REPEAT):
            cols = slice(head * HEAD_DIM, (head + 1) * HEAD_DIM)
            value = part[:, cols].astype(F32) + first[where, cols] * scales[where, :]
            queries[head, where, :] = value.astype(BF16)
    window.absorb(queries, tops, acc)


def far_kernel(info, reach, queries, old_tops, old_acc, own0, *refs):
    others = refs[:3]
    mine_ref, send_ref, sums_ref, tops, acc, kv, own, bounds, sems = refs[3:]
    _, x, core = place()
    blocks = []
    for shift, other in enumerate(others, 1):
        wrapped = x < shift
        blocks.append((other.at[pl.ds(0, PAIR)], 12 + shift - jnp.where(wrapped, 4, 0)))
        blocks.append((other.at[pl.ds(PAIR, PAIR)], shift + jnp.where(wrapped, 12, 0)))
    window = Window(reach[0], blocks, kv, bounds, sems)
    own[:, : 2 * HEAD_DIM] = own0[...]
    own[:, 2 * HEAD_DIM :] = jnp.ones((PAIR, HEAD_DIM), BF16)
    window.absorb(queries, tops, acc)

    @pl.when(info[6] < PAIR)
    def _():
        in_first = lax.broadcasted_iota(jnp.int32, (PAIR, HEAD_DIM), 0) < info[6]
        for head in range(REPEAT):
            tops[head] = jnp.where(in_first, tops[head], NEGATIVE)
            acc[head] = jnp.where(jnp.concatenate([in_first, in_first], axis=1), acc[head], 0.0)

    def own_visible(part):
        row = lax.broadcasted_iota(jnp.int32, (TILE, PAIR), 0) + part.start
        column = lax.broadcasted_iota(jnp.int32, (TILE, PAIR), 1)
        return (column <= row) & (column >= document_start(info, row))

    sweep(queries, own, tops, acc, slice(0, PAIR), own_visible)
    for side in range(CORES):
        where = slice(side * TOK, (side + 1) * TOK)
        squares = jnp.zeros((TOK, HEAD_DIM), F32)
        outs = []
        for head in range(REPEAT):
            summed = acc[head, where, :]
            out = (summed[:, :HEAD_DIM] / summed[:, HEAD_DIM:]).astype(BF16)
            outs.append(out)
            widened = out.astype(F32)
            squares += widened * widened
        whole = jnp.concatenate(outs, axis=1)

        @pl.when(core == side)
        def _():
            mine_ref[...] = whole

        @pl.when(core != side)
        def _():
            send_ref[...] = whole

        sums = row_sums(squares)
        for to in range(TP):
            sums_ref[side * TP + to] = sums


def last_kernel(sums, mine, theirs, out_ref):
    core = place()[2]
    scale = row_scale(sums)
    for ref, side in ((mine, core), (theirs, 1 - core)):
        cols = pl.ds(pl.multiple_of(side * COLS, COLS), COLS)
        out_ref[:, cols] = (ref[...].astype(F32) * scale).astype(BF16)


CTX = ("z", "x", "core")


def move(value, z_shift=0, x_shift=0, core_shift=0, keep=lambda x: True):
    pairs = []
    for z in range(Z):
        for x in range(X):
            for core in range(CORES):
                to = ((z + z_shift) % Z * X + (x + x_shift) % X) * CORES
                if keep(x):
                    pairs.append(((z * X + x) * CORES + core, to + (core + core_shift) % CORES))
    return lax.ppermute(value, CTX, pairs)


def swap(value):
    return move(value, core_shift=1)


def exchange(sums):
    return lax.all_to_all(sums, ("core", "tp"), 0, 0, tiled=True)


def shape(dims, kind):
    return jax.ShapeDtypeStruct(dims, kind)


def shards(query_one, key_one, value_one, segments, query_base, key_two, value_two):
    core = lax.axis_index("core")

    def halves(arrays):
        low = jnp.stack([array[:, : array.shape[1] // 2] for array in arrays])
        high = jnp.stack([array[:, array.shape[1] // 2 :] for array in arrays])
        return jnp.where(core == 0, low, high), jnp.where(core == 0, high, low)

    segments_r = swap(segments)
    own_keep, own_send = halves((key_one, value_one, key_two, value_two))
    own0, packed, state, info = call(
        prep_kernel,
        (
            shape((PAIR, 2 * HEAD_DIM), BF16),
            shape((PAIR, 2 * HEAD_DIM), BF16),
            shape((144, HEAD_DIM), BF16),
            shape((8,), jnp.int32),
        ),
        [SMEM, SMEM, VMEM, VMEM],
        (VMEM,) * 3 + (SMEM,),
        name="prep",
    )(segments, segments_r, own_keep, swap(own_send))
    keep, query_send = halves((query_one, query_base))
    queries_r = swap(query_send)

    own1 = move(own0, z_shift=1)
    near = [move(state, x_shift=shift) for shift in (1, 2, 3)]
    prefix, plane, later1 = call(
        plane_kernel,
        (
            shape((HEAD_DIM + 8, HEAD_DIM), F32),
            shape((144, HEAD_DIM), BF16),
            shape((PAIR, 2 * HEAD_DIM), BF16),
        ),
        [SMEM] + [VMEM] * 6,
        (VMEM,) * 3,
        name="plane",
    )(info, state, *near, own1, queries_r)
    far = [move(plane, z_shift=back) for back in (1, 2, 3, 4)]

    own2 = move(later1, z_shift=1)

    inside, query = call(
        inside_kernel,
        (shape((PAIR, COLS), F32), shape((PAIR, COLS), BF16)),
        [SMEM] + [VMEM] * 3,
        (VMEM,) * 2,
        name="inside",
    )(info, keep, queries_r, packed)
    first, sums, reach, pair12, later2 = call(
        first_kernel,
        (
            shape((PAIR, COLS), F32),
            shape((CORES * TP, 8, PAIR), F32),
            shape((1,), jnp.int32),
            shape((2 * PAIR, 2 * HEAD_DIM), BF16),
            shape((PAIR, 2 * HEAD_DIM), BF16),
        ),
        [SMEM] + [VMEM] * 9,
        (VMEM, VMEM, SMEM, VMEM, VMEM),
        name="first",
    )(info, prefix, *far, inside, query, own1, own2)
    own3 = move(later2, z_shift=1)
    own4 = move(own3, z_shift=1)


    all_sums = exchange(sums)
    x_shifts = (1, 2, 3)
    others12 = [move(pair12, x_shift=shift) for shift in x_shifts]
    payloads34 = call(
        payload_kernel,
        (shape((2 * PAIR, 2 * HEAD_DIM), BF16),) * 3,
        [VMEM] * 7,
        (VMEM,) * 3,
        name="payload",
    )(own0, own3, own4, *others12, all_sums)
    others34 = [move(value, x_shift=shift) for shift, value in zip(x_shifts, payloads34)]
    queries, tops, acc = call(
        near_kernel,
        (
            shape((REPEAT, PAIR, HEAD_DIM), BF16),
            shape((REPEAT, PAIR, HEAD_DIM), F32),
            shape((REPEAT, PAIR, 2 * HEAD_DIM), F32),
        ),
        [SMEM] + [VMEM] * 11,
        (VMEM,) * 3,
        scratch=(
            pltpu.VMEM((SLOTS * PAIR, 3 * HEAD_DIM), BF16),
            pltpu.VMEM((PAIR, HEAD_DIM), F32),
            pltpu.SMEM((SLOTS,), jnp.int32),
            pltpu.SemaphoreType.DMA((10,)),
        ),
        name="near",
    )(
        reach, all_sums, first, keep, queries_r, own1, own2, own3, own4, *others12
    )
    mine, send, out_sums, _, _ = call(
        far_kernel,
        (
            shape((TOK, COLS), BF16),
            shape((TOK, COLS), BF16),
            shape((CORES * TP, 8, TOK), F32),
            shape((REPEAT, PAIR, HEAD_DIM), F32),
            shape((REPEAT, PAIR, 2 * HEAD_DIM), F32),
        ),
        [SMEM, SMEM] + [VMEM] * 7,
        (VMEM,) * 5,
        scratch=(
            pltpu.VMEM((SLOTS * PAIR, 3 * HEAD_DIM), BF16),
            pltpu.VMEM((PAIR, 3 * HEAD_DIM), BF16),
            pltpu.SMEM((SLOTS,), jnp.int32),
            pltpu.SemaphoreType.DMA((10,)),
        ),
        aliases={3: 3, 4: 4},
        name="far",
    )(info, reach, queries, tops, acc, own0, *others34)
    theirs = swap(send)
    return call(
        last_kernel, shape((TOK, 2 * COLS), BF16), [VMEM] * 3, VMEM, name="last"
    )(exchange(out_sums), mine, theirs)


def solution(mesh):
    grid = Mesh(mesh.devices.reshape(Z, X, CORES, TP), ("z", "x", "core", "tp"))
    tokens, both = P(CTX), P(CTX, "tp")
    return jax.shard_map(
        shards,
        mesh=grid,
        in_specs=(both,) * 3 + (tokens,) + (both,) * 3,
        out_specs=both,
        check_vma=False,
    )
```

```python
import jax
import jax.numpy as jnp
from jax import lax
from jax.experimental import pallas as pl
from jax.experimental.pallas import tpu as pltpu
from jax.sharding import Mesh, PartitionSpec as P

HEAD_DIM = 128
WIDTH = 4096
EPSILON = 1e-05
NEGATIVE = -1e30

TOK = 192
PAIR = 384
REPEAT = 4
COLS = REPEAT * HEAD_DIM
Z, X, CORES, TP = 8, 4, 2, 4
CHUNK = 2
SCALE = HEAD_DIM ** (-0.5) * 1.4426950408889634

F32 = jnp.float32
BF16 = jnp.bfloat16
VMEM = pl.BlockSpec(memory_space=pltpu.VMEM)
SMEM = pl.BlockSpec(memory_space=pltpu.SMEM)
HBM = pl.BlockSpec(memory_space=pltpu.HBM)


def place():
    return lax.axis_index("z"), lax.axis_index("x"), lax.axis_index("core")


def call(kernel, outs, specs_in, specs_out, scratch=(), aliases=None, limit=16, name=None):
    return pl.pallas_call(
        kernel,
        out_shape=outs,
        in_specs=specs_in,
        out_specs=specs_out,
        scratch_shapes=list(scratch),
        input_output_aliases=aliases or {},
        compiler_params=pltpu.CompilerParams(vmem_limit_bytes=limit * 2**20),
        name=name,
    )


def count_below(ref, doc):
    found = jnp.int32(0)
    for step in (128, 64, 32, 16, 8, 4, 2, 1):
        tried = found + step
        last = ref[jnp.minimum(tried, TOK) - 1]
        found = jnp.where((tried <= TOK) & (last < doc), tried, found)
    return found


def half(core):
    return pl.ds(pl.multiple_of(core * HEAD_DIM, HEAD_DIM), HEAD_DIM)


def rows_of(core):
    return pl.ds(pl.multiple_of(core * TOK, 64), TOK)


def prep_kernel(seg, seg_r, own, other, own0_ref, first_ref, state_ref, info_ref):
    core = place()[2]
    for side, ref in ((core, own), (1 - core, other)):
        first_ref[rows_of(side), :HEAD_DIM] = ref[0]
        first_ref[rows_of(side), HEAD_DIM:] = ref[1]
        own0_ref[rows_of(side), :HEAD_DIM] = ref[2]
        own0_ref[rows_of(side), HEAD_DIM:] = ref[3]
    below = [count_below(seg, d) for d in (1, 2, 3)]
    below_r = [count_below(seg_r, d) for d in (1, 2, 3)]
    bounds = [a + b for a, b in zip(below, below_r)]
    first = jnp.where(core == 0, seg[0], seg_r[0])
    last = jnp.where(core == 0, seg_r[TOK - 1], seg[TOK - 1])

    def pick(values, doc):
        out = jnp.int32(0)
        for d in (1, 2, 3):
            out = jnp.where(doc == d, values[d - 1], out)
        return out

    count = PAIR - pick(bounds, last)
    first_end = jnp.where(first == 3, PAIR, pick(bounds, first + 1))
    for place_in, value in enumerate((*bounds, first, last, count, first_end, 0)):
        info_ref[place_in] = jnp.int32(value)
    rows = lax.broadcasted_iota(jnp.int32, (PAIR, HEAD_DIM), 0)
    masked = jnp.where(rows >= PAIR - count, first_ref[:, :HEAD_DIM].astype(F32), 0.0)
    state = lax.dot_general(
        masked.astype(BF16),
        first_ref[:, HEAD_DIM:],
        (((0,), (0,)), ((), ())),
        preferred_element_type=F32,
    )
    state_ref[:HEAD_DIM] = state.astype(BF16)
    state_ref[HEAD_DIM:] = notes(last.astype(F32), count.astype(F32)).astype(BF16)


def notes(last, count):
    row = lax.broadcasted_iota(jnp.int32, (16, HEAD_DIM), 0)
    high = jnp.floor(count * (1.0 / 64.0))
    return jnp.where(
        row == 0, last, jnp.where(row == 1, high, jnp.where(row == 2, count - 64.0 * high, 0.0))
    )


def read_state(ref):
    tail = ref[HEAD_DIM:].astype(F32)
    return ref[:HEAD_DIM].astype(F32), tail[0:1], tail[1:2] * 64.0 + tail[2:3]


def plane_kernel(
    info, own, from1, from2, from3, own1, queries_r, prefix_ref, plane_ref, later1_ref
):
    x = place()[1]
    later1_ref[...] = own1[...]
    first = info[3].astype(F32)
    items = [read_state(ref) for ref in (own, from1, from2, from3)]
    prefix = jnp.zeros((HEAD_DIM, HEAD_DIM), F32)
    prefix_count = jnp.zeros((1, HEAD_DIM), F32)
    for shift in (1, 2, 3):
        state, doc, count = items[shift]
        chosen = jnp.where((doc == first) & (x >= shift), 1.0, 0.0)
        prefix += state * chosen
        prefix_count += count * chosen
    prefix_ref[:HEAD_DIM] = prefix
    prefix_ref[HEAD_DIM:] = jnp.broadcast_to(prefix_count, (8, HEAD_DIM))
    last = items[0][1]
    for item in items[1:]:
        last = jnp.maximum(last, item[1])
    total = jnp.zeros((HEAD_DIM, HEAD_DIM), F32)
    total_count = jnp.zeros((1, HEAD_DIM), F32)
    for state, doc, count in items:
        chosen = jnp.where(doc == last, 1.0, 0.0)
        total += state * chosen
        total_count += count * chosen
    plane_ref[:HEAD_DIM] = total.astype(BF16)
    plane_ref[HEAD_DIM:] = notes(last, total_count).astype(BF16)


def document_start(info, rows):
    start = jnp.zeros_like(rows)
    for d in range(3):
        start = jnp.where(rows >= info[d], jnp.maximum(start, info[d]), start)
    return start


def split_dot(wide, narrow):
    high = wide.astype(BF16)
    low = (wide - high.astype(F32)).astype(BF16)
    return jnp.dot(high, narrow, preferred_element_type=F32) + jnp.dot(
        low, narrow, preferred_element_type=F32
    )


def inside_kernel(info, keep, queries_r, packed, inside_ref, query_ref):
    core = place()[2]
    query_ref[rows_of(core), :] = keep[0]
    query_ref[rows_of(1 - core), :] = queries_r[0]
    row = lax.broadcasted_iota(jnp.int32, (PAIR, PAIR), 0)
    column = lax.broadcasted_iota(jnp.int32, (PAIR, PAIR), 1)
    visible = (column <= row) & (column >= document_start(info, row))
    for head in range(REPEAT):
        cols = slice(head * HEAD_DIM, (head + 1) * HEAD_DIM)
        scores = lax.dot_general(
            query_ref[:, cols],
            packed[:, :HEAD_DIM],
            (((1,), (1,)), ((), ())),
            preferred_element_type=F32,
        )
        scores = jnp.where(visible, scores, 0.0)
        inside_ref[:, cols] = split_dot(scores, packed[:, HEAD_DIM:])


def row_sums(squares):
    high = squares.astype(BF16)
    low = (squares - high.astype(F32)).astype(BF16)
    ones = jnp.ones((8, squares.shape[1]), BF16)
    dims = (((1,), (1,)), ((), ()))
    return lax.dot_general(ones, high, dims, preferred_element_type=F32) + lax.dot_general(
        ones, low, dims, preferred_element_type=F32
    )


def first_kernel(
    info, prefix, from1, from2, from3, from4, inside, query, own1, own2,
    first_ref, sums_ref, count_ref, pair12_ref, later2_ref
):
    pair12_ref[:PAIR] = own1[...]
    pair12_ref[PAIR:] = own2[...]
    later2_ref[...] = own2[...]
    z = place()[0]
    first = info[3].astype(F32)
    state = prefix[:HEAD_DIM]
    count = prefix[HEAD_DIM : HEAD_DIM + 1]
    for back, ref in enumerate((from1, from2, from3, from4), 1):
        one_state, doc, one_count = read_state(ref)
        chosen = jnp.where((doc == first) & (z >= back), 1.0, 0.0)
        state += one_state * chosen
        count += one_count * chosen
    count_ref[0] = jnp.max(count).astype(jnp.int32)
    high = state.astype(BF16)
    low = (state - high.astype(F32)).astype(BF16)
    in_first = lax.broadcasted_iota(jnp.int32, (PAIR, HEAD_DIM), 0) < info[6]
    squares = jnp.zeros((PAIR, HEAD_DIM), F32)
    for head in range(REPEAT):
        cols = slice(head * HEAD_DIM, (head + 1) * HEAD_DIM)
        queries = query[:, cols]
        earlier = jnp.dot(queries, high, preferred_element_type=F32) + jnp.dot(
            queries, low, preferred_element_type=F32
        )
        out = inside[:, cols] + jnp.where(in_first, earlier, 0.0)
        first_ref[:, cols] = out
        squares += out * out
    sums = row_sums(squares)
    for to in range(CORES * TP):
        sums_ref[to] = sums


def row_scale(sums):
    total = sums[0]
    for device in range(1, CORES * TP):
        total = total + sums[device]
    return lax.transpose(lax.rsqrt(total * (1.0 / WIDTH) + EPSILON), (1, 0))[:, :1]


def payload_kernel(own0, own3, own4, *payloads):
    x = place()[1]
    for shift, payload in enumerate(payloads, 1):
        payload[:PAIR] = own3[...]

        @pl.when(x + shift < X)
        def _():
            payload[PAIR:] = own0[...]

        @pl.when(x + shift >= X)
        def _():
            payload[PAIR:] = own4[...]


TILE = 128
TILES = [(head, slice(at, at + TILE)) for head in range(REPEAT) for at in range(0, PAIR, TILE)]


def scores_of(queries, keys, head, part, rows):
    return lax.dot_general(
        queries[head, part],
        keys[rows, :HEAD_DIM],
        (((1,), (1,)), ((), ())),
        preferred_element_type=F32,
    )


def sweep(queries, kv, tops, acc, rows, visible=None):
    ahead = scores_of(queries, kv, *TILES[0], rows)
    for at, (head, part) in enumerate(TILES):
        scores = ahead
        if at + 1 < len(TILES):
            ahead = scores_of(queries, kv, *TILES[at + 1], rows)
        if visible is not None:
            scores = jnp.where(visible(part), scores, NEGATIVE)
        top = jnp.max(scores, axis=1, keepdims=True)
        old_top = tops[head, part]
        top = jnp.maximum(old_top, top)
        wide_top = jnp.concatenate([top] * (scores.shape[1] // HEAD_DIM), axis=1)
        weights = jnp.exp2((scores - wide_top) * SCALE)
        summed = jnp.dot(weights.astype(BF16), kv[rows, HEAD_DIM:], preferred_element_type=F32)
        tops[head, part] = top
        shrink = jnp.exp2((old_top - top) * SCALE)
        acc[head, part] = acc[head, part] * jnp.concatenate([shrink, shrink], axis=1) + summed


class Window:
    def __init__(self, prior, blocks, kv, bounds, sems):
        self.kv, self.bounds = kv, bounds
        used = jnp.int32(0)
        self.copies = []
        for at, (ref, distance) in enumerate(blocks):
            distance = jnp.int32(distance)
            needed = (distance >= 1) & (distance <= 16) & (prior > (distance - 1) * PAIR)
            slot = jnp.minimum(used, bounds.shape[0] - 1)
            rows = pl.ds(pl.multiple_of(slot * PAIR, PAIR), PAIR)
            copy = pltpu.make_async_copy(ref, kv.at[rows, pl.ds(0, 2 * HEAD_DIM)], sems.at[at])
            self.copies.append((needed, copy))

            @pl.when(needed)
            def _():
                copy.start()
                bounds[slot] = jnp.maximum(distance * PAIR - prior, 0)

            used = used + needed.astype(jnp.int32)
        self.steps = (used + CHUNK - 1) // CHUNK
        kv[:, 2 * HEAD_DIM :] = jnp.ones((kv.shape[0], HEAD_DIM), BF16)

        @pl.when(used % CHUNK != 0)
        def _():
            rows = pl.ds(pl.multiple_of(used * PAIR, PAIR), PAIR)
            kv[rows, : 2 * HEAD_DIM] = jnp.zeros((PAIR, 2 * HEAD_DIM), BF16)
            bounds[used] = jnp.int32(PAIR)

    def absorb(self, queries, tops, acc):
        for needed, copy in self.copies:
            pl.when(needed)(copy.wait)

        @pl.loop(0, self.steps)
        def _(step):
            rows = pl.ds(pl.multiple_of(step * CHUNK * PAIR, CHUNK * PAIR), CHUNK * PAIR)
            low0, low1 = self.bounds[step * CHUNK], self.bounds[step * CHUNK + 1]
            whole = (low0 == 0) & (low1 == 0)

            @pl.when(whole)
            def _():
                sweep(queries, self.kv, tops, acc, rows)

            @pl.when(jnp.logical_not(whole))
            def _():
                column = lax.broadcasted_iota(jnp.int32, (1, CHUNK * PAIR), 1)
                seen = column >= jnp.where(column < PAIR, low0, PAIR + low1)
                sweep(queries, self.kv, tops, acc, rows, lambda part: seen)


SLOTS = 10


def near_kernel(
    reach, sums, first, keep, queries_r, own1, own2, own3, own4, *refs
):
    others = refs[:3]
    queries, tops, acc, kv, scales, bounds, sems = refs[3:]
    _, x, core = place()
    blocks = [(own1, 4), (own2, 8), (own3, 12), (own4, 16)]
    for shift, other in enumerate(others, 1):
        wrapped = jnp.where(x < shift, 4, 0)
        blocks.append((other.at[pl.ds(0, PAIR)], 4 + shift - wrapped))
        blocks.append((other.at[pl.ds(PAIR, PAIR)], 8 + shift - wrapped))
    window = Window(reach[0], blocks, kv, bounds, sems)
    tops[...] = jnp.full(tops.shape, NEGATIVE, F32)
    acc[...] = jnp.zeros(acc.shape, F32)
    scales[...] = jnp.broadcast_to(row_scale(sums), (PAIR, HEAD_DIM))
    for part, where in ((keep.at[1], rows_of(core)), (queries_r.at[1], rows_of(1 - core))):
        for head in range(REPEAT):
            cols = slice(head * HEAD_DIM, (head + 1) * HEAD_DIM)
            value = part[:, cols].astype(F32) + first[where, cols] * scales[where, :]
            queries[head, where, :] = value.astype(BF16)
    window.absorb(queries, tops, acc)


def far_kernel(info, reach, queries, old_tops, old_acc, own0, *refs):
    others = refs[:3]
    mine_ref, send_ref, sums_ref, tops, acc, kv, own, bounds, sems = refs[3:]
    _, x, core = place()
    blocks = []
    for shift, other in enumerate(others, 1):
        wrapped = x < shift
        blocks.append((other.at[pl.ds(0, PAIR)], 12 + shift - jnp.where(wrapped, 4, 0)))
        blocks.append((other.at[pl.ds(PAIR, PAIR)], shift + jnp.where(wrapped, 12, 0)))
    window = Window(reach[0], blocks, kv, bounds, sems)
    own[:, : 2 * HEAD_DIM] = own0[...]
    own[:, 2 * HEAD_DIM :] = jnp.ones((PAIR, HEAD_DIM), BF16)
    window.absorb(queries, tops, acc)

    @pl.when(info[6] < PAIR)
    def _():
        in_first = lax.broadcasted_iota(jnp.int32, (PAIR, HEAD_DIM), 0) < info[6]
        for head in range(REPEAT):
            tops[head] = jnp.where(in_first, tops[head], NEGATIVE)
            acc[head] = jnp.where(jnp.concatenate([in_first, in_first], axis=1), acc[head], 0.0)

    def own_visible(part):
        row = lax.broadcasted_iota(jnp.int32, (TILE, PAIR), 0) + part.start
        column = lax.broadcasted_iota(jnp.int32, (TILE, PAIR), 1)
        return (column <= row) & (column >= document_start(info, row))

    sweep(queries, own, tops, acc, slice(0, PAIR), own_visible)
    for side in range(CORES):
        where = slice(side * TOK, (side + 1) * TOK)
        squares = jnp.zeros((TOK, HEAD_DIM), F32)
        outs = []
        for head in range(REPEAT):
            summed = acc[head, where, :]
            out = (summed[:, :HEAD_DIM] / summed[:, HEAD_DIM:]).astype(BF16)
            outs.append(out)
            widened = out.astype(F32)
            squares += widened * widened
        whole = jnp.concatenate(outs, axis=1)

        @pl.when(core == side)
        def _():
            mine_ref[...] = whole

        @pl.when(core != side)
        def _():
            send_ref[...] = whole

        sums = row_sums(squares)
        for to in range(TP):
            sums_ref[side * TP + to] = sums


def last_kernel(sums, mine, theirs, out_ref):
    core = place()[2]
    scale = row_scale(sums)
    for ref, side in ((mine, core), (theirs, 1 - core)):
        cols = pl.ds(pl.multiple_of(side * COLS, COLS), COLS)
        out_ref[:, cols] = (ref[...].astype(F32) * scale).astype(BF16)


CTX = ("z", "x", "core")


def move(value, z_shift=0, x_shift=0, core_shift=0, keep=lambda x: True):
    pairs = []
    for z in range(Z):
        for x in range(X):
            for core in range(CORES):
                to = ((z + z_shift) % Z * X + (x + x_shift) % X) * CORES
                if keep(x):
                    pairs.append(((z * X + x) * CORES + core, to + (core + core_shift) % CORES))
    return lax.ppermute(value, CTX, pairs)


def swap(value):
    return move(value, core_shift=1)


def exchange(sums):
    return lax.all_to_all(sums, ("core", "tp"), 0, 0, tiled=True)


def shape(dims, kind):
    return jax.ShapeDtypeStruct(dims, kind)


def shards(query_one, key_one, value_one, segments, query_base, key_two, value_two):
    core = lax.axis_index("core")

    def halves(arrays):
        low = jnp.stack([array[:, : array.shape[1] // 2] for array in arrays])
        high = jnp.stack([array[:, array.shape[1] // 2 :] for array in arrays])
        return jnp.where(core == 0, low, high), jnp.where(core == 0, high, low)

    segments_r = swap(segments)
    own_keep, own_send = halves((key_one, value_one, key_two, value_two))
    own0, packed, state, info = call(
        prep_kernel,
        (
            shape((PAIR, 2 * HEAD_DIM), BF16),
            shape((PAIR, 2 * HEAD_DIM), BF16),
            shape((144, HEAD_DIM), BF16),
            shape((8,), jnp.int32),
        ),
        [SMEM, SMEM, VMEM, VMEM],
        (VMEM,) * 3 + (SMEM,),
        name="prep",
    )(segments, segments_r, own_keep, swap(own_send))
    keep, query_send = halves((query_one, query_base))
    queries_r = swap(query_send)

    own1 = move(own0, z_shift=1)
    near = [move(state, x_shift=shift) for shift in (1, 2, 3)]
    prefix, plane, later1 = call(
        plane_kernel,
        (
            shape((HEAD_DIM + 8, HEAD_DIM), F32),
            shape((144, HEAD_DIM), BF16),
            shape((PAIR, 2 * HEAD_DIM), BF16),
        ),
        [SMEM] + [VMEM] * 6,
        (VMEM,) * 3,
        name="plane",
    )(info, state, *near, own1, queries_r)
    far = [move(plane, z_shift=back) for back in (1, 2, 3, 4)]

    own2 = move(later1, z_shift=1)

    inside, query = call(
        inside_kernel,
        (shape((PAIR, COLS), F32), shape((PAIR, COLS), BF16)),
        [SMEM] + [VMEM] * 3,
        (VMEM,) * 2,
        name="inside",
    )(info, keep, queries_r, packed)
    first, sums, reach, pair12, later2 = call(
        first_kernel,
        (
            shape((PAIR, COLS), F32),
            shape((CORES * TP, 8, PAIR), F32),
            shape((1,), jnp.int32),
            shape((2 * PAIR, 2 * HEAD_DIM), BF16),
            shape((PAIR, 2 * HEAD_DIM), BF16),
        ),
        [SMEM] + [VMEM] * 9,
        (VMEM, VMEM, SMEM, VMEM, VMEM),
        name="first",
    )(info, prefix, *far, inside, query, own1, own2)
    own3 = move(later2, z_shift=1)
    own4 = move(own3, z_shift=1)


    all_sums = exchange(sums)
    x_shifts = (1, 2, 3)
    others12 = [move(pair12, x_shift=shift) for shift in x_shifts]
    payloads34 = call(
        payload_kernel,
        (shape((2 * PAIR, 2 * HEAD_DIM), BF16),) * 3,
        [VMEM] * 3,
        (VMEM,) * 3,
        name="payload",
    )(own0, own3, own4)
    others34 = [move(value, x_shift=shift) for shift, value in zip(x_shifts, payloads34)]
    queries, tops, acc = call(
        near_kernel,
        (
            shape((REPEAT, PAIR, HEAD_DIM), BF16),
            shape((REPEAT, PAIR, HEAD_DIM), F32),
            shape((REPEAT, PAIR, 2 * HEAD_DIM), F32),
        ),
        [SMEM] + [VMEM] * 11,
        (VMEM,) * 3,
        scratch=(
            pltpu.VMEM((SLOTS * PAIR, 3 * HEAD_DIM), BF16),
            pltpu.VMEM((PAIR, HEAD_DIM), F32),
            pltpu.SMEM((SLOTS,), jnp.int32),
            pltpu.SemaphoreType.DMA((10,)),
        ),
        name="near",
    )(
        reach, all_sums, first, keep, queries_r, own1, own2, own3, own4, *others12
    )
    mine, send, out_sums, _, _ = call(
        far_kernel,
        (
            shape((TOK, COLS), BF16),
            shape((TOK, COLS), BF16),
            shape((CORES * TP, 8, TOK), F32),
            shape((REPEAT, PAIR, HEAD_DIM), F32),
            shape((REPEAT, PAIR, 2 * HEAD_DIM), F32),
        ),
        [SMEM, SMEM] + [VMEM] * 7,
        (VMEM,) * 5,
        scratch=(
            pltpu.VMEM((SLOTS * PAIR, 3 * HEAD_DIM), BF16),
            pltpu.VMEM((PAIR, 3 * HEAD_DIM), BF16),
            pltpu.SMEM((SLOTS,), jnp.int32),
            pltpu.SemaphoreType.DMA((10,)),
        ),
        aliases={3: 3, 4: 4},
        name="far",
    )(info, reach, queries, tops, acc, own0, *others34)
    theirs = swap(send)
    return call(
        last_kernel, shape((TOK, 2 * COLS), BF16), [VMEM] * 3, VMEM, name="last"
    )(exchange(out_sums), mine, theirs)


def solution(mesh):
    grid = Mesh(mesh.devices.reshape(Z, X, CORES, TP), ("z", "x", "core", "tp"))
    tokens, both = P(CTX), P(CTX, "tp")
    return jax.shard_map(
        shards,
        mesh=grid,
        in_specs=(both,) * 3 + (tokens,) + (both,) * 3,
        out_specs=both,
        check_vma=False,
    )
```

```python
import jax
import jax.numpy as jnp
from jax import lax
from jax.experimental import pallas as pl
from jax.experimental.pallas import tpu as pltpu
from jax.sharding import Mesh, PartitionSpec as P

HEAD_DIM = 128
WIDTH = 4096
EPSILON = 1e-05
NEGATIVE = -1e30

TOK = 192
PAIR = 384
REPEAT = 4
COLS = REPEAT * HEAD_DIM
Z, X, CORES, TP = 8, 4, 2, 4
CHUNK = 2
SCALE = HEAD_DIM ** (-0.5) * 1.4426950408889634

F32 = jnp.float32
BF16 = jnp.bfloat16
VMEM = pl.BlockSpec(memory_space=pltpu.VMEM)
SMEM = pl.BlockSpec(memory_space=pltpu.SMEM)
HBM = pl.BlockSpec(memory_space=pltpu.HBM)


def place():
    return lax.axis_index("z"), lax.axis_index("x"), lax.axis_index("core")


def call(kernel, outs, specs_in, specs_out, scratch=(), aliases=None, limit=16, name=None):
    return pl.pallas_call(
        kernel,
        out_shape=outs,
        in_specs=specs_in,
        out_specs=specs_out,
        scratch_shapes=list(scratch),
        input_output_aliases=aliases or {},
        compiler_params=pltpu.CompilerParams(vmem_limit_bytes=limit * 2**20),
        name=name,
    )


def count_below(ref, doc):
    found = jnp.int32(0)
    for step in (128, 64, 32, 16, 8, 4, 2, 1):
        tried = found + step
        last = ref[jnp.minimum(tried, TOK) - 1]
        found = jnp.where((tried <= TOK) & (last < doc), tried, found)
    return found


def half(core):
    return pl.ds(pl.multiple_of(core * HEAD_DIM, HEAD_DIM), HEAD_DIM)


def rows_of(core):
    return pl.ds(pl.multiple_of(core * TOK, 64), TOK)


def prep_kernel(seg, seg_r, own, other, own0_ref, first_ref, state_ref, info_ref):
    core = place()[2]
    for side, ref in ((core, own), (1 - core, other)):
        first_ref[rows_of(side), :HEAD_DIM] = ref[0]
        first_ref[rows_of(side), HEAD_DIM:] = ref[1]
        own0_ref[rows_of(side), :HEAD_DIM] = ref[2]
        own0_ref[rows_of(side), HEAD_DIM:] = ref[3]
    below = [count_below(seg, d) for d in (1, 2, 3)]
    below_r = [count_below(seg_r, d) for d in (1, 2, 3)]
    bounds = [a + b for a, b in zip(below, below_r)]
    first = jnp.where(core == 0, seg[0], seg_r[0])
    last = jnp.where(core == 0, seg_r[TOK - 1], seg[TOK - 1])

    def pick(values, doc):
        out = jnp.int32(0)
        for d in (1, 2, 3):
            out = jnp.where(doc == d, values[d - 1], out)
        return out

    count = PAIR - pick(bounds, last)
    first_end = jnp.where(first == 3, PAIR, pick(bounds, first + 1))
    for place_in, value in enumerate((*bounds, first, last, count, first_end, 0)):
        info_ref[place_in] = jnp.int32(value)
    rows = lax.broadcasted_iota(jnp.int32, (PAIR, HEAD_DIM), 0)
    masked = jnp.where(rows >= PAIR - count, first_ref[:, :HEAD_DIM].astype(F32), 0.0)
    state = lax.dot_general(
        masked.astype(BF16),
        first_ref[:, HEAD_DIM:],
        (((0,), (0,)), ((), ())),
        preferred_element_type=F32,
    )
    state_ref[:HEAD_DIM] = state.astype(BF16)
    state_ref[HEAD_DIM:] = notes(last.astype(F32), count.astype(F32)).astype(BF16)


def notes(last, count):
    row = lax.broadcasted_iota(jnp.int32, (16, HEAD_DIM), 0)
    high = jnp.floor(count * (1.0 / 64.0))
    return jnp.where(
        row == 0, last, jnp.where(row == 1, high, jnp.where(row == 2, count - 64.0 * high, 0.0))
    )


def read_state(ref):
    tail = ref[HEAD_DIM:].astype(F32)
    return ref[:HEAD_DIM].astype(F32), tail[0:1], tail[1:2] * 64.0 + tail[2:3]


def plane_kernel(
    info, own, from1, from2, from3, own1, queries_r, prefix_ref, plane_ref, later1_ref
):
    x = place()[1]
    later1_ref[...] = own1[...]
    first = info[3].astype(F32)
    items = [read_state(ref) for ref in (own, from1, from2, from3)]
    prefix = jnp.zeros((HEAD_DIM, HEAD_DIM), F32)
    prefix_count = jnp.zeros((1, HEAD_DIM), F32)
    for shift in (1, 2, 3):
        state, doc, count = items[shift]
        chosen = jnp.where((doc == first) & (x >= shift), 1.0, 0.0)
        prefix += state * chosen
        prefix_count += count * chosen
    prefix_ref[:HEAD_DIM] = prefix
    prefix_ref[HEAD_DIM:] = jnp.broadcast_to(prefix_count, (8, HEAD_DIM))
    last = items[0][1]
    for item in items[1:]:
        last = jnp.maximum(last, item[1])
    total = jnp.zeros((HEAD_DIM, HEAD_DIM), F32)
    total_count = jnp.zeros((1, HEAD_DIM), F32)
    for state, doc, count in items:
        chosen = jnp.where(doc == last, 1.0, 0.0)
        total += state * chosen
        total_count += count * chosen
    plane_ref[:HEAD_DIM] = total.astype(BF16)
    plane_ref[HEAD_DIM:] = notes(last, total_count).astype(BF16)


def document_start(info, rows):
    start = jnp.zeros_like(rows)
    for d in range(3):
        start = jnp.where(rows >= info[d], jnp.maximum(start, info[d]), start)
    return start


def split_dot(wide, narrow):
    high = wide.astype(BF16)
    low = (wide - high.astype(F32)).astype(BF16)
    return jnp.dot(high, narrow, preferred_element_type=F32) + jnp.dot(
        low, narrow, preferred_element_type=F32
    )


def inside_kernel(info, keep, queries_r, packed, inside_ref, query_ref):
    core = place()[2]
    query_ref[rows_of(core), :] = keep[0]
    query_ref[rows_of(1 - core), :] = queries_r[0]
    row = lax.broadcasted_iota(jnp.int32, (PAIR, PAIR), 0)
    column = lax.broadcasted_iota(jnp.int32, (PAIR, PAIR), 1)
    visible = (column <= row) & (column >= document_start(info, row))
    for head in range(REPEAT):
        cols = slice(head * HEAD_DIM, (head + 1) * HEAD_DIM)
        scores = lax.dot_general(
            query_ref[:, cols],
            packed[:, :HEAD_DIM],
            (((1,), (1,)), ((), ())),
            preferred_element_type=F32,
        )
        scores = jnp.where(visible, scores, 0.0)
        inside_ref[:, cols] = split_dot(scores, packed[:, HEAD_DIM:])


def row_sums(squares):
    high = squares.astype(BF16)
    low = (squares - high.astype(F32)).astype(BF16)
    ones = jnp.ones((8, squares.shape[1]), BF16)
    dims = (((1,), (1,)), ((), ()))
    return lax.dot_general(ones, high, dims, preferred_element_type=F32) + lax.dot_general(
        ones, low, dims, preferred_element_type=F32
    )


def first_kernel(
    info, prefix, from1, from2, from3, from4, inside, query, own1, own2,
    first_ref, sums_ref, count_ref, pair12_ref, later2_ref
):
    pair12_ref[:PAIR] = own1[...]
    pair12_ref[PAIR:] = own2[...]
    later2_ref[...] = own2[...]
    z = place()[0]
    first = info[3].astype(F32)
    state = prefix[:HEAD_DIM]
    count = prefix[HEAD_DIM : HEAD_DIM + 1]
    for back, ref in enumerate((from1, from2, from3, from4), 1):
        one_state, doc, one_count = read_state(ref)
        chosen = jnp.where((doc == first) & (z >= back), 1.0, 0.0)
        state += one_state * chosen
        count += one_count * chosen
    count_ref[0] = jnp.max(count).astype(jnp.int32)
    high = state.astype(BF16)
    low = (state - high.astype(F32)).astype(BF16)
    in_first = lax.broadcasted_iota(jnp.int32, (PAIR, HEAD_DIM), 0) < info[6]
    squares = jnp.zeros((PAIR, HEAD_DIM), F32)
    for head in range(REPEAT):
        cols = slice(head * HEAD_DIM, (head + 1) * HEAD_DIM)
        queries = query[:, cols]
        earlier = jnp.dot(queries, high, preferred_element_type=F32) + jnp.dot(
            queries, low, preferred_element_type=F32
        )
        out = inside[:, cols] + jnp.where(in_first, earlier, 0.0)
        first_ref[:, cols] = out
        squares += out * out
    sums = row_sums(squares)
    for to in range(CORES * TP):
        sums_ref[to] = sums


def row_scale(sums):
    total = sums[0]
    for device in range(1, CORES * TP):
        total = total + sums[device]
    return lax.transpose(lax.rsqrt(total * (1.0 / WIDTH) + EPSILON), (1, 0))[:, :1]


def payload_kernel(own0, own3, own4, _, *payloads):
    x = place()[1]
    for shift, payload in enumerate(payloads, 1):
        payload[:PAIR] = own3[...]

        @pl.when(x + shift < X)
        def _():
            payload[PAIR:] = own0[...]

        @pl.when(x + shift >= X)
        def _():
            payload[PAIR:] = own4[...]


TILE = 128
TILES = [(head, slice(at, at + TILE)) for head in range(REPEAT) for at in range(0, PAIR, TILE)]


def scores_of(queries, keys, head, part, rows):
    return lax.dot_general(
        queries[head, part],
        keys[rows, :HEAD_DIM],
        (((1,), (1,)), ((), ())),
        preferred_element_type=F32,
    )


def sweep(queries, kv, tops, acc, rows, visible=None):
    ahead = scores_of(queries, kv, *TILES[0], rows)
    for at, (head, part) in enumerate(TILES):
        scores = ahead
        if at + 1 < len(TILES):
            ahead = scores_of(queries, kv, *TILES[at + 1], rows)
        if visible is not None:
            scores = jnp.where(visible(part), scores, NEGATIVE)
        top = jnp.max(scores, axis=1, keepdims=True)
        old_top = tops[head, part]
        top = jnp.maximum(old_top, top)
        wide_top = jnp.concatenate([top] * (scores.shape[1] // HEAD_DIM), axis=1)
        weights = jnp.exp2((scores - wide_top) * SCALE)
        summed = jnp.dot(weights.astype(BF16), kv[rows, HEAD_DIM:], preferred_element_type=F32)
        tops[head, part] = top
        shrink = jnp.exp2((old_top - top) * SCALE)
        acc[head, part] = acc[head, part] * jnp.concatenate([shrink, shrink], axis=1) + summed


class Window:
    def __init__(self, prior, blocks, kv, bounds, sems):
        self.kv, self.bounds = kv, bounds
        used = jnp.int32(0)
        self.copies = []
        for at, (ref, distance) in enumerate(blocks):
            distance = jnp.int32(distance)
            needed = (distance >= 1) & (distance <= 16) & (prior > (distance - 1) * PAIR)
            slot = jnp.minimum(used, bounds.shape[0] - 1)
            rows = pl.ds(pl.multiple_of(slot * PAIR, PAIR), PAIR)
            copy = pltpu.make_async_copy(ref, kv.at[rows, pl.ds(0, 2 * HEAD_DIM)], sems.at[at])
            self.copies.append((needed, copy))

            @pl.when(needed)
            def _():
                copy.start()
                bounds[slot] = jnp.maximum(distance * PAIR - prior, 0)

            used = used + needed.astype(jnp.int32)
        self.steps = (used + CHUNK - 1) // CHUNK
        kv[:, 2 * HEAD_DIM :] = jnp.ones((kv.shape[0], HEAD_DIM), BF16)

        @pl.when(used % CHUNK != 0)
        def _():
            rows = pl.ds(pl.multiple_of(used * PAIR, PAIR), PAIR)
            kv[rows, : 2 * HEAD_DIM] = jnp.zeros((PAIR, 2 * HEAD_DIM), BF16)
            bounds[used] = jnp.int32(PAIR)

    def absorb(self, queries, tops, acc):
        for needed, copy in self.copies:
            pl.when(needed)(copy.wait)

        @pl.loop(0, self.steps)
        def _(step):
            rows = pl.ds(pl.multiple_of(step * CHUNK * PAIR, CHUNK * PAIR), CHUNK * PAIR)
            low0, low1 = self.bounds[step * CHUNK], self.bounds[step * CHUNK + 1]
            whole = (low0 == 0) & (low1 == 0)

            @pl.when(whole)
            def _():
                sweep(queries, self.kv, tops, acc, rows)

            @pl.when(jnp.logical_not(whole))
            def _():
                column = lax.broadcasted_iota(jnp.int32, (1, CHUNK * PAIR), 1)
                seen = column >= jnp.where(column < PAIR, low0, PAIR + low1)
                sweep(queries, self.kv, tops, acc, rows, lambda part: seen)


SLOTS = 10


def near_kernel(
    reach, sums, first, keep, queries_r, own1, own2, own3, own4, *refs
):
    others = refs[:3]
    queries, tops, acc, kv, scales, bounds, sems = refs[3:]
    _, x, core = place()
    blocks = [(own1, 4), (own2, 8), (own3, 12), (own4, 16)]
    for shift, other in enumerate(others, 1):
        wrapped = jnp.where(x < shift, 4, 0)
        blocks.append((other.at[pl.ds(0, PAIR)], 4 + shift - wrapped))
        blocks.append((other.at[pl.ds(PAIR, PAIR)], 8 + shift - wrapped))
    window = Window(reach[0], blocks, kv, bounds, sems)
    tops[...] = jnp.full(tops.shape, NEGATIVE, F32)
    acc[...] = jnp.zeros(acc.shape, F32)
    scales[...] = jnp.broadcast_to(row_scale(sums), (PAIR, HEAD_DIM))
    for part, where in ((keep.at[1], rows_of(core)), (queries_r.at[1], rows_of(1 - core))):
        for head in range(REPEAT):
            cols = slice(head * HEAD_DIM, (head + 1) * HEAD_DIM)
            value = part[:, cols].astype(F32) + first[where, cols] * scales[where, :]
            queries[head, where, :] = value.astype(BF16)
    window.absorb(queries, tops, acc)


def far_kernel(info, reach, queries, old_tops, old_acc, own0, *refs):
    others = refs[:3]
    mine_ref, send_ref, sums_ref, tops, acc, kv, own, bounds, sems = refs[3:]
    _, x, core = place()
    blocks = []
    for shift, other in enumerate(others, 1):
        wrapped = x < shift
        blocks.append((other.at[pl.ds(0, PAIR)], 12 + shift - jnp.where(wrapped, 4, 0)))
        blocks.append((other.at[pl.ds(PAIR, PAIR)], shift + jnp.where(wrapped, 12, 0)))
    window = Window(reach[0], blocks, kv, bounds, sems)
    own[:, : 2 * HEAD_DIM] = own0[...]
    own[:, 2 * HEAD_DIM :] = jnp.ones((PAIR, HEAD_DIM), BF16)
    window.absorb(queries, tops, acc)

    @pl.when(info[6] < PAIR)
    def _():
        in_first = lax.broadcasted_iota(jnp.int32, (PAIR, HEAD_DIM), 0) < info[6]
        for head in range(REPEAT):
            tops[head] = jnp.where(in_first, tops[head], NEGATIVE)
            acc[head] = jnp.where(jnp.concatenate([in_first, in_first], axis=1), acc[head], 0.0)

    def own_visible(part):
        row = lax.broadcasted_iota(jnp.int32, (TILE, PAIR), 0) + part.start
        column = lax.broadcasted_iota(jnp.int32, (TILE, PAIR), 1)
        return (column <= row) & (column >= document_start(info, row))

    sweep(queries, own, tops, acc, slice(0, PAIR), own_visible)
    for side in range(CORES):
        where = slice(side * TOK, (side + 1) * TOK)
        squares = jnp.zeros((TOK, HEAD_DIM), F32)
        outs = []
        for head in range(REPEAT):
            summed = acc[head, where, :]
            out = (summed[:, :HEAD_DIM] / summed[:, HEAD_DIM:]).astype(BF16)
            outs.append(out)
            widened = out.astype(F32)
            squares += widened * widened
        whole = jnp.concatenate(outs, axis=1)

        @pl.when(core == side)
        def _():
            mine_ref[...] = whole

        @pl.when(core != side)
        def _():
            send_ref[...] = whole

        sums = row_sums(squares)
        for to in range(TP):
            sums_ref[side * TP + to] = sums


def last_kernel(sums, mine, theirs, out_ref):
    core = place()[2]
    scale = row_scale(sums)
    for ref, side in ((mine, core), (theirs, 1 - core)):
        cols = pl.ds(pl.multiple_of(side * COLS, COLS), COLS)
        out_ref[:, cols] = (ref[...].astype(F32) * scale).astype(BF16)


CTX = ("z", "x", "core")


def move(value, z_shift=0, x_shift=0, core_shift=0, keep=lambda x: True):
    pairs = []
    for z in range(Z):
        for x in range(X):
            for core in range(CORES):
                to = ((z + z_shift) % Z * X + (x + x_shift) % X) * CORES
                if keep(x):
                    pairs.append(((z * X + x) * CORES + core, to + (core + core_shift) % CORES))
    return lax.ppermute(value, CTX, pairs)


def swap(value):
    return move(value, core_shift=1)


def exchange(sums):
    return lax.all_to_all(sums, ("core", "tp"), 0, 0, tiled=True)


def shape(dims, kind):
    return jax.ShapeDtypeStruct(dims, kind)


def shards(query_one, key_one, value_one, segments, query_base, key_two, value_two):
    core = lax.axis_index("core")

    def halves(arrays):
        low = jnp.stack([array[:, : array.shape[1] // 2] for array in arrays])
        high = jnp.stack([array[:, array.shape[1] // 2 :] for array in arrays])
        return jnp.where(core == 0, low, high), jnp.where(core == 0, high, low)

    segments_r = swap(segments)
    own_keep, own_send = halves((key_one, value_one, key_two, value_two))
    own0, packed, state, info = call(
        prep_kernel,
        (
            shape((PAIR, 2 * HEAD_DIM), BF16),
            shape((PAIR, 2 * HEAD_DIM), BF16),
            shape((144, HEAD_DIM), BF16),
            shape((8,), jnp.int32),
        ),
        [SMEM, SMEM, VMEM, VMEM],
        (VMEM,) * 3 + (SMEM,),
        name="prep",
    )(segments, segments_r, own_keep, swap(own_send))
    keep, query_send = halves((query_one, query_base))
    queries_r = swap(query_send)

    own1 = move(own0, z_shift=1)
    near = [move(state, x_shift=shift) for shift in (1, 2, 3)]
    prefix, plane, later1 = call(
        plane_kernel,
        (
            shape((HEAD_DIM + 8, HEAD_DIM), F32),
            shape((144, HEAD_DIM), BF16),
            shape((PAIR, 2 * HEAD_DIM), BF16),
        ),
        [SMEM] + [VMEM] * 6,
        (VMEM,) * 3,
        name="plane",
    )(info, state, *near, own1, queries_r)
    far = [move(plane, z_shift=back) for back in (1, 2, 3, 4)]

    own2 = move(later1, z_shift=1)

    inside, query = call(
        inside_kernel,
        (shape((PAIR, COLS), F32), shape((PAIR, COLS), BF16)),
        [SMEM] + [VMEM] * 3,
        (VMEM,) * 2,
        name="inside",
    )(info, keep, queries_r, packed)
    first, sums, reach, pair12, later2 = call(
        first_kernel,
        (
            shape((PAIR, COLS), F32),
            shape((CORES * TP, 8, PAIR), F32),
            shape((1,), jnp.int32),
            shape((2 * PAIR, 2 * HEAD_DIM), BF16),
            shape((PAIR, 2 * HEAD_DIM), BF16),
        ),
        [SMEM] + [VMEM] * 9,
        (VMEM, VMEM, SMEM, VMEM, VMEM),
        name="first",
    )(info, prefix, *far, inside, query, own1, own2)
    own3 = move(later2, z_shift=1)
    own4 = move(own3, z_shift=1)


    all_sums = exchange(sums)
    x_shifts = (1, 2, 3)
    others12 = [move(pair12, x_shift=shift) for shift in x_shifts]
    payloads34 = call(
        payload_kernel,
        (shape((2 * PAIR, 2 * HEAD_DIM), BF16),) * 3,
        [VMEM] * 4,
        (VMEM,) * 3,
        name="payload",
    )(own0, own3, own4, all_sums)
    others34 = [move(value, x_shift=shift) for shift, value in zip(x_shifts, payloads34)]
    queries, tops, acc = call(
        near_kernel,
        (
            shape((REPEAT, PAIR, HEAD_DIM), BF16),
            shape((REPEAT, PAIR, HEAD_DIM), F32),
            shape((REPEAT, PAIR, 2 * HEAD_DIM), F32),
        ),
        [SMEM] + [VMEM] * 11,
        (VMEM,) * 3,
        scratch=(
            pltpu.VMEM((SLOTS * PAIR, 3 * HEAD_DIM), BF16),
            pltpu.VMEM((PAIR, HEAD_DIM), F32),
            pltpu.SMEM((SLOTS,), jnp.int32),
            pltpu.SemaphoreType.DMA((10,)),
        ),
        name="near",
    )(
        reach, all_sums, first, keep, queries_r, own1, own2, own3, own4, *others12
    )
    mine, send, out_sums, _, _ = call(
        far_kernel,
        (
            shape((TOK, COLS), BF16),
            shape((TOK, COLS), BF16),
            shape((CORES * TP, 8, TOK), F32),
            shape((REPEAT, PAIR, HEAD_DIM), F32),
            shape((REPEAT, PAIR, 2 * HEAD_DIM), F32),
        ),
        [SMEM, SMEM] + [VMEM] * 7,
        (VMEM,) * 5,
        scratch=(
            pltpu.VMEM((SLOTS * PAIR, 3 * HEAD_DIM), BF16),
            pltpu.VMEM((PAIR, 3 * HEAD_DIM), BF16),
            pltpu.SMEM((SLOTS,), jnp.int32),
            pltpu.SemaphoreType.DMA((10,)),
        ),
        aliases={3: 3, 4: 4},
        name="far",
    )(info, reach, queries, tops, acc, own0, *others34)
    theirs = swap(send)
    return call(
        last_kernel, shape((TOK, 2 * COLS), BF16), [VMEM] * 3, VMEM, name="last"
    )(exchange(out_sums), mine, theirs)


def solution(mesh):
    grid = Mesh(mesh.devices.reshape(Z, X, CORES, TP), ("z", "x", "core", "tp"))
    tokens, both = P(CTX), P(CTX, "tp")
    return jax.shard_map(
        shards,
        mesh=grid,
        in_specs=(both,) * 3 + (tokens,) + (both,) * 3,
        out_specs=both,
        check_vma=False,
    )
```

```python
import jax
import jax.numpy as jnp
from jax import lax
from jax.experimental import pallas as pl
from jax.experimental.pallas import tpu as pltpu
from jax.sharding import Mesh, PartitionSpec as P

HEAD_DIM = 128
WIDTH = 4096
EPSILON = 1e-05
NEGATIVE = -1e30

TOK = 192
PAIR = 384
REPEAT = 4
COLS = REPEAT * HEAD_DIM
Z, X, CORES, TP = 8, 4, 2, 4
SCALE = HEAD_DIM ** (-0.5) * 1.4426950408889634

F32 = jnp.float32
BF16 = jnp.bfloat16
VMEM = pl.BlockSpec(memory_space=pltpu.VMEM)
SMEM = pl.BlockSpec(memory_space=pltpu.SMEM)
HBM = pl.BlockSpec(memory_space=pltpu.HBM)


def place():
    return lax.axis_index("z"), lax.axis_index("x"), lax.axis_index("core")


def call(kernel, outs, specs_in, specs_out, scratch=(), aliases=None, limit=16, name=None):
    return pl.pallas_call(
        kernel,
        out_shape=outs,
        in_specs=specs_in,
        out_specs=specs_out,
        scratch_shapes=list(scratch),
        input_output_aliases=aliases or {},
        compiler_params=pltpu.CompilerParams(vmem_limit_bytes=limit * 2**20),
        name=name,
    )


def count_below(ref, doc):
    found = jnp.int32(0)
    for step in (128, 64, 32, 16, 8, 4, 2, 1):
        tried = found + step
        last = ref[jnp.minimum(tried, TOK) - 1]
        found = jnp.where((tried <= TOK) & (last < doc), tried, found)
    return found


def half(core):
    return pl.ds(pl.multiple_of(core * HEAD_DIM, HEAD_DIM), HEAD_DIM)


def rows_of(core):
    return pl.ds(pl.multiple_of(core * TOK, 64), TOK)


def prep_kernel(seg, seg_r, own, other, own0_ref, first_ref, state_ref, info_ref):
    core = place()[2]
    for side, ref in ((core, own), (1 - core, other)):
        first_ref[rows_of(side), :HEAD_DIM] = ref[0]
        first_ref[rows_of(side), HEAD_DIM:] = ref[1]
        own0_ref[rows_of(side), :HEAD_DIM] = ref[2]
        own0_ref[rows_of(side), HEAD_DIM:] = ref[3]
    below = [count_below(seg, d) for d in (1, 2, 3)]
    below_r = [count_below(seg_r, d) for d in (1, 2, 3)]
    bounds = [a + b for a, b in zip(below, below_r)]
    first = jnp.where(core == 0, seg[0], seg_r[0])
    last = jnp.where(core == 0, seg_r[TOK - 1], seg[TOK - 1])

    def pick(values, doc):
        out = jnp.int32(0)
        for d in (1, 2, 3):
            out = jnp.where(doc == d, values[d - 1], out)
        return out

    count = PAIR - pick(bounds, last)
    first_end = jnp.where(first == 3, PAIR, pick(bounds, first + 1))
    for place_in, value in enumerate((*bounds, first, last, count, first_end, 0)):
        info_ref[place_in] = jnp.int32(value)
    rows = lax.broadcasted_iota(jnp.int32, (PAIR, HEAD_DIM), 0)
    masked = jnp.where(rows >= PAIR - count, first_ref[:, :HEAD_DIM].astype(F32), 0.0)
    state = lax.dot_general(
        masked.astype(BF16),
        first_ref[:, HEAD_DIM:],
        (((0,), (0,)), ((), ())),
        preferred_element_type=F32,
    )
    state_ref[:HEAD_DIM] = state.astype(BF16)
    state_ref[HEAD_DIM:] = notes(last.astype(F32), count.astype(F32)).astype(BF16)


def notes(last, count):
    row = lax.broadcasted_iota(jnp.int32, (16, HEAD_DIM), 0)
    high = jnp.floor(count * (1.0 / 64.0))
    return jnp.where(
        row == 0, last, jnp.where(row == 1, high, jnp.where(row == 2, count - 64.0 * high, 0.0))
    )


def read_state(ref):
    tail = ref[HEAD_DIM:].astype(F32)
    return ref[:HEAD_DIM].astype(F32), tail[0:1], tail[1:2] * 64.0 + tail[2:3]


def plane_kernel(
    info, own, from1, from2, from3, own1, queries_r, prefix_ref, plane_ref, later1_ref
):
    x = place()[1]
    later1_ref[...] = own1[...]
    first = info[3].astype(F32)
    items = [read_state(ref) for ref in (own, from1, from2, from3)]
    prefix = jnp.zeros((HEAD_DIM, HEAD_DIM), F32)
    prefix_count = jnp.zeros((1, HEAD_DIM), F32)
    for shift in (1, 2, 3):
        state, doc, count = items[shift]
        chosen = jnp.where((doc == first) & (x >= shift), 1.0, 0.0)
        prefix += state * chosen
        prefix_count += count * chosen
    prefix_ref[:HEAD_DIM] = prefix
    prefix_ref[HEAD_DIM:] = jnp.broadcast_to(prefix_count, (8, HEAD_DIM))
    last = items[0][1]
    for item in items[1:]:
        last = jnp.maximum(last, item[1])
    total = jnp.zeros((HEAD_DIM, HEAD_DIM), F32)
    total_count = jnp.zeros((1, HEAD_DIM), F32)
    for state, doc, count in items:
        chosen = jnp.where(doc == last, 1.0, 0.0)
        total += state * chosen
        total_count += count * chosen
    plane_ref[:HEAD_DIM] = total.astype(BF16)
    plane_ref[HEAD_DIM:] = notes(last, total_count).astype(BF16)


def document_start(info, rows):
    start = jnp.zeros_like(rows)
    for d in range(3):
        start = jnp.where(rows >= info[d], jnp.maximum(start, info[d]), start)
    return start


def split_dot(wide, narrow):
    high = wide.astype(BF16)
    low = (wide - high.astype(F32)).astype(BF16)
    return jnp.dot(high, narrow, preferred_element_type=F32) + jnp.dot(
        low, narrow, preferred_element_type=F32
    )


def inside_kernel(info, keep, queries_r, packed, inside_ref, query_ref):
    core = place()[2]
    query_ref[rows_of(core), :] = keep[0]
    query_ref[rows_of(1 - core), :] = queries_r[0]
    row = lax.broadcasted_iota(jnp.int32, (PAIR, PAIR), 0)
    column = lax.broadcasted_iota(jnp.int32, (PAIR, PAIR), 1)
    visible = (column <= row) & (column >= document_start(info, row))
    for head in range(REPEAT):
        cols = slice(head * HEAD_DIM, (head + 1) * HEAD_DIM)
        scores = lax.dot_general(
            query_ref[:, cols],
            packed[:, :HEAD_DIM],
            (((1,), (1,)), ((), ())),
            preferred_element_type=F32,
        )
        scores = jnp.where(visible, scores, 0.0)
        inside_ref[:, cols] = split_dot(scores, packed[:, HEAD_DIM:])


def row_sums(squares):
    high = squares.astype(BF16)
    low = (squares - high.astype(F32)).astype(BF16)
    ones = jnp.ones((8, squares.shape[1]), BF16)
    dims = (((1,), (1,)), ((), ()))
    return lax.dot_general(ones, high, dims, preferred_element_type=F32) + lax.dot_general(
        ones, low, dims, preferred_element_type=F32
    )


def first_kernel(
    info, prefix, from1, from2, from3, from4, inside, query, own1, own2,
    first_ref, sums_ref, count_ref, pair12_ref, later2_ref
):
    pair12_ref[:PAIR] = own1[...]
    pair12_ref[PAIR:] = own2[...]
    later2_ref[...] = own2[...]
    z = place()[0]
    first = info[3].astype(F32)
    state = prefix[:HEAD_DIM]
    count = prefix[HEAD_DIM : HEAD_DIM + 1]
    for back, ref in enumerate((from1, from2, from3, from4), 1):
        one_state, doc, one_count = read_state(ref)
        chosen = jnp.where((doc == first) & (z >= back), 1.0, 0.0)
        state += one_state * chosen
        count += one_count * chosen
    count_ref[0] = jnp.max(count).astype(jnp.int32)
    high = state.astype(BF16)
    low = (state - high.astype(F32)).astype(BF16)
    in_first = lax.broadcasted_iota(jnp.int32, (PAIR, HEAD_DIM), 0) < info[6]
    squares = jnp.zeros((PAIR, HEAD_DIM), F32)
    for head in range(REPEAT):
        cols = slice(head * HEAD_DIM, (head + 1) * HEAD_DIM)
        queries = query[:, cols]
        earlier = jnp.dot(queries, high, preferred_element_type=F32) + jnp.dot(
            queries, low, preferred_element_type=F32
        )
        out = inside[:, cols] + jnp.where(in_first, earlier, 0.0)
        first_ref[:, cols] = out
        squares += out * out
    sums = row_sums(squares)
    for to in range(CORES * TP):
        sums_ref[to] = sums


def row_scale(sums):
    total = sums[0]
    for device in range(1, CORES * TP):
        total = total + sums[device]
    return lax.transpose(lax.rsqrt(total * (1.0 / WIDTH) + EPSILON), (1, 0))[:, :1]


def payload_kernel(own0, own3, own4, *refs):
    x = place()[1]
    for shift, payload in enumerate(refs[4:], 1):
        payload[:PAIR] = own3[...]

        @pl.when(x + shift < X)
        def _():
            payload[PAIR:] = own0[...]

        @pl.when(x + shift >= X)
        def _():
            payload[PAIR:] = own4[...]


TILE = 384
TILES = [(head, slice(at, at + TILE)) for head in range(REPEAT) for at in range(0, PAIR, TILE)]


def scores_of(queries, keys, head, part, rows):
    return lax.dot_general(
        queries[head, part],
        keys[rows, :HEAD_DIM],
        (((1,), (1,)), ((), ())),
        preferred_element_type=F32,
    )


def sweep(queries, kv, tops, acc, rows, visible=None):
    ahead = scores_of(queries, kv, *TILES[0], rows)
    for at, (head, part) in enumerate(TILES):
        scores = ahead
        if at + 1 < len(TILES):
            ahead = scores_of(queries, kv, *TILES[at + 1], rows)
        if visible is not None:
            scores = jnp.where(visible(part), scores, NEGATIVE)
        top = jnp.max(scores, axis=1, keepdims=True)
        old_top = tops[head, part]
        top = jnp.maximum(old_top, top)
        wide_top = jnp.concatenate([top] * (scores.shape[1] // HEAD_DIM), axis=1)
        weights = jnp.exp2((scores - wide_top) * SCALE)
        summed = jnp.dot(weights.astype(BF16), kv[rows, HEAD_DIM:], preferred_element_type=F32)
        tops[head, part] = top
        shrink = jnp.exp2((old_top - top) * SCALE)
        acc[head, part] = acc[head, part] * jnp.concatenate([shrink, shrink], axis=1) + summed


class Window:
    def __init__(self, prior, blocks, chunk, kv, bounds, sems):
        self.kv, self.bounds, self.chunk = kv, bounds, chunk
        used = jnp.int32(0)
        self.copies = []
        for at, (ref, distance) in enumerate(blocks):
            distance = jnp.int32(distance)
            needed = (distance >= 1) & (distance <= 16) & (prior > (distance - 1) * PAIR)
            slot = jnp.minimum(used, bounds.shape[0] - 1)
            rows = pl.ds(pl.multiple_of(slot * PAIR, PAIR), PAIR)
            copy = pltpu.make_async_copy(ref, kv.at[rows, pl.ds(0, 2 * HEAD_DIM)], sems.at[at])
            self.copies.append((needed, copy))

            @pl.when(needed)
            def _():
                copy.start()
                bounds[slot] = jnp.maximum(distance * PAIR - prior, 0)

            used = used + needed.astype(jnp.int32)
        self.steps = (used + chunk - 1) // chunk
        kv[:, 2 * HEAD_DIM :] = jnp.ones((kv.shape[0], HEAD_DIM), BF16)

        for extra in range(chunk - 1):

            @pl.when(used + extra < self.steps * chunk)
            def _():
                spare = jnp.minimum(used + extra, bounds.shape[0] - 1)
                rows = pl.ds(pl.multiple_of(spare * PAIR, PAIR), PAIR)
                kv[rows, : 2 * HEAD_DIM] = jnp.zeros((PAIR, 2 * HEAD_DIM), BF16)
                bounds[spare] = jnp.int32(PAIR)

    def absorb(self, queries, tops, acc):
        for needed, copy in self.copies:
            pl.when(needed)(copy.wait)

        @pl.loop(0, self.steps)
        def _(step):
            keys = self.chunk * PAIR
            rows = pl.ds(pl.multiple_of(step * keys, keys), keys)
            lows = [self.bounds[step * self.chunk + slot] for slot in range(self.chunk)]
            hidden = lows[0]
            for low in lows[1:]:
                hidden = hidden + low

            @pl.when(hidden == 0)
            def _():
                sweep(queries, self.kv, tops, acc, rows)

            @pl.when(hidden != 0)
            def _():
                column = lax.broadcasted_iota(jnp.int32, (1, keys), 1)
                start = lows[0]
                for slot in range(1, self.chunk):
                    start = jnp.where(column >= slot * PAIR, slot * PAIR + lows[slot], start)
                sweep(queries, self.kv, tops, acc, rows, lambda part: column >= start)


NEAR_SLOTS, NEAR_CHUNK = 10, 5
FAR_SLOTS, FAR_CHUNK = 6, 3


def near_kernel(
    reach, sums, first, keep, queries_r, own1, own2, own3, own4, *refs
):
    others = refs[:3]
    queries, tops, acc, kv, scales, bounds, sems = refs[3:]
    _, x, core = place()
    blocks = [(own1, 4), (own2, 8), (own3, 12), (own4, 16)]
    for shift, other in enumerate(others, 1):
        wrapped = jnp.where(x < shift, 4, 0)
        blocks.append((other.at[pl.ds(0, PAIR)], 4 + shift - wrapped))
        blocks.append((other.at[pl.ds(PAIR, PAIR)], 8 + shift - wrapped))
    window = Window(reach[0], blocks, NEAR_CHUNK, kv, bounds, sems)
    tops[...] = jnp.full(tops.shape, NEGATIVE, F32)
    acc[...] = jnp.zeros(acc.shape, F32)
    scales[...] = jnp.broadcast_to(row_scale(sums), (PAIR, HEAD_DIM))
    for part, where in ((keep.at[1], rows_of(core)), (queries_r.at[1], rows_of(1 - core))):
        for head in range(REPEAT):
            cols = slice(head * HEAD_DIM, (head + 1) * HEAD_DIM)
            value = part[:, cols].astype(F32) + first[where, cols] * scales[where, :]
            queries[head, where, :] = value.astype(BF16)
    window.absorb(queries, tops, acc)


def far_kernel(info, reach, queries, old_tops, old_acc, own0, *refs):
    others = refs[:3]
    mine_ref, send_ref, sums_ref, tops, acc, kv, own, bounds, sems = refs[3:]
    _, x, core = place()
    blocks = []
    for shift, other in enumerate(others, 1):
        wrapped = x < shift
        blocks.append((other.at[pl.ds(0, PAIR)], 12 + shift - jnp.where(wrapped, 4, 0)))
        blocks.append((other.at[pl.ds(PAIR, PAIR)], shift + jnp.where(wrapped, 12, 0)))
    window = Window(reach[0], blocks, FAR_CHUNK, kv, bounds, sems)
    own[:, : 2 * HEAD_DIM] = own0[...]
    own[:, 2 * HEAD_DIM :] = jnp.ones((PAIR, HEAD_DIM), BF16)
    window.absorb(queries, tops, acc)

    @pl.when(info[6] < PAIR)
    def _():
        in_first = lax.broadcasted_iota(jnp.int32, (PAIR, HEAD_DIM), 0) < info[6]
        for head in range(REPEAT):
            tops[head] = jnp.where(in_first, tops[head], NEGATIVE)
            acc[head] = jnp.where(jnp.concatenate([in_first, in_first], axis=1), acc[head], 0.0)

    def own_visible(part):
        row = lax.broadcasted_iota(jnp.int32, (TILE, PAIR), 0) + part.start
        column = lax.broadcasted_iota(jnp.int32, (TILE, PAIR), 1)
        return (column <= row) & (column >= document_start(info, row))

    sweep(queries, own, tops, acc, slice(0, PAIR), own_visible)
    for side in range(CORES):
        where = slice(side * TOK, (side + 1) * TOK)
        squares = jnp.zeros((TOK, HEAD_DIM), F32)
        outs = []
        for head in range(REPEAT):
            summed = acc[head, where, :]
            out = (summed[:, :HEAD_DIM] / summed[:, HEAD_DIM:]).astype(BF16)
            outs.append(out)
            widened = out.astype(F32)
            squares += widened * widened
        whole = jnp.concatenate(outs, axis=1)

        @pl.when(core == side)
        def _():
            mine_ref[...] = whole

        @pl.when(core != side)
        def _():
            send_ref[...] = whole

        sums = row_sums(squares)
        for to in range(TP):
            sums_ref[side * TP + to] = sums


def last_kernel(sums, mine, theirs, out_ref):
    core = place()[2]
    scale = row_scale(sums)
    for ref, side in ((mine, core), (theirs, 1 - core)):
        cols = pl.ds(pl.multiple_of(side * COLS, COLS), COLS)
        out_ref[:, cols] = (ref[...].astype(F32) * scale).astype(BF16)


CTX = ("z", "x", "core")


def move(value, z_shift=0, x_shift=0, core_shift=0, keep=lambda x: True):
    pairs = []
    for z in range(Z):
        for x in range(X):
            for core in range(CORES):
                to = ((z + z_shift) % Z * X + (x + x_shift) % X) * CORES
                if keep(x):
                    pairs.append(((z * X + x) * CORES + core, to + (core + core_shift) % CORES))
    return lax.ppermute(value, CTX, pairs)


def swap(value):
    return move(value, core_shift=1)


def exchange(sums):
    return lax.all_to_all(sums, ("core", "tp"), 0, 0, tiled=True)


def shape(dims, kind):
    return jax.ShapeDtypeStruct(dims, kind)


def shards(query_one, key_one, value_one, segments, query_base, key_two, value_two):
    core = lax.axis_index("core")

    def halves(arrays):
        low = jnp.stack([array[:, : array.shape[1] // 2] for array in arrays])
        high = jnp.stack([array[:, array.shape[1] // 2 :] for array in arrays])
        return jnp.where(core == 0, low, high), jnp.where(core == 0, high, low)

    segments_r = swap(segments)
    own_keep, own_send = halves((key_one, value_one, key_two, value_two))
    own0, packed, state, info = call(
        prep_kernel,
        (
            shape((PAIR, 2 * HEAD_DIM), BF16),
            shape((PAIR, 2 * HEAD_DIM), BF16),
            shape((144, HEAD_DIM), BF16),
            shape((8,), jnp.int32),
        ),
        [SMEM, SMEM, VMEM, VMEM],
        (VMEM,) * 3 + (SMEM,),
        name="prep",
    )(segments, segments_r, own_keep, swap(own_send))
    keep, query_send = halves((query_one, query_base))
    queries_r = swap(query_send)

    own1 = move(own0, z_shift=1)
    near = [move(state, x_shift=shift) for shift in (1, 2, 3)]
    prefix, plane, later1 = call(
        plane_kernel,
        (
            shape((HEAD_DIM + 8, HEAD_DIM), F32),
            shape((144, HEAD_DIM), BF16),
            shape((PAIR, 2 * HEAD_DIM), BF16),
        ),
        [SMEM] + [VMEM] * 6,
        (VMEM,) * 3,
        name="plane",
    )(info, state, *near, own1, queries_r)
    far = [move(plane, z_shift=back) for back in (1, 2, 3, 4)]

    own2 = move(later1, z_shift=1)

    inside, query = call(
        inside_kernel,
        (shape((PAIR, COLS), F32), shape((PAIR, COLS), BF16)),
        [SMEM] + [VMEM] * 3,
        (VMEM,) * 2,
        name="inside",
    )(info, keep, queries_r, packed)
    first, sums, reach, pair12, later2 = call(
        first_kernel,
        (
            shape((PAIR, COLS), F32),
            shape((CORES * TP, 8, PAIR), F32),
            shape((1,), jnp.int32),
            shape((2 * PAIR, 2 * HEAD_DIM), BF16),
            shape((PAIR, 2 * HEAD_DIM), BF16),
        ),
        [SMEM] + [VMEM] * 9,
        (VMEM, VMEM, SMEM, VMEM, VMEM),
        name="first",
    )(info, prefix, *far, inside, query, own1, own2)
    own3 = move(later2, z_shift=1)
    own4 = move(own3, z_shift=1)


    all_sums = exchange(sums)
    x_shifts = (1, 2, 3)
    others12 = [move(pair12, x_shift=shift) for shift in x_shifts]
    payloads34 = call(
        payload_kernel,
        (shape((2 * PAIR, 2 * HEAD_DIM), BF16),) * 3,
        [VMEM] * 7,
        (VMEM,) * 3,
        name="payload",
    )(own0, own3, own4, *others12, all_sums)
    others34 = [move(value, x_shift=shift) for shift, value in zip(x_shifts, payloads34)]
    queries, tops, acc = call(
        near_kernel,
        (
            shape((REPEAT, PAIR, HEAD_DIM), BF16),
            shape((REPEAT, PAIR, HEAD_DIM), F32),
            shape((REPEAT, PAIR, 2 * HEAD_DIM), F32),
        ),
        [SMEM] + [VMEM] * 11,
        (VMEM,) * 3,
        scratch=(
            pltpu.VMEM((NEAR_SLOTS * PAIR, 3 * HEAD_DIM), BF16),
            pltpu.VMEM((PAIR, HEAD_DIM), F32),
            pltpu.SMEM((NEAR_SLOTS,), jnp.int32),
            pltpu.SemaphoreType.DMA((10,)),
        ),
        limit=24,
        name="near",
    )(
        reach, all_sums, first, keep, queries_r, own1, own2, own3, own4, *others12
    )
    mine, send, out_sums, _, _ = call(
        far_kernel,
        (
            shape((TOK, COLS), BF16),
            shape((TOK, COLS), BF16),
            shape((CORES * TP, 8, TOK), F32),
            shape((REPEAT, PAIR, HEAD_DIM), F32),
            shape((REPEAT, PAIR, 2 * HEAD_DIM), F32),
        ),
        [SMEM, SMEM] + [VMEM] * 7,
        (VMEM,) * 5,
        scratch=(
            pltpu.VMEM((FAR_SLOTS * PAIR, 3 * HEAD_DIM), BF16),
            pltpu.VMEM((PAIR, 3 * HEAD_DIM), BF16),
            pltpu.SMEM((FAR_SLOTS,), jnp.int32),
            pltpu.SemaphoreType.DMA((10,)),
        ),
        aliases={3: 3, 4: 4},
        name="far",
    )(info, reach, queries, tops, acc, own0, *others34)
    theirs = swap(send)
    return call(
        last_kernel, shape((TOK, 2 * COLS), BF16), [VMEM] * 3, VMEM, name="last"
    )(exchange(out_sums), mine, theirs)


def solution(mesh):
    grid = Mesh(mesh.devices.reshape(Z, X, CORES, TP), ("z", "x", "core", "tp"))
    tokens, both = P(CTX), P(CTX, "tp")
    return jax.shard_map(
        shards,
        mesh=grid,
        in_specs=(both,) * 3 + (tokens,) + (both,) * 3,
        out_specs=both,
        check_vma=False,
    )
```
